32 devices in a mesh: seq: 8 (over z, x), head: 4 (over y, core).
Axes of the slice: x: 2, y: 2, z: 4, core: 2. Of those that a mesh axis runs over, the one named last changes fastest.
Arguments:
- inputs: float32 [2048, 2048], P('seq'), may hold values from -6 to 6
- gains: float32 [2, 2048], replicated, may hold values from 0.5 to 1.5
- w_proj: bfloat16 [2048, 4, 2048], P(None, None, 'head'), may hold values from -0.125 to 0.125
- w_gates: bfloat16 [2, 2048, 16], P(None, None, 'head'), may hold values from -0.125 to 0.125
- decay: float32 [2, 16], P(None, 'head'), may hold values from -10 to 1
- conv_w: float32 [3, 4, 2048], P(None, None, 'head'), may hold values from -3 to 3
- head_gain: float32 [16, 128], P('head'), may hold values from 0.5 to 1.5
- w_out: bfloat16 [2048, 2048], P('head'), may hold values from -0.25 to 0.25
- w_up: bfloat16 [2048, 2, 5632], P(None, None, 'head'), may hold values from -0.125 to 0.125
- w_down: bfloat16 [5632, 2048], P('head'), may hold values from -0.15625 to 0.15625
- seq_first: int32 [32], P('seq'), may hold values from 0 to 1, as said below
- cotangent: float32 [2048, 2048], P('seq'), may hold values from -6 to 6
Outputs:
- output: float32 [2048, 2048], P('seq')
- grad_inputs: float32 [2048, 2048], P('seq')
- grad_gains: float32 [2, 2048], replicated
- grad_w_proj: float32 [2048, 4, 2048], P('seq', None, 'head')
- grad_w_gates: float32 [2, 2048, 16], P(None, None, 'head')
- grad_decay: float32 [2, 16], P(None, 'head')
- grad_conv_w: float32 [3, 4, 2048], P(None, None, 'head')
- grad_head_gain: float32 [16, 128], P('head')
- grad_w_out: float32 [2048, 2048], P('head', 'seq')
- grad_w_up: float32 [2048, 2, 5632], P('seq', None, 'head')
- grad_w_down: float32 [5632, 2048], P('head', 'seq')
The draws below stay inside these ranges and needn't reach their ends.
Inputs may be any that keep to these rules, and one draw needn't show every extreme that they name: seq_first[0] is 1. One sequence begins on the first device of seq and ends on the last one.
All inputs are finite; a program needn't handle non-finite values.
Results may differ from the reference program's by a relative error of at most 0.033.
Values may be sent and summed in bfloat16 or wider, within the bound.
A program may use at most 256 MiB of HBM per device.

```python
from functools import partial
import jax
import jax.numpy as jnp
from jax import lax

D = 2048
HEADS = 16
HDIM = 128
FF = 5632
GROUP = 64
KCONV = 4
TOK_DEV = 256
INNER = 2048
TOKENS = 2048
GROUPS = 32


def draw_decay(key, part):
    key = jax.random.fold_in(key, 7)
    rate_key, bias_key = jax.random.split(key)
    rate = jax.random.uniform(rate_key, (HEADS,), jnp.float32, -9.0, -1.0)
    bias = jax.random.uniform(bias_key, (HEADS,), jnp.float32, -1.0, 1.0)
    return jnp.stack([rate, bias])


def draw_seq_first(key, part):
    key = jax.random.fold_in(key, 11)
    keys_split = jax.random.split(key, 3)
    per_device = TOK_DEV // GROUP
    begin = jax.random.randint(keys_split[0], (), 0, per_device)
    finish = jax.random.randint(keys_split[1], (), GROUPS - per_device + 1, GROUPS + 1)
    position = jnp.arange(GROUPS)
    extra = jax.random.randint(keys_split[2], (GROUPS,), 0, 2) == 0
    outside = (position < begin) | (position > finish)
    flags = (position == 0) | (position == begin) | (position == finish) | extra & outside
    return flags.astype(jnp.int32)


def level_of(key, extent, pieces, least, high):
    loudness, own = 1.0, jax.random.fold_in(key, 6)
    for dim, blocks in pieces:
        heights = jnp.exp(jax.random.uniform(jax.random.fold_in(own, dim), (blocks,), jnp.float32, least / len(pieces), high / len(pieces)))
        loudness = loudness * jnp.repeat(heights, extent[dim] // blocks).reshape([-1 if axis == dim else 1 for axis in range(len(extent))])
    return loudness


def gaussian(key, dims, scale, bound, pieces=(), held_as=jnp.bfloat16):
    drawn = jax.random.normal(key, dims, jnp.float32) * scale
    if len(pieces) > 0:
        drawn = level_of(key, dims, pieces, -0.22, 0.18) * drawn
    return jnp.clip(drawn, min=-bound, max=bound).astype(held_as)


def setup_inputs(seed: int = 0) -> dict:
    splits = jax.random.split(jax.random.key(seed), 13)
    return {
        "inputs": gaussian(splits[0], (TOKENS, D), 1.0, 6.0, ((0, 8),), jnp.float32),
        "gains": jnp.clip(1.0 + 0.1 * jax.random.normal(splits[1], (2, D), jnp.float32), 0.5, 1.5),
        "w_proj": gaussian(splits[2], (D, 4, INNER), D ** -0.5, 0.125, ((2, 4),)),
        "w_gates": gaussian(splits[3], (2, D, HEADS), D ** -0.5, 0.125, ((2, 4),)),
        "decay": draw_decay(jax.random.fold_in(splits[12], 71), 0),
        "conv_w": gaussian(splits[5], (3, KCONV, INNER), KCONV ** -0.5, 3.0, ((2, 4),), jnp.float32),
        "head_gain": jnp.clip(1.0 + 0.1 * jax.random.normal(splits[6], (HEADS, HDIM), jnp.float32), 0.5, 1.5),
        "w_out": gaussian(splits[7], (INNER, D), (INNER // 4) ** -0.5, 0.25, ((0, 4),)),
        "w_up": gaussian(splits[8], (D, 2, FF), D ** -0.5, 0.125, ((2, 4),)),
        "w_down": gaussian(splits[9], (FF, D), (FF // 4) ** -0.5, 0.15625, ((0, 4),)),
        "seq_first": draw_seq_first(jax.random.fold_in(splits[12], 71), 0),
        "cotangent": gaussian(splits[11], (TOKENS, D), 1.0, 6.0, ((0, 8),), jnp.float32),
    }


EPS = 1e-06
HIGH = lax.Precision.HIGHEST

@jax.custom_vjp
def low(v):
    return lax.optimization_barrier(v.astype(jnp.bfloat16)).astype(jnp.float32)

@jax.custom_vjp
def low_back(v):
    return v

def low_keep(v):
    return (low(v), None)

def low_pass(kept, grad):
    return (grad,)

def back_keep(v):
    return (v, None)

def back_low(kept, grad):
    return (low(grad),)
low.defvjp(low_keep, low_pass)
low_back.defvjp(back_keep, back_low)

def rms_scale(values, gain):
    return values * lax.rsqrt(lax.optimization_barrier(jnp.mean(values * values, axis=-1, keepdims=True)) + EPS) * gain

def matmul_heads(left, right):
    return jnp.einsum('hij,hjk->hik', left, right, precision=HIGH)

def conv_gates(extended, gate_in, conv_w, decay, first_flags):
    tokens = gate_in.shape[0]
    width = conv_w.shape[1]
    offset = jnp.arange(tokens) % GROUP
    starts = jnp.repeat(first_flags, GROUP).astype(jnp.float32)
    conv_sum = jnp.zeros((tokens,) + extended.shape[1:], jnp.float32)
    for tap_index in range(width):
        keep_tap = 1.0 - starts * (offset < width - 1 - tap_index).astype(jnp.float32)
        conv_sum = conv_sum + conv_w[:, tap_index][None] * extended[tap_index:tap_index + tokens] * keep_tap[:, None, None]
    heads = decay.shape[1]
    activated = jax.nn.silu(conv_sum).reshape(tokens, 3, heads, -1)
    queries = activated[:, 0]
    keys_all = activated[:, 1]
    values = activated[:, 2]
    queries = queries * lax.rsqrt(lax.optimization_barrier(jnp.sum(queries * queries, axis=-1, keepdims=True)) + EPS) * queries.shape[-1] ** (-0.5)
    keys_all = keys_all * lax.rsqrt(lax.optimization_barrier(jnp.sum(keys_all * keys_all, axis=-1, keepdims=True)) + EPS)
    strength = jax.nn.sigmoid(gate_in[:, 0])
    logdecay = -jnp.exp(decay[0]) * jax.nn.softplus(gate_in[:, 1] + decay[1])
    return (queries, keys_all, values, strength, logdecay)

def to_blocks(array):
    blocks = array.reshape((-1, GROUP) + array.shape[1:])
    return jnp.moveaxis(blocks, 1, 2)

def group_terms(queries, keys_all, values, strength, logdecay):
    query_blocks = to_blocks(queries)
    key_blocks = to_blocks(keys_all)
    value_blocks = to_blocks(values)
    strength_blocks = to_blocks(strength)
    cumulative = jnp.cumsum(to_blocks(logdecay), axis=-1)
    growth = jnp.exp(cumulative)
    size = cumulative.shape[-1]
    lower_strict = jnp.tril(jnp.ones((size, size), jnp.float32), -1)
    lower_incl = jnp.tril(jnp.ones((size, size), jnp.float32))
    spread = cumulative[..., :, None] - cumulative[..., None, :]
    fade_strict = jnp.exp(jnp.where(lower_strict > 0, spread, 0.0)) * lower_strict
    fade_incl = jnp.exp(jnp.where(lower_incl > 0, spread, 0.0)) * lower_incl
    key_gram = jnp.einsum('nhid,nhjd->nhij', key_blocks, key_blocks, precision=HIGH)
    system = jnp.eye(size, dtype=jnp.float32) + strength_blocks[..., :, None] * key_gram * fade_strict
    right = jnp.concatenate([strength_blocks[..., None] * key_blocks * growth[..., None], strength_blocks[..., None] * value_blocks], axis=-1)
    solved = jax.scipy.linalg.solve_triangular(system, right, lower=True, unit_diagonal=True)
    hdim = key_blocks.shape[-1]
    weights_w = solved[..., :hdim]
    values_u = solved[..., hdim:]
    scores = jnp.einsum('nhid,nhjd->nhij', query_blocks, key_blocks, precision=HIGH) * fade_incl
    key_fade = key_blocks * jnp.exp(cumulative[..., -1:] - cumulative)[..., None]
    query_grow = query_blocks * growth[..., None]
    last_growth = growth[..., -1]
    return (query_grow, scores, weights_w, values_u, key_fade, last_growth)

def core(terms, state_in, keep):

    def advance(state, item):
        query_grow, scores, weights_w, values_u, key_fade, last_growth, keep_one = item
        state = state * keep_one
        fresh = values_u - matmul_heads(weights_w, state)
        result = matmul_heads(query_grow, state) + matmul_heads(scores, fresh)
        state = last_growth[:, None, None] * state + jnp.einsum('hcd,hce->hde', key_fade, fresh, precision=HIGH)
        return (state, result)
    state_end, results = lax.scan(advance, state_in, tuple(terms) + (keep,))
    heads = results.shape[1]
    results = jnp.moveaxis(results, 2, 1).reshape(-1, heads, results.shape[-1])
    return (results, state_end)

def out_gate(recurrent, gate_values, head_gain):
    normed = rms_scale(recurrent, head_gain)
    return (normed * jax.nn.silu(gate_values)).reshape(recurrent.shape[0], -1)

def swiglu(gate_up):
    return jax.nn.silu(gate_up[:, 0]) * gate_up[:, 1]

def forward(inputs, gains, w_proj, w_gates, decay, conv_w, head_gain, w_out, w_up, w_down, seq_first):
    tokens = inputs.shape[0]
    normed_in = low(rms_scale(inputs, gains[0]))
    projected = low_back(jnp.einsum('td,dkc->tkc', normed_in, w_proj, precision=HIGH))
    gate_in = low_back(jnp.einsum('td,idh->tih', normed_in, w_gates, precision=HIGH))
    qkv = low(projected[:, :3])
    rim = jnp.zeros((KCONV - 1,) + qkv.shape[1:], jnp.float32)
    extended = jnp.concatenate([rim, qkv], axis=0)
    queries, keys_all, values, strength, logdecay = conv_gates(extended, gate_in, conv_w, decay, seq_first)
    terms = group_terms(queries, keys_all, values, strength, logdecay)
    keep = 1.0 - seq_first.astype(jnp.float32)
    recurrent, state_end = core(terms, jnp.zeros((HEADS, HDIM, HDIM), jnp.float32), keep)
    gated = low(out_gate(recurrent, projected[:, 3].reshape(tokens, HEADS, HDIM), head_gain))
    middle = inputs + low_back(jnp.dot(gated, w_out, precision=HIGH))
    normed_mid = low(rms_scale(middle, gains[1]))
    gate_up = low_back(jnp.einsum('td,dkf->tkf', normed_mid, w_up, precision=HIGH))
    hidden = low(swiglu(gate_up))
    return middle + low_back(jnp.dot(hidden, w_down, precision=HIGH))

def reference(inputs, gains, w_proj, w_gates, decay, conv_w, head_gain, w_out, w_up, w_down, seq_first, cotangent):
    floats = tuple((array.astype(jnp.float32) for array in (inputs, gains, w_proj, w_gates, decay, conv_w, head_gain, w_out, w_up, w_down)))
    output, backward = jax.vjp(partial(forward, seq_first=seq_first), *floats)
    grads = backward(cotangent.astype(jnp.float32))
    return (output, grads[0], grads[1], grads[2], grads[3], grads[4], grads[5], grads[6], grads[7], grads[8], grads[9])
```

```python
from functools import partial

import jax
import jax.numpy as jnp
from jax import lax
from jax.sharding import PartitionSpec as P

GROUP = 64


EPS = 1e-06
HIGH = lax.Precision.HIGHEST


def shifted(array, axis, by):
    length = lax.axis_size(axis)
    pairs = [(i, i + by) for i in range(length) if 0 <= i + by < length]
    return lax.ppermute(array, axis, pairs)


def carried_in(array, axis, join, neutral):
    place = lax.axis_index(axis)
    gathered = jax.tree.map(
        lambda a, kind: lax.all_gather(a.astype(kind), axis), array, (jnp.bfloat16, jnp.bfloat16)
    )
    state = jax.tree.map(lambda a, e: jnp.zeros_like(a) + jnp.asarray(e, a.dtype), array, neutral)

    def carried_one(hop, state):
        return join(
            state,
            jax.tree.map(
                lambda a, own: lax.dynamic_index_in_dim(a, hop, 0, False).astype(own.dtype),
                gathered,
                array,
            ),
        )

    return lax.fori_loop(0, place, carried_one, state)


def prefix_2(array, axis, join, neutral):
    count = lax.axis_size(axis)
    place = lax.axis_index(axis)
    ahead = count - 1 - place
    gathered = jax.tree.map(
        lambda a, kind: lax.all_gather(a.astype(kind), axis),
        array,
        jax.tree.map(lambda a: jnp.bfloat16 if a.dtype == jnp.float32 else a.dtype, array),
    )
    state = jax.tree.map(lambda a, e: jnp.zeros_like(a) + jnp.asarray(e, a.dtype), array, neutral)

    def prefix_one(hop, state):
        source = count - 1 - hop
        return join(
            state,
            jax.tree.map(
                lambda a, own: lax.dynamic_index_in_dim(a, source, 0, False).astype(own.dtype),
                gathered,
                array,
            ),
        )

    return lax.fori_loop(0, ahead, prefix_one, state)


def rms_scale(values, gain):
    return values * lax.rsqrt(jnp.mean(values * values, axis=-1, keepdims=True) + EPS) * gain


def matmul_heads(left, right):
    return jnp.einsum("hij,hjk->hik", left, right, precision=HIGH)


def conv_gates(extended, gate_in, conv_w, decay, first_flags):
    tokens = gate_in.shape[0]
    width = conv_w.shape[1]
    offset = jnp.arange(tokens) % GROUP
    starts = jnp.repeat(first_flags, GROUP).astype(jnp.float32)
    conv_sum = jnp.zeros((tokens,) + extended.shape[1:], jnp.float32)
    for tap_index in range(width):
        keep_tap = 1.0 - starts * (offset < width - 1 - tap_index).astype(jnp.float32)
        conv_sum = (
            conv_sum
            + conv_w[:, tap_index][None]
            * extended[tap_index : tap_index + tokens]
            * keep_tap[:, None, None]
        )
    heads = decay.shape[1]
    activated = jax.nn.silu(conv_sum).reshape(tokens, 3, heads, -1)
    queries = activated[:, 0]
    keys_all = activated[:, 1]
    values = activated[:, 2]
    queries = (
        queries
        * lax.rsqrt(jnp.sum(queries * queries, axis=-1, keepdims=True) + EPS)
        * queries.shape[-1] ** (-0.5)
    )
    keys_all = keys_all * lax.rsqrt(jnp.sum(keys_all * keys_all, axis=-1, keepdims=True) + EPS)
    strength = jax.nn.sigmoid(gate_in[:, 0])
    logdecay = -jnp.exp(decay[0]) * jax.nn.softplus(gate_in[:, 1] + decay[1])
    return (queries, keys_all, values, strength, logdecay)


def to_blocks(array):
    blocks = array.reshape((-1, GROUP) + array.shape[1:])
    return jnp.moveaxis(blocks, 1, 2)


def group_terms(queries, keys_all, values, strength, logdecay):
    query_blocks = to_blocks(queries)
    key_blocks = to_blocks(keys_all)
    value_blocks = to_blocks(values)
    strength_blocks = to_blocks(strength)
    cumulative = jnp.cumsum(to_blocks(logdecay), axis=-1)
    growth = jnp.exp(cumulative)
    size = cumulative.shape[-1]
    lower_strict = jnp.tril(jnp.ones((size, size), jnp.float32), -1)
    lower_incl = jnp.tril(jnp.ones((size, size), jnp.float32))
    spread = cumulative[..., :, None] - cumulative[..., None, :]
    fade_strict = jnp.exp(jnp.where(lower_strict > 0, spread, 0.0)) * lower_strict
    fade_incl = jnp.exp(jnp.where(lower_incl > 0, spread, 0.0)) * lower_incl
    key_gram = jnp.einsum("nhid,nhjd->nhij", key_blocks, key_blocks, precision=HIGH)
    system = (
        jnp.eye(size, dtype=jnp.float32) + strength_blocks[..., :, None] * key_gram * fade_strict
    )
    right = jnp.concatenate(
        [
            strength_blocks[..., None] * key_blocks * growth[..., None],
            strength_blocks[..., None] * value_blocks,
        ],
        axis=-1,
    )
    solved = jax.scipy.linalg.solve_triangular(system, right, lower=True, unit_diagonal=True)
    hdim = key_blocks.shape[-1]
    weights_w = solved[..., :hdim]
    values_u = solved[..., hdim:]
    scores = jnp.einsum("nhid,nhjd->nhij", query_blocks, key_blocks, precision=HIGH) * fade_incl
    key_fade = key_blocks * jnp.exp(cumulative[..., -1:] - cumulative)[..., None]
    query_grow = query_blocks * growth[..., None]
    last_growth = growth[..., -1]
    return (query_grow, scores, weights_w, values_u, key_fade, last_growth)


def state_maps(terms, keep):
    query_grow, scores, weights_w, values_u, key_fade, last_growth = terms
    size = weights_w.shape[-1]
    identity_matrix = jnp.eye(size, dtype=jnp.float32)
    factor = last_growth[..., None, None] * identity_matrix - jnp.einsum(
        "nhcd,nhce->nhde", key_fade, weights_w, precision=HIGH
    )
    offset = jnp.einsum("nhcd,nhce->nhde", key_fade, values_u, precision=HIGH)
    factor = factor * keep[:, None, None, None]

    def compose(carry, item):
        return ((matmul_heads(item[0], carry[0]), matmul_heads(item[0], carry[1]) + item[1]), None)

    start = (
        jnp.broadcast_to(identity_matrix, factor.shape[1:]),
        jnp.zeros(offset.shape[1:], jnp.float32),
    )
    (matrix, constant), unused = lax.scan(compose, start, (factor, offset))
    return (matrix, constant)


def combine(earlier, later):
    return (matmul_heads(later[0], earlier[0]), matmul_heads(later[0], earlier[1]) + later[1])


def core(terms, state_in, keep):

    def advance(state, item):
        query_grow, scores, weights_w, values_u, key_fade, last_growth, keep_one = item
        state = state * keep_one
        fresh = values_u - matmul_heads(weights_w, state)
        result = matmul_heads(query_grow, state) + matmul_heads(scores, fresh)
        state = last_growth[:, None, None] * state + jnp.einsum(
            "hcd,hce->hde", key_fade, fresh, precision=HIGH
        )
        return (state, result)

    state_end, results = lax.scan(advance, state_in, tuple(terms) + (keep,))
    heads = results.shape[1]
    results = jnp.moveaxis(results, 2, 1).reshape(-1, heads, results.shape[-1])
    return (results, state_end)


def out_gate(recurrent, gate_values, head_gain):
    normed = rms_scale(recurrent, head_gain)
    return (normed * jax.nn.silu(gate_values)).reshape(recurrent.shape[0], -1)


def swiglu(gate_up):
    return jax.nn.silu(gate_up[:, 0]) * gate_up[:, 1]


def across(array, axis, mask):
    return lax.ppermute(array, axis, [(i, i ^ mask) for i in range(lax.axis_size(axis))])


def mirrored(array):
    return across(array, "seq", lax.axis_size("seq") - 2)


def mirrored_shared(array):
    half = array.shape[0] // 2
    odd = lax.axis_index("head") % 2
    mine = mirrored(lax.dynamic_slice_in_dim(array, odd * half, half, 0))
    other = across(mine, "head", 1)
    first = jnp.where(odd == 0, mine, other)
    second = jnp.where(odd == 0, other, mine)
    return jnp.concatenate([first, second], axis=0)


def own_half_columns(array, of):
    width = array.shape[1] // 2
    return lax.dynamic_slice_in_dim(array, of * width, width, 1)


def sum_in_half(partials):
    count = len(partials)
    bits = []
    bit = 1
    while bit < count:
        bits.append(bit)
        bit *= 2
    done = []
    for part, order in ((0, bits), (1, bits[::-1])):
        held = {}
        for m in range(count):
            rows = partials[m].shape[0] // 2
            held[m] = partials[m][part * rows : (part + 1) * rows]
        for bit in order:
            sent = sorted(m for m in held if m & bit)
            block = jnp.concatenate([held[m].astype(jnp.bfloat16) for m in sent], axis=0)
            got = across(block, "seq", bit).astype(jnp.float32)
            rows = got.shape[0] // len(sent)
            held = {
                m: held[m] + got[k * rows : (k + 1) * rows]
                for k, m in enumerate(sorted(m for m in held if not m & bit))
            }
        done.append(held[0])
    return jnp.concatenate(done, axis=0)


def shards(
    inputs,
    gains,
    w_proj,
    w_gates,
    decay,
    conv_w,
    head_gain,
    w_out,
    w_up,
    w_down,
    seq_first,
    cotangent,
):
    tokens = inputs.shape[0]
    heads_here = decay.shape[1]
    hdim = head_gain.shape[1]
    rim_width = conv_w.shape[1] - 1
    owners = lax.axis_size("seq")
    place = lax.axis_index("seq")
    half = place // (owners // 2)
    masks = range(owners // 2)
    kept = inputs.shape[1] // owners

    def owned(array, mask):
        return lax.dynamic_slice_in_dim(array, (place ^ mask) * kept, kept, 1)

    def owned_half(array, mask):
        within = (place ^ mask) % (owners // 2)
        return lax.dynamic_slice_in_dim(array, within * kept, kept, 1)

    normed_in, norm_in_back = jax.vjp(rms_scale, inputs, gains[0])
    normed_low = normed_in.astype(jnp.bfloat16)
    projected = jnp.einsum("td,dkc->tkc", normed_low, w_proj, preferred_element_type=jnp.float32)
    gate_in = jnp.einsum("td,idh->tih", normed_low, w_gates, preferred_element_type=jnp.float32)
    qkv_low = projected[:, :3].astype(jnp.bfloat16)
    rim = shifted(qkv_low[tokens - rim_width :], "seq", 1)
    extended = jnp.concatenate([rim, qkv_low], axis=0).astype(jnp.float32)
    mixed, mixed_back = jax.vjp(
        partial(conv_gates, first_flags=seq_first), extended, gate_in, conv_w, decay
    )
    terms, terms_back = jax.vjp(group_terms, mixed[0], mixed[1], mixed[2], mixed[3], mixed[4])
    keep = 1.0 - seq_first.astype(jnp.float32)
    factors, offsets = state_maps(terms, keep)
    identity = (
        jnp.broadcast_to(jnp.eye(hdim, dtype=jnp.float32), factors.shape),
        jnp.zeros_like(offsets),
    )
    prefix = carried_in((factors, offsets), "seq", combine, identity)
    state_in = prefix[1]
    (recurrent, state_end), core_back = jax.vjp(partial(core, keep=keep), terms, state_in)
    gate_values = projected[:, 3].reshape(tokens, heads_here, hdim)
    gated, gated_back = jax.vjp(out_gate, recurrent, gate_values, head_gain)
    gated_low = gated.astype(jnp.bfloat16)
    attn_part = jnp.dot(gated_low, w_out, preferred_element_type=jnp.float32)
    middle = inputs + lax.psum(attn_part.astype(jnp.bfloat16), "head").astype(jnp.float32)
    normed_mid, norm_mid_back = jax.vjp(rms_scale, middle, gains[1])
    normed_mid_low = normed_mid.astype(jnp.bfloat16)
    gate_up = jnp.einsum("td,dkf->tkf", normed_mid_low, w_up, preferred_element_type=jnp.float32)
    hidden, hidden_back = jax.vjp(swiglu, gate_up)
    hidden_low = hidden.astype(jnp.bfloat16)
    mlp_part = jnp.dot(hidden_low, w_down, preferred_element_type=jnp.float32)
    output = middle + lax.psum(mlp_part.astype(jnp.bfloat16), "head").astype(jnp.float32)
    grad_low = cotangent.astype(jnp.bfloat16)
    grad_hidden = jnp.einsum("td,fd->tf", grad_low, w_down, preferred_element_type=jnp.float32)
    (grad_gate_up,) = hidden_back(grad_hidden)
    grad_gate_up_low = grad_gate_up.astype(jnp.bfloat16)
    normed_mid_far = mirrored_shared(normed_mid_low)
    grad_low_far = mirrored_shared(grad_low)
    gate_up_far = jnp.einsum(
        "td,dkf->tkf", normed_mid_far, w_up, preferred_element_type=jnp.float32
    )
    grad_hidden_far = jnp.einsum(
        "td,fd->tf", grad_low_far, w_down, preferred_element_type=jnp.float32
    )
    hidden_far, hidden_far_back = jax.vjp(swiglu, gate_up_far)
    (grad_gate_up_far,) = hidden_far_back(grad_hidden_far)
    both = lambda near, far: jnp.concatenate([near, far.astype(near.dtype)], axis=0)
    hidden_both = both(hidden_low, hidden_far)
    grad_gate_up_both = both(grad_gate_up_low, grad_gate_up_far)
    normed_mid_both = both(normed_mid_low, normed_mid_far)
    grad_low_both = both(grad_low, grad_low_far)
    up_parts = [
        jnp.einsum(
            "td,tkf->dkf", owned(normed_mid_both, m), grad_gate_up_both, preferred_element_type=jnp.float32
        ).astype(jnp.bfloat16)
        for m in masks
    ]
    down_parts = [
        jnp.einsum(
            "tf,td->fd", hidden_both, owned(grad_low_both, m), preferred_element_type=jnp.float32
        ).astype(jnp.bfloat16)
        for m in masks
    ]
    grad_normed_mid = lax.psum(
        jnp.einsum(
            "tkf,dkf->td", grad_gate_up_low, w_up, preferred_element_type=jnp.float32
        ).astype(jnp.bfloat16),
        "head",
    ).astype(jnp.float32)
    grad_middle_norm, grad_gain_mid = norm_mid_back(grad_normed_mid)
    grad_middle = cotangent + grad_middle_norm
    grad_attn_low = grad_middle.astype(jnp.bfloat16)
    gated_both = both(gated_low, mirrored(gated_low))
    grad_attn_far = mirrored_shared(own_half_columns(grad_attn_low, 1 - half))
    grad_attn_both = both(own_half_columns(grad_attn_low, half), grad_attn_far)
    wout_parts = [
        jnp.einsum(
            "tc,td->cd", gated_both, owned_half(grad_attn_both, m), preferred_element_type=jnp.float32
        ).astype(jnp.bfloat16)
        for m in masks
    ]
    grad_gated = jnp.einsum("td,cd->tc", grad_attn_low, w_out, preferred_element_type=jnp.float32)
    grad_recurrent, grad_gate_values, grad_head_gain = gated_back(grad_gated)
    grad_terms_out, local_state_grad = core_back((grad_recurrent, jnp.zeros_like(state_in)))
    suffix = prefix_2((jnp.swapaxes(factors, 1, 2), local_state_grad), "seq", combine, identity)
    grad_terms_state, unused_grad = core_back((jnp.zeros_like(recurrent), suffix[1]))
    grad_terms = jax.tree.map(jnp.add, grad_terms_out, grad_terms_state)
    grad_mixed = terms_back(grad_terms)
    grad_extended, grad_gate_in, grad_conv, grad_decay = mixed_back(grad_mixed)
    rim_grad = shifted(grad_extended[:rim_width], "seq", -1)
    grad_qkv = jnp.concatenate(
        [grad_extended[rim_width:tokens], grad_extended[tokens:] + rim_grad], axis=0
    )
    grad_projected = jnp.concatenate(
        [grad_qkv, grad_gate_values.reshape(tokens, 1, -1)], axis=1
    ).astype(jnp.bfloat16)
    grad_gate_low = grad_gate_in.astype(jnp.bfloat16)
    normed_far = mirrored_shared(own_half_columns(normed_low, 1 - half))
    normed_both = both(own_half_columns(normed_low, half), normed_far)
    grad_projected_both = both(grad_projected, mirrored(grad_projected))
    proj_parts = [
        jnp.einsum(
            "td,tkc->dkc", owned_half(normed_both, m), grad_projected_both, preferred_element_type=jnp.float32
        ).astype(jnp.bfloat16)
        for m in masks
    ]
    grad_wgates = jnp.einsum(
        "td,tih->idh", normed_low, grad_gate_low, preferred_element_type=jnp.float32
    )
    grad_normed_part = jnp.einsum(
        "tkc,dkc->td", grad_projected, w_proj, preferred_element_type=jnp.float32
    )
    grad_normed_part = grad_normed_part + jnp.einsum(
        "tih,idh->td", grad_gate_low, w_gates, preferred_element_type=jnp.float32
    )
    grad_normed_in = lax.psum(grad_normed_part.astype(jnp.bfloat16), "head").astype(jnp.float32)
    grad_in_norm, grad_gain_in = norm_in_back(grad_normed_in)
    grad_inputs = grad_middle + grad_in_norm
    summed = (
        lax.psum(grad_conv.astype(jnp.bfloat16), "seq").astype(jnp.float32),
        lax.psum(grad_wgates.astype(jnp.bfloat16), "seq").astype(jnp.float32),
        lax.psum(grad_decay.astype(jnp.bfloat16), "seq").astype(jnp.float32),
        lax.psum(grad_head_gain.astype(jnp.bfloat16), "seq").astype(jnp.float32),
        lax.psum(jnp.stack([grad_gain_in, grad_gain_mid]).astype(jnp.bfloat16), "seq").astype(
            jnp.float32
        ),
    )
    grad_proj_part = sum_in_half(proj_parts)
    grad_up_part = sum_in_half(up_parts)
    grad_wout_part = sum_in_half(wout_parts)
    grad_down_part = sum_in_half(down_parts)
    return (
        output,
        grad_inputs,
        summed[4],
        grad_proj_part,
        summed[1],
        summed[2],
        summed[0],
        summed[3],
        grad_wout_part,
        grad_up_part,
        grad_down_part,
    )


def solution(mesh):
    placed = (
        P("seq", None),
        P(),
        P(None, None, "head"),
        P(None, None, "head"),
        P(None, "head"),
        P(None, None, "head"),
        P("head", None),
        P("head", None),
        P(None, None, "head"),
        P("head", None),
        P("seq"),
        P("seq", None),
    )
    return jax.shard_map(
        shards,
        mesh=mesh,
        in_specs=placed,
        out_specs=(
            P("seq", None),
            P("seq", None),
            P(),
            P("seq", None, "head"),
            P(None, None, "head"),
            P(None, "head"),
            P(None, None, "head"),
            P("head", None),
            P("head", "seq"),
            P("seq", None, "head"),
            P("head", "seq"),
        ),
        check_vma=False,
    )
```

```python
import functools

import jax
import jax.numpy as jnp
from jax import lax
from jax.experimental import pallas as pl
from jax.experimental.pallas import tpu as pltpu
from jax.sharding import PartitionSpec as P

EPS = 1e-06
GROUP = 64
BF = jnp.bfloat16
F32 = jnp.float32


def mm(a, b, ca=1, cb=0):
    return lax.dot_general(
        a.astype(BF), b.astype(BF), (((ca,), (cb,)), ((), ())), preferred_element_type=F32
    )


def split(a):
    high = a.astype(BF)
    return high, (a - high.astype(F32)).astype(BF)


def mm3(a, b, ca=1, cb=0):
    ah, al = split(a)
    bh, bl = split(b)
    return mm(ah, bh, ca, cb) + (mm(ah, bl, ca, cb) + mm(al, bh, ca, cb))


def mm_exact(a, b):
    return lax.dot_general(
        a, b, (((1,), (0,)), ((), ())), preferred_element_type=F32, precision=lax.Precision.HIGHEST
    )


def sigmoid(v):
    return 1.0 / (1.0 + jnp.exp(-v))


def softplus(v):
    return jnp.maximum(v, 0.0) + jnp.log1p(jnp.exp(-jnp.abs(v)))


def block_sums(first_ref, shape, axis):
    block = lax.broadcasted_iota(jnp.int32, shape, axis) // GROUP
    seen = jnp.zeros(shape, F32)
    starts = jnp.zeros(shape, F32)
    for b in range(first_ref.shape[0]):
        flag = first_ref[b].astype(F32)
        seen = seen + jnp.where(block >= b, flag, 0.0)
        starts = starts + jnp.where(block == b, flag, 0.0)
    return seen, starts


def gate_rows(gates_ref, decay_ref, heads):
    rows = []
    size = gates_ref.shape[1]
    for h in range(heads):
        rate = jnp.exp(jnp.full((1, size), decay_ref[0, h], F32))
        bias = decay_ref[1, h]
        rows.append(-rate * softplus(gates_ref[heads + h : heads + h + 1, :] + bias))
    return jnp.concatenate(rows, axis=0)


def tap_keeps(starts, taps):
    size = starts.shape[0]
    offset = lax.broadcasted_iota(jnp.int32, (size, 1), 0) % GROUP
    return [1.0 - jnp.where(offset < taps - 1 - j, starts, 0.0) for j in range(taps)]


def convolved(ext_ref, part, cols, convw_ref, keeps):
    size = ext_ref.shape[1] - 8
    taps = len(keeps)
    total = None
    for j in range(taps):
        shifted = ext_ref[part, pl.ds(8 - (taps - 1) + j, size), cols]
        if j < taps - 1:
            shifted = shifted * keeps[j]
        term = shifted * convw_ref[part, j : j + 1, cols]
        total = term if total is None else total + term
    return total


def fade_of(cum_col, cum_row, seen_col, seen_row):
    size = cum_col.shape[0]
    row = lax.broadcasted_iota(jnp.int32, (size, size), 0)
    col = lax.broadcasted_iota(jnp.int32, (size, size), 1)
    inside = (row > col) & (seen_col == seen_row)
    fade = jnp.where(inside, jnp.exp(jnp.minimum(cum_col - cum_row, 0.0)), 0.0)
    return jnp.where(row == col, 1.0, fade), inside


def fill_ext(ext, proj_ref, rim_ref):
    size = proj_ref.shape[1]
    for part in range(3):
        ext[part, pl.ds(0, 8), :] = rim_ref[part]
        ext[part, pl.ds(8, size), :] = proj_ref[part].astype(BF).astype(F32)


def tri(size, upper):
    row = lax.broadcasted_iota(jnp.int32, (size, size), 0)
    col = lax.broadcasted_iota(jnp.int32, (size, size), 1)
    return jnp.where((row <= col) if upper else (row >= col), 1.0, 0.0).astype(F32)


class Scan:
    def __init__(self, first_ref, decay_ref, gates_ref, heads):
        size = gates_ref.shape[1]
        self.log_rows = gate_rows(gates_ref, decay_ref, heads)
        self.seen_row, _ = block_sums(first_ref, (1, size), 1)
        self.seen_col, self.starts = block_sums(first_ref, (size, 1), 0)
        padded = jnp.concatenate([self.log_rows, jnp.zeros((8 - heads, size), F32)], axis=0)
        self.cum_rows = mm_exact(padded, tri(size, True))
        strength_rows = sigmoid(gates_ref[0:heads, :])
        both = jnp.concatenate([self.cum_rows[0:heads], strength_rows], axis=0)
        both = jnp.concatenate([both, jnp.zeros((128 - 2 * heads, size), F32)], axis=0)
        cols = both.T
        self.cum_cols = [cols[:, h : h + 1] for h in range(heads)]
        self.strength = [cols[:, heads + h : heads + h + 1] for h in range(heads)]

    def of(self, h):
        cum_col, cum_row = self.cum_cols[h], self.cum_rows[h : h + 1, :]
        size = cum_col.shape[0]
        last = cum_col[size - 1 : size, :]
        fade, inside = fade_of(cum_col, cum_row, self.seen_col, self.seen_row)
        growth = jnp.where(self.seen_col == 0.0, jnp.exp(cum_col), 0.0)
        last_seen = self.seen_col[size - 1 : size, :]
        to_end = jnp.where(self.seen_col == last_seen, jnp.exp(jnp.minimum(last - cum_col, 0.0)), 0.0)
        carry = jnp.where(last_seen == 0.0, jnp.exp(last), 0.0)
        return fade, inside, growth, to_end, carry


def unit(a, scale):
    inverse = lax.rsqrt(jnp.sum(a * a, axis=1, keepdims=True) + EPS)
    return a * (inverse * scale), inverse


MESH = pl.DeviceIdType.MESH


class Ring:
    def __init__(self):
        self.count = lax.axis_size("seq")
        self.place = lax.axis_index("seq")
        self.head = lax.axis_index("head")
        self.side = self.place % 2
        self.pair = self.place // 2
        self.pairs = self.count // 2
        self.partner = self.place + 1 - 2 * self.side
        self.cross = self.place + 2 * self.side - 1

    def device(self, place):
        return (place, self.head)

    def greet(self):
        barrier = pltpu.get_barrier_semaphore()

        def tell(place):
            pl.semaphore_signal(barrier, inc=1, device_id=self.device(place), device_id_type=MESH)

        tell(self.partner)
        for place in (self.place - 2, self.place + 2, self.cross):
            pl.when((place >= 0) & (place < self.count))(functools.partial(tell, place))

    def met(self):
        inside = lambda place: jnp.where((place >= 0) & (place < self.count), 1, 0)
        known = 1 + inside(self.place - 2) + inside(self.place + 2) + inside(self.cross)
        pl.semaphore_wait(pltpu.get_barrier_semaphore(), known)

    def copy(self, source, target, sems, index, place):
        return pltpu.make_async_remote_copy(
            src_ref=source, dst_ref=target, send_sem=sems[0].at[index], recv_sem=sems[1].at[index],
            device_id=self.device(place), device_id_type=MESH,
        )


def forward_kernel(
    heads, first_ref, decay_ref, gates_ref, proj_ref, convw_ref, gain_ref,
    gated_ref, rec_ref, lift_ref, inv_ref, solved_ref, gram_ref, score_ref, state_ref, pair_ref, rim_ref,
    ext, base, maps, other, chain_in, chain_out, state_out, state_in, rim_out, rim_in, send_sems, recv_sems,
):
    ring = Ring()
    ring.greet()
    sems = (send_sems, recv_sems)
    size = proj_ref.shape[1]
    hdim = proj_ref.shape[2] // heads
    taps = convw_ref.shape[1]
    mine = heads // 2
    for part in range(3):
        rows = proj_ref[part].astype(BF).astype(F32)
        ext[part, pl.ds(8, size), :] = rows
        rim_out[part] = rows[size - 8 :, :]
    scan = Scan(first_ref, decay_ref, gates_ref, heads)
    ring.met()
    has_before, has_after = ring.place > 0, ring.place < ring.count - 1
    rim_copy = ring.copy(rim_out, rim_in, sems, 0, ring.place + 1)
    pl.when(has_after)(rim_copy.start)

    @pl.when(ring.place == 0)
    def _():
        rim_in[...] = jnp.zeros_like(rim_in)

    keeps = tap_keeps(scan.starts, taps)
    eye = lax.broadcasted_iota(jnp.int32, (size, size), 0) == lax.broadcasted_iota(
        jnp.int32, (size, size), 1
    )
    apart = lax.broadcasted_iota(jnp.int32, (size, size), 0) ^ lax.broadcasted_iota(
        jnp.int32, (size, size), 1
    )
    pl.when(has_before)(rim_copy.wait_recv)
    for part in range(3):
        ext[part, pl.ds(0, 8), :] = rim_in[part]
        rim_ref[part] = rim_in[part]
    held = []
    for h in range(heads):
        cols = pl.ds(h * hdim, hdim)
        acts = []
        for part in range(3):
            u = convolved(ext, part, cols, convw_ref, keeps)
            acts.append(u * sigmoid(u))
        q, _ = unit(acts[0], hdim ** -0.5)
        k, _ = unit(acts[1], 1.0)
        v = acts[2]
        fade, inside, growth, to_end, carry = scan.of(h)
        beta = scan.strength[h]
        gram = mm(k, k, 1, 1) * jnp.where(inside, fade, 0.0)
        score = mm(q, k, 1, 1) * fade
        gram_ref[h] = gram.astype(BF)
        score_ref[h] = score.astype(BF)
        system = beta * gram
        held.append((q, k, v, growth, to_end, carry, beta, system))
    inverses = [jnp.where(eye, 1.0, 0.0) - jnp.where(apart == 1, t[7], 0.0) for t in held]
    block = 2
    while block < size:
        level = (apart >= block) & (apart < 2 * block)
        inner = [mm(jnp.where(level, t[7], 0.0), inv) for t, inv in zip(held, inverses)]
        inverses = [inv - mm(inv, y) for inv, y in zip(inverses, inner)]
        block *= 2
    left = [jnp.where(eye, 1.0, 0.0) - inv - mm3(t[7], inv) for t, inv in zip(held, inverses)]
    inverses = [inv + mm(inv, r) for inv, r in zip(inverses, left)]
    for h in range(heads):
        q, k, v, growth, to_end, carry, beta, system = held[h]
        inv = inverses[h].astype(BF)
        inv_ref[h] = inv
        right = jnp.concatenate([beta * growth * k, beta * v], axis=1)
        solved = mm(inv, right).astype(BF)
        solved_ref[h] = solved
        ends = mm(k * to_end, solved, 0, 0)
        factor = jnp.where(eye[:hdim, :hdim], carry, 0.0) - ends[:, :hdim]
        maps[h] = jnp.concatenate([factor, ends[:, hdim:]], axis=1).astype(BF)
    map_copy = ring.copy(
        maps.at[pl.ds((1 - ring.side) * mine, mine)], other, sems, 1, ring.partner
    )
    map_copy.start()
    for h in range(heads):
        q, k, v, growth, to_end, carry, beta, system = held[h]
        mixed = mm(score_ref[h], solved_ref[h])
        lift_ref[h] = (q * growth - mixed[:, :hdim]).astype(BF)
        base[h] = mixed[:, hdim:]
    map_copy.wait_recv()
    chain_copy = ring.copy(chain_out, chain_in, sems, 2, ring.place + 2)
    from_before, to_after = ring.pair > 0, ring.pair < ring.pairs - 1
    whole, before = [], []
    for i in range(mine):
        own, far = maps[ring.side * mine + i], other[i]
        early = jnp.where(ring.side == 0, own, far)
        late = jnp.where(ring.side == 0, far, own)
        both = mm(late[:, :hdim], early)
        whole.append((both[:, :hdim].astype(BF), both[:, hdim:] + late[:, hdim:].astype(F32)))
        before.append(early)
        pair_ref[0, i] = early[:, :hdim]
        pair_ref[1, i] = late[:, :hdim]
        pair_ref[2, i] = whole[i][0]

    @pl.when(jnp.logical_not(from_before))
    def _():
        chain_in[...] = jnp.zeros_like(chain_in)

    pl.when(from_before)(chain_copy.wait_recv)
    for i in range(mine):
        chain_out[i] = (mm(whole[i][0], chain_in[i]) + whole[i][1]).astype(BF)
    pl.when(to_after)(chain_copy.start)
    for i in range(mine):
        first = chain_in[i]
        second = (mm(before[i][:, :hdim], first) + before[i][:, hdim:].astype(F32)).astype(BF)
        state_out[i] = jnp.where(ring.side == 0, second, first)
        state_ref[ring.side * mine + i] = jnp.where(ring.side == 0, first, second)
    state_copy = ring.copy(state_out, state_in, sems, 3, ring.partner)
    state_copy.start()
    state_copy.wait_recv()
    for i in range(mine):
        state_ref[(1 - ring.side) * mine + i] = state_in[i]
    for h in range(heads):
        cols = pl.ds(h * hdim, hdim)
        rec = mm(lift_ref[h], state_ref[h]) + base[h]
        rec_ref[h] = rec
        inverse = lax.rsqrt(jnp.mean(rec * rec, axis=1, keepdims=True) + EPS)
        gate = proj_ref[3, :, cols]
        gated_ref[:, cols] = (
            rec * inverse * gain_ref[h : h + 1, :] * (gate * sigmoid(gate))
        ).astype(BF)
    pl.when(has_after)(rim_copy.wait_send)
    map_copy.wait_send()
    pl.when(to_after)(chain_copy.wait_send)
    state_copy.wait_send()


def recurrent_forward(first, decay, gates, proj, convw, gain):
    heads = decay.shape[1]
    parts, size, width = proj.shape
    hdim = width // heads
    mine = heads // 2
    shape = jax.ShapeDtypeStruct
    vm = pl.BlockSpec(memory_space=pltpu.VMEM)
    sm = pl.BlockSpec(memory_space=pltpu.SMEM)
    square = shape((heads, size, size), BF)
    states = lambda count: pltpu.VMEM((count, hdim, hdim), BF)
    return pl.pallas_call(
        functools.partial(forward_kernel, heads),
        out_shape=(
            shape((size, width), BF), shape((heads, size, hdim), F32), shape((heads, size, hdim), BF),
            square, shape((heads, size, 2 * hdim), BF), square, square,
            shape((heads, hdim, hdim), BF), shape((3, mine, hdim, hdim), BF), shape((3, 8, width), F32),
        ),
        in_specs=[sm, sm, vm, vm, vm, vm],
        out_specs=(vm,) * 10,
        scratch_shapes=[
            pltpu.VMEM((3, size + 8, width), F32), pltpu.VMEM((heads, size, hdim), F32),
            pltpu.VMEM((heads, hdim, 2 * hdim), BF), pltpu.VMEM((mine, hdim, 2 * hdim), BF),
            states(mine), states(mine), states(mine), states(mine),
            pltpu.VMEM((3, 8, width), F32), pltpu.VMEM((3, 8, width), F32),
            pltpu.SemaphoreType.DMA((4,)), pltpu.SemaphoreType.DMA((4,)),
        ],
        compiler_params=pltpu.CompilerParams(
            vmem_limit_bytes=56 << 20, collective_id=1, has_side_effects=True
        ),
        name="recurrent_forward",
    )(first, decay, gates, proj, convw, gain)


def unit_back(a, inverse, scale, grad):
    along = jnp.sum(a * grad, axis=1, keepdims=True)
    return scale * (inverse * grad - a * (inverse * inverse * inverse * along))


def backward_kernel(
    heads, first_ref, decay_ref, gates_ref, proj_ref, rim_ref, convw_ref,
    gain_ref, grad_gated_ref, rec_ref, lift_ref, inv_ref, solved_ref, gram_ref, score_ref, state_ref, pair_ref,
    grad_proj_ref, grad_convw_ref, grad_gates_ref, grad_decay_ref, grad_gain_ref,
    ext, back, grad_rec, local, other, chain_in, chain_out, state_out, state_in, grad_end_all,
    edge_out, edge_in, last_rows, send_sems, recv_sems,
):
    ring = Ring()
    ring.greet()
    sems = (send_sems, recv_sems)
    mine = heads // 2
    size = proj_ref.shape[1]
    hdim = proj_ref.shape[2] // heads
    taps = convw_ref.shape[1]
    for h in range(heads):
        cols = pl.ds(h * hdim, hdim)
        rec = rec_ref[h]
        inverse = lax.rsqrt(jnp.mean(rec * rec, axis=1, keepdims=True) + EPS)
        gate = proj_ref[3, :, cols]
        sig = sigmoid(gate)
        gain = gain_ref[h : h + 1, :]
        normed = rec * inverse
        grad_gated = grad_gated_ref[:, cols]
        by_normed = grad_gated * normed
        grad_proj_ref[3, :, cols] = (
            by_normed * gain * (sig * (1.0 + gate * (1.0 - sig)))
        ).astype(BF)
        active = gate * sig
        grad_gain_ref[h : h + 1, :] = jnp.sum(by_normed * active, axis=0, keepdims=True)
        grad_normed = grad_gated * (active * gain)
        along = jnp.mean(rec * grad_normed, axis=1, keepdims=True)
        grad_rec[h] = inverse * grad_normed - rec * (inverse * inverse * inverse * along)
        local[h] = mm(lift_ref[h], grad_rec[h], 0, 0).astype(BF)
    ring.met()
    local_copy = ring.copy(
        local.at[pl.ds((1 - ring.side) * mine, mine)], other, sems, 0, ring.partner
    )
    local_copy.start()
    fill_ext(ext, proj_ref, rim_ref)
    scan = Scan(first_ref, decay_ref, gates_ref, heads)
    keeps = tap_keeps(scan.starts, taps)
    local_copy.wait_recv()
    chain_copy = ring.copy(chain_out, chain_in, sems, 1, ring.place - 2)
    from_after, to_before = ring.pair < ring.pairs - 1, ring.pair > 0

    @pl.when(jnp.logical_not(from_after))
    def _():
        chain_in[...] = jnp.zeros_like(chain_in)

    pl.when(from_after)(chain_copy.wait_recv)
    lates = []
    for i in range(mine):
        own, far = local[ring.side * mine + i], other[i]
        early = jnp.where(ring.side == 0, own, far)
        late = jnp.where(ring.side == 0, far, own)
        lates.append(late.astype(F32))
        both = early.astype(F32) + mm(pair_ref[0, i], late, 0, 0)
        chain_out[i] = (mm(pair_ref[2, i], chain_in[i], 0, 0) + both).astype(BF)
    pl.when(to_before)(chain_copy.start)
    for i in range(mine):
        last = chain_in[i]
        mid = (mm(pair_ref[1, i], last, 0, 0) + lates[i]).astype(BF)
        state_out[i] = jnp.where(ring.side == 0, last, mid)
        grad_end_all[ring.side * mine + i] = jnp.where(ring.side == 0, mid, last)
    state_copy = ring.copy(state_out, state_in, sems, 2, ring.partner)
    state_copy.start()
    state_copy.wait_recv()
    for i in range(mine):
        grad_end_all[(1 - ring.side) * mine + i] = state_in[i]
    grad_cums = []
    grad_strengths = []
    for h in range(heads):
        cols = pl.ds(h * hdim, hdim)
        fade, inside, growth, to_end, carry = scan.of(h)
        beta = scan.strength[h]
        sums, sigs, acts = [], [], []
        for part in range(3):
            u = convolved(ext, part, cols, convw_ref, keeps)
            s = sigmoid(u)
            sums.append(u)
            sigs.append(s)
            acts.append(u * s)
        q, q_inv = unit(acts[0], hdim ** -0.5)
        k, k_inv = unit(acts[1], 1.0)
        v = acts[2]
        state, grad_out, grad_end = state_ref[h], grad_rec[h], grad_end_all[h]
        solved = solved_ref[h]
        score = score_ref[h]
        weights, values = solved[:, :hdim], solved[:, hdim:]
        k_end = k * to_end
        fresh = values.astype(F32) - mm(weights, state)
        grad_fresh = mm(score, grad_out, 0, 0) + mm(k_end, grad_end)
        over_state = mm(jnp.concatenate([grad_out, grad_fresh], axis=0), state, 1, 1)
        grad_q_grow = over_state[:size]
        grad_weights = -over_state[size:]
        grad_k_end = mm(fresh, grad_end, 1, 1)
        grad_score = mm(grad_out, fresh, 1, 1)
        grad_carry = jnp.sum(
            jnp.sum(grad_end.astype(F32) * state.astype(F32), axis=1, keepdims=True), axis=0, keepdims=True
        )
        grad_right = mm(inv_ref[h], jnp.concatenate([grad_weights, grad_fresh], axis=1), 0, 0)
        grad_system = -mm(grad_right, solved, 1, 1)
        gram = gram_ref[h].astype(F32)
        by_gram = grad_system * gram
        grad_gram = jnp.where(inside, grad_system * (beta * fade), 0.0)
        grad_pair = jnp.where(fade > 0.0, grad_score * fade, 0.0)
        stacked = jnp.concatenate([grad_gram, grad_pair], axis=0)
        forward_terms = mm(stacked, k)
        back_terms = mm(stacked, jnp.concatenate([k, q], axis=0), 0, 0)
        grad_right_k, grad_right_v = grad_right[:, :hdim], grad_right[:, hdim:]
        beta_growth = beta * growth
        grad_q = forward_terms[size:] + growth * grad_q_grow
        grad_k = forward_terms[:size] + back_terms + beta_growth * grad_right_k + to_end * grad_k_end
        grad_v = beta * grad_right_v
        right_k = jnp.sum(grad_right_k * k, axis=1, keepdims=True) * growth
        right_v = jnp.sum(grad_right_v * v, axis=1, keepdims=True)
        by_rows = jnp.sum(by_gram, axis=1, keepdims=True)
        grad_strengths.append(by_rows + right_k + right_v)
        spread = beta * by_gram + jnp.where(inside, grad_score * score.astype(F32), 0.0)
        ends = jnp.sum(grad_k_end * k_end, axis=1, keepdims=True)
        grad_cum = (
            jnp.sum(spread, axis=1, keepdims=True)
            + beta * right_k
            + jnp.sum(grad_q_grow * q, axis=1, keepdims=True) * growth
            - ends
        )
        to_last = jnp.sum(ends, axis=0, keepdims=True) + grad_carry * carry
        is_last = lax.broadcasted_iota(jnp.int32, (size, 1), 0) == size - 1
        grad_cum = grad_cum + jnp.where(is_last, to_last, 0.0)
        grad_cums.append((grad_cum, jnp.sum(spread, axis=0, keepdims=True)))
        grads = (
            unit_back(acts[0], q_inv, hdim ** -0.5, grad_q),
            unit_back(acts[1], k_inv, 1.0, grad_k),
            grad_v,
        )
        for part in range(3):
            u, s = sums[part], sigs[part]
            grad_u = grads[part] * (s * (1.0 + u * (1.0 - s)))
            total = None
            taps_here = []
            for j in range(taps):
                kept = grad_u * keeps[j] if j < taps - 1 else grad_u
                shifted = ext[part, pl.ds(8 - (taps - 1) + j, size), cols]
                taps_here.append(jnp.sum(kept * shifted, axis=0, keepdims=True))
                back[j, pl.ds(0, 8), :] = jnp.zeros((8, hdim), F32)
                back[j, pl.ds(8, size), :] = kept * convw_ref[part, j : j + 1, cols]
                back[j, pl.ds(8 + size, 8), :] = jnp.zeros((8, hdim), F32)
            grad_convw_ref[part, :, cols] = jnp.concatenate(taps_here, axis=0)
            for j in range(taps):
                term = back[j, pl.ds(8 + (taps - 1) - j, size), :]
                total = term if total is None else total + term
            grad_proj_ref[part, :, cols] = total.astype(BF)
            last_rows[part, :, cols] = total[size - 16 :, :]
            edge = None
            for j in range(taps):
                term = back[j, pl.ds((taps - 1) - j, 8), :]
                edge = term if edge is None else edge + term
            edge_out[part, :, cols] = edge
    edge_copy = ring.copy(edge_out, edge_in, sems, 3, ring.place - 1)
    has_before, has_after = ring.place > 0, ring.place < ring.count - 1
    pl.when(has_before)(edge_copy.start)
    columns = jnp.concatenate(
        [g for g, _ in grad_cums] + grad_strengths + [jnp.zeros((size, 128 - 2 * heads), F32)], axis=1
    )
    rows = columns.T
    cum_rows = rows[0:heads] - jnp.concatenate([r for _, r in grad_cums], axis=0)
    padded = jnp.concatenate([cum_rows, jnp.zeros((8 - heads, size), F32)], axis=0)
    grad_logs = mm_exact(padded, tri(size, False))[0:heads]
    strength = sigmoid(gates_ref[0:heads, :])
    grad_gates_ref[0:heads, :] = rows[heads : 2 * heads] * strength * (1.0 - strength)
    by_rate = jnp.sum(grad_logs * scan.log_rows, axis=1, keepdims=True)
    slopes = []
    for h in range(heads):
        rate = jnp.exp(jnp.full((1, size), decay_ref[0, h], F32))
        slopes.append(-rate * sigmoid(gates_ref[heads + h : heads + h + 1, :] + decay_ref[1, h]))
    grad_bias = grad_logs * jnp.concatenate(slopes, axis=0)
    grad_gates_ref[heads : 2 * heads, :] = grad_bias
    by_bias = jnp.sum(grad_bias, axis=1, keepdims=True)
    grad_decay_ref[...] = jnp.concatenate(
        [by_rate, by_bias, jnp.zeros((heads, 126), F32)], axis=1
    )

    @pl.when(jnp.logical_not(has_after))
    def _():
        edge_in[...] = jnp.zeros_like(edge_in)

    pl.when(has_after)(edge_copy.wait_recv)
    for part in range(3):
        rows = jnp.concatenate(
            [last_rows[part, 0:8, :], last_rows[part, 8:16, :] + edge_in[part]], axis=0
        )
        grad_proj_ref[part, pl.ds(size - 16, 16), :] = rows.astype(BF)
    local_copy.wait_send()
    pl.when(to_before)(chain_copy.wait_send)
    state_copy.wait_send()
    pl.when(has_before)(edge_copy.wait_send)


def recurrent_backward(first, decay, gates, proj, rim, convw, gain, grad_gated, saved):
    heads = decay.shape[1]
    parts, size, width = proj.shape
    hdim = width // heads
    mine = heads // 2
    taps = convw.shape[1]
    shape = jax.ShapeDtypeStruct
    vm = pl.BlockSpec(memory_space=pltpu.VMEM)
    sm = pl.BlockSpec(memory_space=pltpu.SMEM)
    states = lambda count: pltpu.VMEM((count, hdim, hdim), BF)
    return pl.pallas_call(
        functools.partial(backward_kernel, heads),
        out_shape=(
            shape((4, size, width), BF), shape((3, taps, width), F32),
            shape((2 * heads, size), F32), shape((heads, 128), F32), shape((heads, hdim), F32),
        ),
        in_specs=[sm, sm] + [vm] * 14,
        out_specs=(vm,) * 5,
        scratch_shapes=[
            pltpu.VMEM((3, size + 8, width), F32), pltpu.VMEM((taps, size + 16, hdim), F32),
            pltpu.VMEM((heads, size, hdim), F32), states(heads), states(mine), states(mine), states(mine),
            states(mine), states(mine), states(heads),
            pltpu.VMEM((3, 8, width), F32), pltpu.VMEM((3, 8, width), F32), pltpu.VMEM((3, 16, width), F32),
            pltpu.SemaphoreType.DMA((4,)), pltpu.SemaphoreType.DMA((4,)),
        ],
        compiler_params=pltpu.CompilerParams(
            vmem_limit_bytes=56 << 20, collective_id=2, has_side_effects=True
        ),
        name="recurrent_backward",
    )(first, decay, gates, proj, rim, convw, gain, grad_gated, *saved)


def rms_scale(values, gain):
    return values * lax.rsqrt(jnp.mean(values * values, axis=-1, keepdims=True) + EPS) * gain


def swiglu(gate_up):
    return jax.nn.silu(gate_up[:, 0]) * gate_up[:, 1]


def dot(left, right, dims):
    return lax.dot_general(left, right, (dims, ((), ())), preferred_element_type=F32)


def over_head(array):
    return lax.psum(array.astype(BF), "head").astype(F32)


def across(array, axis, mask):
    return lax.ppermute(array, axis, [(i, i ^ mask) for i in range(lax.axis_size(axis))])


def mirrored(array):
    return across(array, "seq", lax.axis_size("seq") - 2)


def mirrored_shared(array):
    half = array.shape[0] // 2
    odd = lax.axis_index("head") % 2
    mine = mirrored(lax.dynamic_slice_in_dim(array, odd * half, half, 0))
    other = across(mine, "head", 1)
    first = jnp.where(odd == 0, mine, other)
    second = jnp.where(odd == 0, other, mine)
    return jnp.concatenate([first, second], axis=0)


def own_half_columns(array, of):
    width = array.shape[1] // 2
    return lax.dynamic_slice_in_dim(array, of * width, width, 1)


def sum_in_half(partials):
    count = len(partials)
    bits = []
    bit = 1
    while bit < count:
        bits.append(bit)
        bit *= 2
    done = []
    for part, order in ((0, bits), (1, bits[::-1])):
        held = {}
        for m in range(count):
            rows = partials[m].shape[0] // 2
            held[m] = partials[m][part * rows : (part + 1) * rows]
        for bit in order:
            sent = sorted(m for m in held if m & bit)
            block = jnp.concatenate([held[m].astype(jnp.bfloat16) for m in sent], axis=0)
            got = across(block, "seq", bit).astype(jnp.float32)
            rows = got.shape[0] // len(sent)
            held = {
                m: held[m] + got[k * rows : (k + 1) * rows]
                for k, m in enumerate(sorted(m for m in held if not m & bit))
            }
        done.append(held[0])
    return jnp.concatenate(done, axis=0)


def shards(
    inputs,
    gains,
    w_proj,
    w_gates,
    decay,
    conv_w,
    head_gain,
    w_out,
    w_up,
    w_down,
    seq_first,
    cotangent,
):
    tokens = inputs.shape[0]
    heads_here = decay.shape[1]
    owners = lax.axis_size("seq")
    place = lax.axis_index("seq")
    half = place // (owners // 2)
    masks = range(owners // 2)
    kept = inputs.shape[1] // owners

    def owned(array, mask):
        return lax.dynamic_slice_in_dim(array, (place ^ mask) * kept, kept, 1)

    def owned_half(array, mask):
        within = (place ^ mask) % (owners // 2)
        return lax.dynamic_slice_in_dim(array, within * kept, kept, 1)

    normed_in, norm_in_back = jax.vjp(rms_scale, inputs, gains[0])
    normed_low = normed_in.astype(BF)
    projected = jnp.einsum("td,dkc->ktc", normed_low, w_proj, preferred_element_type=F32)
    gate_in = jnp.einsum("td,idh->iht", normed_low, w_gates, preferred_element_type=F32)
    gate_in = gate_in.reshape(2 * heads_here, tokens)
    gated_low, recurrent, lift, inverse, solved, gram, score, state, pair, rim = recurrent_forward(
        seq_first, decay, gate_in, projected, conv_w, head_gain
    )
    attn_part = jnp.dot(gated_low, w_out, preferred_element_type=jnp.float32)
    middle = inputs + lax.psum(attn_part.astype(jnp.bfloat16), "head").astype(jnp.float32)
    normed_mid, norm_mid_back = jax.vjp(rms_scale, middle, gains[1])
    normed_mid_low = normed_mid.astype(jnp.bfloat16)
    gate_up = jnp.einsum("td,dkf->tkf", normed_mid_low, w_up, preferred_element_type=jnp.float32)
    hidden, hidden_back = jax.vjp(swiglu, gate_up)
    hidden_low = hidden.astype(jnp.bfloat16)
    mlp_part = jnp.dot(hidden_low, w_down, preferred_element_type=jnp.float32)
    output = middle + lax.psum(mlp_part.astype(jnp.bfloat16), "head").astype(jnp.float32)
    grad_low = cotangent.astype(jnp.bfloat16)
    grad_hidden = jnp.einsum("td,fd->tf", grad_low, w_down, preferred_element_type=jnp.float32)
    (grad_gate_up,) = hidden_back(grad_hidden)
    grad_gate_up_low = grad_gate_up.astype(jnp.bfloat16)
    normed_mid_far = mirrored_shared(normed_mid_low)
    grad_low_far = mirrored_shared(grad_low)
    gate_up_far = jnp.einsum(
        "td,dkf->tkf", normed_mid_far, w_up, preferred_element_type=jnp.float32
    )
    grad_hidden_far = jnp.einsum(
        "td,fd->tf", grad_low_far, w_down, preferred_element_type=jnp.float32
    )
    hidden_far, hidden_far_back = jax.vjp(swiglu, gate_up_far)
    (grad_gate_up_far,) = hidden_far_back(grad_hidden_far)
    both = lambda near, far: jnp.concatenate([near, far.astype(near.dtype)], axis=0)
    hidden_both = both(hidden_low, hidden_far)
    grad_gate_up_both = both(grad_gate_up_low, grad_gate_up_far)
    normed_mid_both = both(normed_mid_low, normed_mid_far)
    grad_low_both = both(grad_low, grad_low_far)
    up_parts = [
        jnp.einsum(
            "td,tkf->dkf", owned(normed_mid_both, m), grad_gate_up_both, preferred_element_type=jnp.float32
        ).astype(jnp.bfloat16)
        for m in masks
    ]
    down_parts = [
        jnp.einsum(
            "tf,td->fd", hidden_both, owned(grad_low_both, m), preferred_element_type=jnp.float32
        ).astype(jnp.bfloat16)
        for m in masks
    ]
    grad_normed_mid = lax.psum(
        jnp.einsum(
            "tkf,dkf->td", grad_gate_up_low, w_up, preferred_element_type=jnp.float32
        ).astype(jnp.bfloat16),
        "head",
    ).astype(jnp.float32)
    grad_middle_norm, grad_gain_mid = norm_mid_back(grad_normed_mid)
    grad_middle = cotangent + grad_middle_norm
    grad_attn_low = grad_middle.astype(jnp.bfloat16)
    gated_both = both(gated_low, mirrored(gated_low))
    grad_attn_far = mirrored_shared(own_half_columns(grad_attn_low, 1 - half))
    grad_attn_both = both(own_half_columns(grad_attn_low, half), grad_attn_far)
    wout_parts = [
        jnp.einsum(
            "tc,td->cd", gated_both, owned_half(grad_attn_both, m), preferred_element_type=jnp.float32
        ).astype(jnp.bfloat16)
        for m in masks
    ]
    grad_gated = jnp.einsum("td,cd->tc", grad_attn_low, w_out, preferred_element_type=jnp.float32)
    grad_projected, grad_conv, grad_gate_in, grad_decay, grad_head_gain = recurrent_backward(
        seq_first, decay, gate_in, projected, rim, conv_w, head_gain, grad_gated,
        (recurrent, lift, inverse, solved, gram, score, state, pair),
    )
    grad_decay = grad_decay[:, :2].T
    grad_gate_low = grad_gate_in.reshape(2, heads_here, tokens).astype(BF)
    normed_far = mirrored_shared(own_half_columns(normed_low, 1 - half))
    normed_both = both(own_half_columns(normed_low, half), normed_far)
    grad_projected_both = jnp.concatenate([grad_projected, mirrored(grad_projected)], axis=1)
    proj_parts = [
        jnp.einsum(
            "td,ktc->dkc", owned_half(normed_both, m), grad_projected_both, preferred_element_type=jnp.float32
        ).astype(jnp.bfloat16)
        for m in masks
    ]
    grad_wgates = jnp.einsum(
        "td,iht->idh", normed_low, grad_gate_low, preferred_element_type=jnp.float32
    )
    grad_normed_part = jnp.einsum(
        "ktc,dkc->td", grad_projected, w_proj, preferred_element_type=jnp.float32
    )
    grad_normed_part = grad_normed_part + jnp.einsum(
        "iht,idh->td", grad_gate_low, w_gates, preferred_element_type=jnp.float32
    )
    grad_normed_in = lax.psum(grad_normed_part.astype(jnp.bfloat16), "head").astype(jnp.float32)
    grad_in_norm, grad_gain_in = norm_in_back(grad_normed_in)
    grad_inputs = grad_middle + grad_in_norm
    summed = (
        lax.psum(grad_conv.astype(jnp.bfloat16), "seq").astype(jnp.float32),
        lax.psum(grad_wgates.astype(jnp.bfloat16), "seq").astype(jnp.float32),
        lax.psum(grad_decay.astype(jnp.bfloat16), "seq").astype(jnp.float32),
        lax.psum(grad_head_gain.astype(jnp.bfloat16), "seq").astype(jnp.float32),
        lax.psum(jnp.stack([grad_gain_in, grad_gain_mid]).astype(jnp.bfloat16), "seq").astype(
            jnp.float32
        ),
    )
    grad_proj_part = sum_in_half(proj_parts)
    grad_up_part = sum_in_half(up_parts)
    grad_wout_part = sum_in_half(wout_parts)
    grad_down_part = sum_in_half(down_parts)
    return (
        output,
        grad_inputs,
        summed[4],
        grad_proj_part,
        summed[1],
        summed[2],
        summed[0],
        summed[3],
        grad_wout_part,
        grad_up_part,
        grad_down_part,
    )


def solution(mesh):
    placed = (
        P("seq", None),
        P(),
        P(None, None, "head"),
        P(None, None, "head"),
        P(None, "head"),
        P(None, None, "head"),
        P("head", None),
        P("head", None),
        P(None, None, "head"),
        P("head", None),
        P("seq"),
        P("seq", None),
    )
    return jax.shard_map(
        shards,
        mesh=mesh,
        in_specs=placed,
        out_specs=(
            P("seq", None),
            P("seq", None),
            P(),
            P("seq", None, "head"),
            P(None, None, "head"),
            P(None, "head"),
            P(None, None, "head"),
            P("head", None),
            P("head", "seq"),
            P("seq", None, "head"),
            P("head", "seq"),
        ),
        check_vma=False,
    )
```

```python
import functools

import jax
import jax.numpy as jnp
from jax import lax
from jax.experimental import pallas as pl
from jax.experimental.pallas import tpu as pltpu
from jax.sharding import PartitionSpec as P

EPS = 1e-06
GROUP = 64
BF = jnp.bfloat16
F32 = jnp.float32


def mm(a, b, ca=1, cb=0):
    return lax.dot_general(
        a.astype(BF), b.astype(BF), (((ca,), (cb,)), ((), ())), preferred_element_type=F32
    )


def split(a):
    high = a.astype(BF)
    return high, (a - high.astype(F32)).astype(BF)


def mm3(a, b, ca=1, cb=0):
    ah, al = split(a)
    bh, bl = split(b)
    return mm(ah, bh, ca, cb) + (mm(ah, bl, ca, cb) + mm(al, bh, ca, cb))


def mm_exact(a, b):
    return lax.dot_general(
        a, b, (((1,), (0,)), ((), ())), preferred_element_type=F32, precision=lax.Precision.HIGHEST
    )


def sigmoid(v):
    return 1.0 / (1.0 + jnp.exp(-v))


def softplus(v):
    return jnp.maximum(v, 0.0) + jnp.log1p(jnp.exp(-jnp.abs(v)))


def block_sums(first_ref, shape, axis):
    block = lax.broadcasted_iota(jnp.int32, shape, axis) // GROUP
    seen = jnp.zeros(shape, F32)
    starts = jnp.zeros(shape, F32)
    for b in range(first_ref.shape[0]):
        flag = first_ref[b].astype(F32)
        seen = seen + jnp.where(block >= b, flag, 0.0)
        starts = starts + jnp.where(block == b, flag, 0.0)
    return seen, starts


def gate_rows(gates_ref, decay_ref, heads):
    rows = []
    size = gates_ref.shape[1]
    for h in range(heads):
        rate = jnp.exp(jnp.full((1, size), decay_ref[0, h], F32))
        bias = decay_ref[1, h]
        rows.append(-rate * softplus(gates_ref[heads + h : heads + h + 1, :] + bias))
    return jnp.concatenate(rows, axis=0)


def tap_keeps(starts, taps):
    size = starts.shape[0]
    offset = lax.broadcasted_iota(jnp.int32, (size, 1), 0) % GROUP
    return [1.0 - jnp.where(offset < taps - 1 - j, starts, 0.0) for j in range(taps)]


def convolved(ext_ref, part, cols, convw_ref, keeps):
    size = ext_ref.shape[1] - 8
    taps = len(keeps)
    total = None
    for j in range(taps):
        shifted = ext_ref[part, pl.ds(8 - (taps - 1) + j, size), cols]
        if j < taps - 1:
            shifted = shifted * keeps[j]
        term = shifted * convw_ref[part, j : j + 1, cols]
        total = term if total is None else total + term
    return total


def fade_of(cum_col, cum_row, seen_col, seen_row):
    size = cum_col.shape[0]
    row = lax.broadcasted_iota(jnp.int32, (size, size), 0)
    col = lax.broadcasted_iota(jnp.int32, (size, size), 1)
    inside = (row > col) & (seen_col == seen_row)
    fade = jnp.where(inside, jnp.exp(jnp.minimum(cum_col - cum_row, 0.0)), 0.0)
    return jnp.where(row == col, 1.0, fade), inside


def fill_ext(ext, proj_ref, rim_ref):
    size = proj_ref.shape[1]
    for part in range(3):
        ext[part, pl.ds(0, 8), :] = rim_ref[part]
        ext[part, pl.ds(8, size), :] = proj_ref[part].astype(BF).astype(F32)


def tri(size, upper):
    row = lax.broadcasted_iota(jnp.int32, (size, size), 0)
    col = lax.broadcasted_iota(jnp.int32, (size, size), 1)
    return jnp.where((row <= col) if upper else (row >= col), 1.0, 0.0).astype(F32)


class Scan:
    def __init__(self, first_ref, decay_ref, gates_ref, heads):
        size = gates_ref.shape[1]
        self.log_rows = gate_rows(gates_ref, decay_ref, heads)
        self.seen_row, _ = block_sums(first_ref, (1, size), 1)
        self.seen_col, self.starts = block_sums(first_ref, (size, 1), 0)
        padded = jnp.concatenate([self.log_rows, jnp.zeros((8 - heads, size), F32)], axis=0)
        self.cum_rows = mm_exact(padded, tri(size, True))
        strength_rows = sigmoid(gates_ref[0:heads, :])
        both = jnp.concatenate([self.cum_rows[0:heads], strength_rows], axis=0)
        both = jnp.concatenate([both, jnp.zeros((128 - 2 * heads, size), F32)], axis=0)
        cols = both.T
        self.cum_cols = [cols[:, h : h + 1] for h in range(heads)]
        self.strength = [cols[:, heads + h : heads + h + 1] for h in range(heads)]

    def of(self, h):
        cum_col, cum_row = self.cum_cols[h], self.cum_rows[h : h + 1, :]
        size = cum_col.shape[0]
        last = cum_col[size - 1 : size, :]
        fade, inside = fade_of(cum_col, cum_row, self.seen_col, self.seen_row)
        growth = jnp.where(self.seen_col == 0.0, jnp.exp(cum_col), 0.0)
        last_seen = self.seen_col[size - 1 : size, :]
        to_end = jnp.where(self.seen_col == last_seen, jnp.exp(jnp.minimum(last - cum_col, 0.0)), 0.0)
        carry = jnp.where(last_seen == 0.0, jnp.exp(last), 0.0)
        return fade, inside, growth, to_end, carry


def unit(a, scale):
    inverse = lax.rsqrt(jnp.sum(a * a, axis=1, keepdims=True) + EPS)
    return a * (inverse * scale), inverse


MESH = pl.DeviceIdType.MESH


class Ring:
    def __init__(self):
        self.count = lax.axis_size("seq")
        self.place = lax.axis_index("seq")
        self.head = lax.axis_index("head")
        self.side = self.place % 2
        self.pair = self.place // 2
        self.pairs = self.count // 2
        self.partner = self.place + 1 - 2 * self.side
        self.cross = self.place + 2 * self.side - 1
        self.mirror = self.count - 2 - self.place + 2 * self.side

    def device(self, place):
        return (place, self.head)

    def across(self):
        return (self.place, (self.head + 2) % lax.axis_size("head"))

    def across_copy(self, source, target, sems, index):
        return pltpu.make_async_remote_copy(
            src_ref=source, dst_ref=target, send_sem=sems[0].at[index], recv_sem=sems[1].at[index],
            device_id=self.across(), device_id_type=MESH,
        )

    def greet(self, mirror=False, across=False):
        barrier = pltpu.get_barrier_semaphore()

        def tell(place):
            pl.semaphore_signal(barrier, inc=1, device_id=self.device(place), device_id_type=MESH)

        tell(self.partner)
        if mirror:
            tell(self.mirror)
        if across:
            pl.semaphore_signal(barrier, inc=1, device_id=self.across(), device_id_type=MESH)
        for place in (self.place - 2, self.place + 2, self.cross):
            pl.when((place >= 0) & (place < self.count))(functools.partial(tell, place))

    def met(self, mirror=False, across=False):
        inside = lambda place: jnp.where((place >= 0) & (place < self.count), 1, 0)
        known = 1 + int(mirror) + int(across) + inside(self.place - 2) + inside(self.place + 2) + inside(self.cross)
        pl.semaphore_wait(pltpu.get_barrier_semaphore(), known)

    def copy(self, source, target, sems, index, place):
        return pltpu.make_async_remote_copy(
            src_ref=source, dst_ref=target, send_sem=sems[0].at[index], recv_sem=sems[1].at[index],
            device_id=self.device(place), device_id_type=MESH,
        )


def forward_kernel(
    heads, first_ref, decay_ref, gates_ref, proj_ref, convw_ref, gain_ref, spread_ref,
    gated_ref, rec_ref, lift_ref, inv_ref, solved_ref, gram_ref, score_ref, state_ref, pair_ref, rim_ref, far_ref,
    ext, base, maps, other, chain_in, chain_out, state_out, state_in, rim_out, rim_in, send_sems, recv_sems,
):
    ring = Ring()
    ring.greet(True)
    sems = (send_sems, recv_sems)
    size = proj_ref.shape[1]
    hdim = proj_ref.shape[2] // heads
    taps = convw_ref.shape[1]
    mine = heads // 2
    for part in range(3):
        rows = proj_ref[part].astype(BF).astype(F32)
        ext[part, pl.ds(8, size), :] = rows
        rim_out[part] = rows[size - 8 :, :]
    scan = Scan(first_ref, decay_ref, gates_ref, heads)
    ring.met(True)
    has_before, has_after = ring.place > 0, ring.place < ring.count - 1
    rim_copy = ring.copy(rim_out, rim_in, sems, 0, ring.place + 1)
    pl.when(has_after)(rim_copy.start)
    far_copy = ring.copy(spread_ref, far_ref, sems, 4, ring.mirror)
    far_copy.start()

    @pl.when(ring.place == 0)
    def _():
        rim_in[...] = jnp.zeros_like(rim_in)

    keeps = tap_keeps(scan.starts, taps)
    eye = lax.broadcasted_iota(jnp.int32, (size, size), 0) == lax.broadcasted_iota(
        jnp.int32, (size, size), 1
    )
    apart = lax.broadcasted_iota(jnp.int32, (size, size), 0) ^ lax.broadcasted_iota(
        jnp.int32, (size, size), 1
    )
    pl.when(has_before)(rim_copy.wait_recv)
    for part in range(3):
        ext[part, pl.ds(0, 8), :] = rim_in[part]
        rim_ref[part] = rim_in[part]
    held = []
    for h in range(heads):
        cols = pl.ds(h * hdim, hdim)
        acts = []
        for part in range(3):
            u = convolved(ext, part, cols, convw_ref, keeps)
            acts.append(u * sigmoid(u))
        q, _ = unit(acts[0], hdim ** -0.5)
        k, _ = unit(acts[1], 1.0)
        v = acts[2]
        fade, inside, growth, to_end, carry = scan.of(h)
        beta = scan.strength[h]
        gram = mm(k, k, 1, 1) * jnp.where(inside, fade, 0.0)
        score = mm(q, k, 1, 1) * fade
        gram_ref[h] = gram.astype(BF)
        score_ref[h] = score.astype(BF)
        system = beta * gram
        held.append((q, k, v, growth, to_end, carry, beta, system))
    inverses = [jnp.where(eye, 1.0, 0.0) - jnp.where(apart == 1, t[7], 0.0) for t in held]
    block = 2
    while block < size:
        level = (apart >= block) & (apart < 2 * block)
        inner = [mm(jnp.where(level, t[7], 0.0), inv) for t, inv in zip(held, inverses)]
        inverses = [inv - mm(inv, y) for inv, y in zip(inverses, inner)]
        block *= 2
    left = [jnp.where(eye, 1.0, 0.0) - inv - mm3(t[7], inv) for t, inv in zip(held, inverses)]
    inverses = [inv + mm(inv, r) for inv, r in zip(inverses, left)]
    for h in range(heads):
        q, k, v, growth, to_end, carry, beta, system = held[h]
        inv = inverses[h].astype(BF)
        inv_ref[h] = inv
        right = jnp.concatenate([beta * growth * k, beta * v], axis=1)
        solved = mm(inv, right).astype(BF)
        solved_ref[h] = solved
        ends = mm(k * to_end, solved, 0, 0)
        factor = jnp.where(eye[:hdim, :hdim], carry, 0.0) - ends[:, :hdim]
        maps[h] = jnp.concatenate([factor, ends[:, hdim:]], axis=1).astype(BF)
    map_copy = ring.copy(
        maps.at[pl.ds((1 - ring.side) * mine, mine)], other, sems, 1, ring.partner
    )
    map_copy.start()
    for h in range(heads):
        q, k, v, growth, to_end, carry, beta, system = held[h]
        mixed = mm(score_ref[h], solved_ref[h])
        lift_ref[h] = (q * growth - mixed[:, :hdim]).astype(BF)
        base[h] = mixed[:, hdim:]
    map_copy.wait_recv()
    chain_copy = ring.copy(chain_out, chain_in, sems, 2, ring.place + 2)
    from_before, to_after = ring.pair > 0, ring.pair < ring.pairs - 1
    whole, before = [], []
    for i in range(mine):
        own, far = maps[ring.side * mine + i], other[i]
        early = jnp.where(ring.side == 0, own, far)
        late = jnp.where(ring.side == 0, far, own)
        both = mm(late[:, :hdim], early)
        whole.append((both[:, :hdim].astype(BF), both[:, hdim:] + late[:, hdim:].astype(F32)))
        before.append(early)
        pair_ref[0, i] = early[:, :hdim]
        pair_ref[1, i] = late[:, :hdim]
        pair_ref[2, i] = whole[i][0]

    @pl.when(jnp.logical_not(from_before))
    def _():
        chain_in[...] = jnp.zeros_like(chain_in)

    pl.when(from_before)(chain_copy.wait_recv)
    for i in range(mine):
        chain_out[i] = (mm(whole[i][0], chain_in[i]) + whole[i][1]).astype(BF)
    pl.when(to_after)(chain_copy.start)
    for i in range(mine):
        first = chain_in[i]
        second = (mm(before[i][:, :hdim], first) + before[i][:, hdim:].astype(F32)).astype(BF)
        state_out[i] = jnp.where(ring.side == 0, second, first)
        state_ref[ring.side * mine + i] = jnp.where(ring.side == 0, first, second)
    state_copy = ring.copy(state_out, state_in, sems, 3, ring.partner)
    state_copy.start()
    state_copy.wait_recv()
    for i in range(mine):
        state_ref[(1 - ring.side) * mine + i] = state_in[i]
    for h in range(heads):
        cols = pl.ds(h * hdim, hdim)
        rec = mm(lift_ref[h], state_ref[h]) + base[h]
        rec_ref[h] = rec
        inverse = lax.rsqrt(jnp.mean(rec * rec, axis=1, keepdims=True) + EPS)
        gate = proj_ref[3, :, cols]
        gated_ref[:, cols] = (
            rec * inverse * gain_ref[h : h + 1, :] * (gate * sigmoid(gate))
        ).astype(BF)
    pl.when(has_after)(rim_copy.wait_send)
    map_copy.wait_send()
    pl.when(to_after)(chain_copy.wait_send)
    state_copy.wait_send()
    far_copy.wait()


def recurrent_forward(first, decay, gates, proj, convw, gain, spread):
    heads = decay.shape[1]
    parts, size, width = proj.shape
    hdim = width // heads
    mine = heads // 2
    shape = jax.ShapeDtypeStruct
    vm = pl.BlockSpec(memory_space=pltpu.VMEM)
    sm = pl.BlockSpec(memory_space=pltpu.SMEM)
    square = shape((heads, size, size), BF)
    states = lambda count: pltpu.VMEM((count, hdim, hdim), BF)
    return pl.pallas_call(
        functools.partial(forward_kernel, heads),
        out_shape=(
            shape((size, width), BF), shape((heads, size, hdim), F32), shape((heads, size, hdim), BF),
            square, shape((heads, size, 2 * hdim), BF), square, square,
            shape((heads, hdim, hdim), BF), shape((3, mine, hdim, hdim), BF), shape((3, 8, width), F32),
            shape(spread.shape, BF),
        ),
        in_specs=[sm, sm, vm, vm, vm, vm, vm],
        out_specs=(vm,) * 11,
        scratch_shapes=[
            pltpu.VMEM((3, size + 8, width), F32), pltpu.VMEM((heads, size, hdim), F32),
            pltpu.VMEM((heads, hdim, 2 * hdim), BF), pltpu.VMEM((mine, hdim, 2 * hdim), BF),
            states(mine), states(mine), states(mine), states(mine),
            pltpu.VMEM((3, 8, width), F32), pltpu.VMEM((3, 8, width), F32),
            pltpu.SemaphoreType.DMA((5,)), pltpu.SemaphoreType.DMA((5,)),
        ],
        compiler_params=pltpu.CompilerParams(
            vmem_limit_bytes=56 << 20, collective_id=1, has_side_effects=True
        ),
        name="recurrent_forward",
    )(first, decay, gates, proj, convw, gain, spread)


def unit_back(a, inverse, scale, grad):
    along = jnp.sum(a * grad, axis=1, keepdims=True)
    return scale * (inverse * grad - a * (inverse * inverse * inverse * along))


def backward_kernel(
    heads, first_ref, decay_ref, gates_ref, proj_ref, rim_ref, convw_ref,
    gain_ref, grad_gated_ref, rec_ref, lift_ref, inv_ref, solved_ref, gram_ref, score_ref, state_ref, pair_ref, grad_held_ref,
    grad_proj_ref, grad_convw_ref, grad_gates_ref, grad_decay_ref, grad_gain_ref, grad_second_ref,
    ext, back, grad_rec, local, other, chain_in, chain_out, state_out, state_in, grad_end_all,
    edge_out, edge_in, last_rows, send_sems, recv_sems,
):
    ring = Ring()
    ring.greet(across=True)
    sems = (send_sems, recv_sems)
    mine = heads // 2
    size = proj_ref.shape[1]
    hdim = proj_ref.shape[2] // heads
    taps = convw_ref.shape[1]
    for h in range(heads):
        cols = pl.ds(h * hdim, hdim)
        rec = rec_ref[h]
        inverse = lax.rsqrt(jnp.mean(rec * rec, axis=1, keepdims=True) + EPS)
        gate = proj_ref[3, :, cols]
        sig = sigmoid(gate)
        gain = gain_ref[h : h + 1, :]
        normed = rec * inverse
        grad_gated = grad_gated_ref[:, cols]
        by_normed = grad_gated * normed
        grad_proj_ref[3, :, cols] = (
            by_normed * gain * (sig * (1.0 + gate * (1.0 - sig)))
        ).astype(BF)
        active = gate * sig
        grad_gain_ref[h : h + 1, :] = jnp.sum(by_normed * active, axis=0, keepdims=True)
        grad_normed = grad_gated * (active * gain)
        along = jnp.mean(rec * grad_normed, axis=1, keepdims=True)
        grad_rec[h] = inverse * grad_normed - rec * (inverse * inverse * inverse * along)
        local[h] = mm(lift_ref[h], grad_rec[h], 0, 0).astype(BF)
    ring.met(across=True)
    second_side = ring.across_copy(grad_held_ref.at[1], grad_second_ref, sems, 4)
    second_side.start()
    local_copy = ring.copy(
        local.at[pl.ds((1 - ring.side) * mine, mine)], other, sems, 0, ring.partner
    )
    local_copy.start()
    fill_ext(ext, proj_ref, rim_ref)
    scan = Scan(first_ref, decay_ref, gates_ref, heads)
    keeps = tap_keeps(scan.starts, taps)
    local_copy.wait_recv()
    chain_copy = ring.copy(chain_out, chain_in, sems, 1, ring.place - 2)
    from_after, to_before = ring.pair < ring.pairs - 1, ring.pair > 0

    @pl.when(jnp.logical_not(from_after))
    def _():
        chain_in[...] = jnp.zeros_like(chain_in)

    pl.when(from_after)(chain_copy.wait_recv)
    lates = []
    for i in range(mine):
        own, far = local[ring.side * mine + i], other[i]
        early = jnp.where(ring.side == 0, own, far)
        late = jnp.where(ring.side == 0, far, own)
        lates.append(late.astype(F32))
        both = early.astype(F32) + mm(pair_ref[0, i], late, 0, 0)
        chain_out[i] = (mm(pair_ref[2, i], chain_in[i], 0, 0) + both).astype(BF)
    pl.when(to_before)(chain_copy.start)
    for i in range(mine):
        last = chain_in[i]
        mid = (mm(pair_ref[1, i], last, 0, 0) + lates[i]).astype(BF)
        state_out[i] = jnp.where(ring.side == 0, last, mid)
        grad_end_all[ring.side * mine + i] = jnp.where(ring.side == 0, mid, last)
    state_copy = ring.copy(state_out, state_in, sems, 2, ring.partner)
    state_copy.start()
    state_copy.wait_recv()
    for i in range(mine):
        grad_end_all[(1 - ring.side) * mine + i] = state_in[i]
    grad_cums = []
    grad_strengths = []
    for h in range(heads):
        cols = pl.ds(h * hdim, hdim)
        fade, inside, growth, to_end, carry = scan.of(h)
        beta = scan.strength[h]
        sums, sigs, acts = [], [], []
        for part in range(3):
            u = convolved(ext, part, cols, convw_ref, keeps)
            s = sigmoid(u)
            sums.append(u)
            sigs.append(s)
            acts.append(u * s)
        q, q_inv = unit(acts[0], hdim ** -0.5)
        k, k_inv = unit(acts[1], 1.0)
        v = acts[2]
        state, grad_out, grad_end = state_ref[h], grad_rec[h], grad_end_all[h]
        solved = solved_ref[h]
        score = score_ref[h]
        weights, values = solved[:, :hdim], solved[:, hdim:]
        k_end = k * to_end
        fresh = values.astype(F32) - mm(weights, state)
        grad_fresh = mm(score, grad_out, 0, 0) + mm(k_end, grad_end)
        over_state = mm(jnp.concatenate([grad_out, grad_fresh], axis=0), state, 1, 1)
        grad_q_grow = over_state[:size]
        grad_weights = -over_state[size:]
        grad_k_end = mm(fresh, grad_end, 1, 1)
        grad_score = mm(grad_out, fresh, 1, 1)
        grad_carry = jnp.sum(
            jnp.sum(grad_end.astype(F32) * state.astype(F32), axis=1, keepdims=True), axis=0, keepdims=True
        )
        grad_right = mm(inv_ref[h], jnp.concatenate([grad_weights, grad_fresh], axis=1), 0, 0)
        grad_system = -mm(grad_right, solved, 1, 1)
        gram = gram_ref[h].astype(F32)
        by_gram = grad_system * gram
        grad_gram = jnp.where(inside, grad_system * (beta * fade), 0.0)
        grad_pair = jnp.where(fade > 0.0, grad_score * fade, 0.0)
        stacked = jnp.concatenate([grad_gram, grad_pair], axis=0)
        forward_terms = mm(stacked, k)
        back_terms = mm(stacked, jnp.concatenate([k, q], axis=0), 0, 0)
        grad_right_k, grad_right_v = grad_right[:, :hdim], grad_right[:, hdim:]
        beta_growth = beta * growth
        grad_q = forward_terms[size:] + growth * grad_q_grow
        grad_k = forward_terms[:size] + back_terms + beta_growth * grad_right_k + to_end * grad_k_end
        grad_v = beta * grad_right_v
        right_k = jnp.sum(grad_right_k * k, axis=1, keepdims=True) * growth
        right_v = jnp.sum(grad_right_v * v, axis=1, keepdims=True)
        by_rows = jnp.sum(by_gram, axis=1, keepdims=True)
        grad_strengths.append(by_rows + right_k + right_v)
        spread = beta * by_gram + jnp.where(inside, grad_score * score.astype(F32), 0.0)
        ends = jnp.sum(grad_k_end * k_end, axis=1, keepdims=True)
        grad_cum = (
            jnp.sum(spread, axis=1, keepdims=True)
            + beta * right_k
            + jnp.sum(grad_q_grow * q, axis=1, keepdims=True) * growth
            - ends
        )
        to_last = jnp.sum(ends, axis=0, keepdims=True) + grad_carry * carry
        is_last = lax.broadcasted_iota(jnp.int32, (size, 1), 0) == size - 1
        grad_cum = grad_cum + jnp.where(is_last, to_last, 0.0)
        grad_cums.append((grad_cum, jnp.sum(spread, axis=0, keepdims=True)))
        grads = (
            unit_back(acts[0], q_inv, hdim ** -0.5, grad_q),
            unit_back(acts[1], k_inv, 1.0, grad_k),
            grad_v,
        )
        for part in range(3):
            u, s = sums[part], sigs[part]
            grad_u = grads[part] * (s * (1.0 + u * (1.0 - s)))
            total = None
            taps_here = []
            for j in range(taps):
                kept = grad_u * keeps[j] if j < taps - 1 else grad_u
                shifted = ext[part, pl.ds(8 - (taps - 1) + j, size), cols]
                taps_here.append(jnp.sum(kept * shifted, axis=0, keepdims=True))
                back[j, pl.ds(0, 8), :] = jnp.zeros((8, hdim), F32)
                back[j, pl.ds(8, size), :] = kept * convw_ref[part, j : j + 1, cols]
                back[j, pl.ds(8 + size, 8), :] = jnp.zeros((8, hdim), F32)
            grad_convw_ref[part, :, cols] = jnp.concatenate(taps_here, axis=0)
            for j in range(taps):
                term = back[j, pl.ds(8 + (taps - 1) - j, size), :]
                total = term if total is None else total + term
            grad_proj_ref[part, :, cols] = total.astype(BF)
            last_rows[part, :, cols] = total[size - 16 :, :]
            edge = None
            for j in range(taps):
                term = back[j, pl.ds((taps - 1) - j, 8), :]
                edge = term if edge is None else edge + term
            edge_out[part, :, cols] = edge
    edge_copy = ring.copy(edge_out, edge_in, sems, 3, ring.place - 1)
    has_before, has_after = ring.place > 0, ring.place < ring.count - 1
    pl.when(has_before)(edge_copy.start)
    columns = jnp.concatenate(
        [g for g, _ in grad_cums] + grad_strengths + [jnp.zeros((size, 128 - 2 * heads), F32)], axis=1
    )
    rows = columns.T
    cum_rows = rows[0:heads] - jnp.concatenate([r for _, r in grad_cums], axis=0)
    padded = jnp.concatenate([cum_rows, jnp.zeros((8 - heads, size), F32)], axis=0)
    grad_logs = mm_exact(padded, tri(size, False))[0:heads]
    strength = sigmoid(gates_ref[0:heads, :])
    grad_gates_ref[0:heads, :] = rows[heads : 2 * heads] * strength * (1.0 - strength)
    by_rate = jnp.sum(grad_logs * scan.log_rows, axis=1, keepdims=True)
    slopes = []
    for h in range(heads):
        rate = jnp.exp(jnp.full((1, size), decay_ref[0, h], F32))
        slopes.append(-rate * sigmoid(gates_ref[heads + h : heads + h + 1, :] + decay_ref[1, h]))
    grad_bias = grad_logs * jnp.concatenate(slopes, axis=0)
    grad_gates_ref[heads : 2 * heads, :] = grad_bias
    by_bias = jnp.sum(grad_bias, axis=1, keepdims=True)
    grad_decay_ref[...] = jnp.concatenate(
        [by_rate, by_bias, jnp.zeros((heads, 126), F32)], axis=1
    )

    @pl.when(jnp.logical_not(has_after))
    def _():
        edge_in[...] = jnp.zeros_like(edge_in)

    pl.when(has_after)(edge_copy.wait_recv)
    for part in range(3):
        rows = jnp.concatenate(
            [last_rows[part, 0:8, :], last_rows[part, 8:16, :] + edge_in[part]], axis=0
        )
        grad_proj_ref[part, pl.ds(size - 16, 16), :] = rows.astype(BF)
    local_copy.wait_send()
    pl.when(to_before)(chain_copy.wait_send)
    state_copy.wait_send()
    pl.when(has_before)(edge_copy.wait_send)
    second_side.wait()


def recurrent_backward(first, decay, gates, proj, rim, convw, gain, grad_gated, saved, grad_held):
    heads = decay.shape[1]
    parts, size, width = proj.shape
    hdim = width // heads
    mine = heads // 2
    taps = convw.shape[1]
    shape = jax.ShapeDtypeStruct
    vm = pl.BlockSpec(memory_space=pltpu.VMEM)
    sm = pl.BlockSpec(memory_space=pltpu.SMEM)
    states = lambda count: pltpu.VMEM((count, hdim, hdim), BF)
    return pl.pallas_call(
        functools.partial(backward_kernel, heads),
        out_shape=(
            shape((4, size, width), BF), shape((3, taps, width), F32),
            shape((2 * heads, size), F32), shape((heads, 128), F32), shape((heads, hdim), F32),
            shape(grad_held.shape[1:], BF),
        ),
        in_specs=[sm, sm] + [vm] * 14 + [pl.BlockSpec(memory_space=pl.ANY)],
        out_specs=(vm,) * 5 + (pl.BlockSpec(memory_space=pl.ANY),),
        scratch_shapes=[
            pltpu.VMEM((3, size + 8, width), F32), pltpu.VMEM((taps, size + 16, hdim), F32),
            pltpu.VMEM((heads, size, hdim), F32), states(heads), states(mine), states(mine), states(mine),
            states(mine), states(mine), states(heads),
            pltpu.VMEM((3, 8, width), F32), pltpu.VMEM((3, 8, width), F32), pltpu.VMEM((3, 16, width), F32),
            pltpu.SemaphoreType.DMA((5,)), pltpu.SemaphoreType.DMA((5,)),
        ],
        compiler_params=pltpu.CompilerParams(
            vmem_limit_bytes=56 << 20, collective_id=2, has_side_effects=True
        ),
        name="recurrent_backward",
    )(first, decay, gates, proj, rim, convw, gain, grad_gated, *saved, grad_held)


class Cube:
    def __init__(self):
        self.count = lax.axis_size("seq")
        self.place = lax.axis_index("seq")
        self.head = lax.axis_index("head")
        self.bits = []
        bit = 1
        while bit < self.count // 2:
            self.bits.append(bit)
            bit *= 2
        self.masks = range(self.count // 2)

    def moved(self, mask, of=None):
        place = self.place if of is None else of
        bit = 1
        while bit <= mask:
            if mask & bit:
                place = place + bit - 2 * bit * ((place // bit) % 2)
            bit *= 2
        return place

    def along(self, mask):
        return (self.moved(mask), self.head)

    def mirror(self):
        return self.along(self.count - 2)

    def beside(self, bit):
        return (self.place, self.moved(bit, self.head))

    def greet(self, devices):
        barrier = pltpu.get_barrier_semaphore()
        for device in devices:
            pl.semaphore_signal(barrier, inc=1, device_id=device, device_id_type=MESH)

    def met(self, count):
        pl.semaphore_wait(pltpu.get_barrier_semaphore(), count)


class Copies:
    def __init__(self, send_sems, recv_sems):
        self.sems = (send_sems, recv_sems)
        self.made = []

    def start(self, source, target, device):
        index = len(self.made)
        copy = pltpu.make_async_remote_copy(
            src_ref=source, dst_ref=target, send_sem=self.sems[0].at[index],
            recv_sem=self.sems[1].at[index], device_id=device, device_id_type=MESH,
        )
        copy.start()
        self.made.append(copy)
        return copy

    def finish(self):
        for copy in self.made:
            copy.wait_send()


LANES = 128


class Spread:
    def __init__(self, cube, copies, held):
        self.cube, self.copies, self.held = cube, copies, held
        self.ways = (
            [cube.mirror()] + [cube.along(bit) for bit in cube.bits],
            [cube.mirror()] + [cube.along(bit) for bit in cube.bits[::-1]],
        )
        self.flights = []

    def send(self, step):
        count = 1 << step
        self.flights = [
            self.copies.start(
                self.held.at[side, pl.ds(0, count)], self.held.at[side, pl.ds(count, count)],
                self.ways[side][step],
            )
            for side in (0, 1)
        ]

    def take(self):
        for copy in self.flights:
            copy.wait_recv()


class HeadSum:
    def __init__(self, cube, copies, part, sibling, kept, across_in, total, chunks):
        self.cube, self.copies, self.chunks = cube, copies, chunks
        self.part, self.sibling, self.kept, self.across_in, self.total = (
            part, sibling, kept, across_in, total,
        )
        size, width = part.shape
        self.span, self.width = size // 2, width // chunks
        low = cube.head % 2
        self.own = pl.ds(pl.multiple_of(low * self.span, self.span), self.span)
        self.other = pl.ds(pl.multiple_of((1 - low) * self.span, self.span), self.span)
        self.flights = {}

    def cols(self, c):
        return pl.ds(c * self.width, self.width)

    def halve(self, c):
        cols = self.cols(c)
        self.flights[c] = self.copies.start(
            self.part.at[self.other, cols], self.sibling.at[:, cols], self.cube.beside(1)
        )

    def cross(self, c):
        cols = self.cols(c)
        self.flights[c].wait_recv()
        self.kept[:, cols] = (
            self.part[self.own, cols].astype(F32) + self.sibling[:, cols].astype(F32)
        ).astype(BF)
        self.flights[c] = self.copies.start(
            self.kept.at[:, cols], self.across_in.at[:, cols], self.cube.beside(2)
        )

    def share(self, c):
        cols = self.cols(c)
        self.flights[c].wait_recv()
        self.total[self.own, cols] = (
            self.kept[:, cols].astype(F32) + self.across_in[:, cols].astype(F32)
        ).astype(BF)
        rows = self.total.at[self.own, cols]
        self.flights[c] = self.copies.start(rows, rows, self.cube.beside(1))

    def arrive(self, c):
        self.flights[c].wait_recv()

    @staticmethod
    def scratch(size, width):
        half = pltpu.VMEM((size // 2, width), BF)
        return [half, half, half, pltpu.VMEM((size, width), BF)]


CHUNKS = 4


def middle_kernel(
    gated_ref, w_out_ref, inputs_ref, gains_ref, own_ref, far_ref, middle_ref, normed_ref, held_ref,
    part, sibling, kept, across_in, total, send_sems, recv_sems,
):
    cube = Cube()
    copies = Copies(send_sems, recv_sems)
    cube.greet([cube.beside(1), cube.beside(2)] + [cube.along(bit) for bit in cube.bits])
    for side in (0, 1):
        held_ref[side, 0] = own_ref[side]
        held_ref[side, 1] = far_ref[side]
    spread = Spread(cube, copies, held_ref)
    sums = HeadSum(cube, copies, part, sibling, kept, across_in, total, CHUNKS)
    for c in range(CHUNKS):
        part[:, sums.cols(c)] = mm(gated_ref[...], w_out_ref[:, sums.cols(c)]).astype(BF)
        if c == 0:
            cube.met(2 + len(cube.bits))
        sums.halve(c)
    spread.send(1)
    for c in range(CHUNKS):
        sums.cross(c)
    spread.take()
    spread.send(2)
    for c in range(CHUNKS):
        sums.share(c)
    for c in range(CHUNKS):
        sums.arrive(c)
    gain = gains_ref[1:2, :]
    for r in range(0, inputs_ref.shape[0], 32):
        rows = pl.ds(r, 32)
        middle = inputs_ref[rows, :] + total[rows, :].astype(F32)
        middle_ref[rows, :] = middle
        inverse = lax.rsqrt(jnp.mean(middle * middle, axis=1, keepdims=True) + EPS)
        normed_ref[rows, :] = (middle * inverse * gain).astype(BF)
    spread.take()
    for step in range(3, len(cube.bits) + 1):
        spread.send(step)
        spread.take()
    copies.finish()


def middle_of(gated, w_out, inputs, gains, own, far):
    size, features = inputs.shape
    owners = lax.axis_size("seq")
    count = 3 * CHUNKS + 2 * (owners.bit_length() - 2)
    shape = jax.ShapeDtypeStruct
    vm = pl.BlockSpec(memory_space=pltpu.VMEM)
    return pl.pallas_call(
        middle_kernel,
        out_shape=(
            shape((size, features), F32), shape((size, features), BF),
            shape((2, owners) + own.shape[1:], BF),
        ),
        in_specs=[vm] * 6,
        out_specs=(vm,) * 3,
        scratch_shapes=[pltpu.VMEM((size, features), BF)] + HeadSum.scratch(size, features) + [
            pltpu.SemaphoreType.DMA((count,)), pltpu.SemaphoreType.DMA((count,)),
        ],
        compiler_params=pltpu.CompilerParams(
            vmem_limit_bytes=40 << 20, collective_id=4, has_side_effects=True
        ),
        name="middle",
    )(gated, w_out, inputs, gains, own, far)


def middle_back_kernel(
    part_ref, middle_ref, cotangent_ref, gains_ref, w_out_ref, part_held_ref,
    grad_middle_ref, grad_low_ref, grad_gated_ref, grad_gain_ref, held_ref,
    sibling, kept, across_in, total, send_sems, recv_sems,
):
    cube = Cube()
    copies = Copies(send_sems, recv_sems)
    cube.greet([cube.beside(1), cube.beside(2)] + [cube.along(bit) for bit in cube.bits])
    held_ref[:, pl.ds(0, 4)] = part_held_ref[...]
    spread = Spread(cube, copies, held_ref)
    sums = HeadSum(cube, copies, part_ref, sibling, kept, across_in, total, CHUNKS)
    cube.met(2 + len(cube.bits))
    for c in range(CHUNKS):
        sums.halve(c)
    spread.send(2)
    for c in range(CHUNKS):
        sums.cross(c)
    for c in range(CHUNKS):
        sums.share(c)
    for c in range(CHUNKS):
        sums.arrive(c)
    grad_gain_ref[...] = norm_back(
        middle_ref, total, gains_ref[1:2, :], cotangent_ref, grad_middle_ref, grad_low_ref
    )
    grad_gated_ref[...] = mm(grad_low_ref[...], w_out_ref[...], 1, 1)
    spread.take()
    for step in range(3, len(cube.bits) + 1):
        spread.send(step)
        spread.take()
    copies.finish()


def norm_back(values_ref, grad_ref, gain, added_ref, out_ref, low_ref):
    gain_sum = None
    for r in range(0, values_ref.shape[0], 32):
        rows = pl.ds(r, 32)
        values = values_ref[rows, :]
        inverse = lax.rsqrt(jnp.mean(values * values, axis=1, keepdims=True) + EPS)
        grad = grad_ref[rows, :].astype(F32)
        scaled = grad * gain
        along = jnp.mean(values * scaled, axis=1, keepdims=True)
        out = added_ref[rows, :] + inverse * scaled - values * (inverse * inverse * inverse * along)
        out_ref[rows, :] = out
        if low_ref is not None:
            low_ref[rows, :] = out.astype(BF)
        here = jnp.sum(grad * (values * inverse), axis=0, keepdims=True)
        gain_sum = here if gain_sum is None else gain_sum + here
    return gain_sum


def middle_back(part, middle, cotangent, gains, w_out, held):
    size, features = middle.shape
    owners = lax.axis_size("seq")
    count = 3 * CHUNKS + 2 * (owners.bit_length() - 3)
    shape = jax.ShapeDtypeStruct
    vm = pl.BlockSpec(memory_space=pltpu.VMEM)
    return pl.pallas_call(
        middle_back_kernel,
        out_shape=(
            shape((size, features), F32), shape((size, features), BF),
            shape((size, w_out.shape[0]), F32), shape((1, features), F32),
            shape((2, owners) + held.shape[2:], BF),
        ),
        in_specs=[vm] * 6,
        out_specs=(vm,) * 5,
        scratch_shapes=HeadSum.scratch(size, features) + [
            pltpu.SemaphoreType.DMA((count,)), pltpu.SemaphoreType.DMA((count,)),
        ],
        compiler_params=pltpu.CompilerParams(
            vmem_limit_bytes=40 << 20, collective_id=5, has_side_effects=True
        ),
        name="middle_back",
    )(part, middle, cotangent, gains, w_out, held)


class Halving:
    def __init__(self, cube, copies, outgoing, incoming):
        self.cube, self.copies, self.outgoing, self.incoming = cube, copies, outgoing, incoming
        self.orders = (cube.bits, cube.bits[::-1])
        self.held = [None, None]
        self.step = [0, 0]
        self.slot = [0, 0]
        self.flying = [None, None]

    def begin(self, partials):
        for side in (0, 1):
            rows = partials[0].shape[0] // 2
            self.held[side] = {m: p[side * rows : (side + 1) * rows] for m, p in partials.items()}
            self.send(side)

    def send(self, side):
        bit = self.orders[side][self.step[side]]
        leaving = sorted(m for m in self.held[side] if m & bit)
        first = self.slot[side]
        for k, m in enumerate(leaving):
            self.outgoing[side, first + k] = self.held[side].pop(m).astype(BF)
        span = pl.ds(first, len(leaving))
        self.flying[side] = (
            self.copies.start(
                self.outgoing.at[side, span], self.incoming.at[side, span], self.cube.along(bit)
            ),
            first,
        )
        self.slot[side] += len(leaving)
        self.step[side] += 1

    def advance(self):
        for side in (0, 1):
            copy, first = self.flying[side]
            copy.wait_recv()
            for k, m in enumerate(sorted(self.held[side])):
                self.held[side][m] = self.held[side][m] + self.incoming[side, first + k].astype(F32)
            if self.step[side] < len(self.orders[side]):
                self.send(side)

    def result(self):
        return [self.held[side][0] for side in (0, 1)]


def ff_tile(tokens, grads, w_gate, w_up, w_down):
    gate = mm(tokens, w_gate)
    up = mm(tokens, w_up)
    grad = mm(grads, w_down, 1, 1)
    sig = sigmoid(gate)
    active = gate * sig
    hidden = (active * up).astype(BF)
    grad_gate = (grad * up * (sig * (1.0 + gate * (1.0 - sig)))).astype(BF)
    return hidden, grad_gate, (grad * active).astype(BF)


def near_kernel(
    tokens_ref, grads_ref, w_up_ref, w_down_ref, grad_held_ref, grad_ref, out_ref, held_ref, grad_first_ref,
    send_sems, recv_sems,
):
    cube = Cube()
    copies = Copies(send_sems, recv_sems)
    cube.greet([cube.mirror(), cube.along(cube.bits[0]), cube.along(cube.bits[-1]), cube.beside(2)])
    rows = held_ref.shape[2]
    for side in (0, 1):
        first = pl.multiple_of((2 * cube.head + side) * rows, rows)
        held_ref[side, 0] = tokens_ref[pl.ds(first, rows), :]
    spread = Spread(cube, copies, held_ref)
    cube.met(4)
    spread.send(0)
    first_side = copies.start(grad_held_ref.at[0], grad_first_ref, cube.beside(2))
    units = w_down_ref.shape[0]
    w_gate, w_up = w_up_ref[:, pl.ds(0, units)], w_up_ref[:, pl.ds(units, units)]
    hidden, grad_gate, grad_up = ff_tile(tokens_ref[...], grads_ref[...], w_gate, w_up, w_down_ref[...])
    spread.take()
    spread.send(1)
    grad_ref[...] = (mm(grad_gate, w_gate, 1, 1) + mm(grad_up, w_up, 1, 1)).astype(BF)
    out_ref[...] = mm(hidden, w_down_ref[...]).astype(BF)
    spread.take()
    first_side.wait_recv()
    copies.finish()


def near_part(tokens, grads, w_up, w_down, grad_held):
    size, features = tokens.shape
    low = jax.ShapeDtypeStruct((size, features), BF)
    rows = size // (2 * lax.axis_size("head"))
    vm = pl.BlockSpec(memory_space=pltpu.VMEM)
    hbm = pl.BlockSpec(memory_space=pl.ANY)
    return pl.pallas_call(
        near_kernel,
        out_shape=(
            low, low, jax.ShapeDtypeStruct((2, 4, rows, features), BF),
            jax.ShapeDtypeStruct(grad_held.shape[1:], BF),
        ),
        in_specs=[vm] * 4 + [hbm],
        out_specs=(vm,) * 3 + (hbm,),
        scratch_shapes=[pltpu.SemaphoreType.DMA((5,)), pltpu.SemaphoreType.DMA((5,))],
        compiler_params=pltpu.CompilerParams(
            vmem_limit_bytes=50 << 20, collective_id=6, has_side_effects=True
        ),
        name="feed_forward",
    )(tokens, grads, w_up, w_down, grad_held)


def tail_kernel(
    near_ref, normed_half_ref, normed_far_ref, gated_ref, gated_far_ref, attn_half_ref, attn_far_ref,
    normed_ref, gates_ref, part_ref, inputs_ref, gains_ref,
    middle_ref, conv_ref, mid_gain_ref, decay_ref, head_gain_ref,
    tok_own_ref, grad_own_ref, grad_first_ref, grad_second_ref, w_up_hbm, w_down_hbm,
    grad_proj_ref, grad_wout_ref, grad_inputs_ref, small_ref, grad_up_ref, grad_down_ref,
    tok_across_ref, tok_sib_ref, tok_both_ref, grad_sib_ref, grad_both_ref,
    far, outgoing, incoming, sibling, kept, across_in, total, small_out, small_in,
    w_up, w_down, blocks, load_sems, block_sems, send_sems, recv_sems,
):
    cube = Cube()
    copies = Copies(send_sems, recv_sems)
    parts, size, width = near_ref.shape
    bits = len(cube.bits)
    loads = [
        pltpu.make_async_copy(source, target, load_sems.at[k])
        for k, (source, target) in enumerate(((w_up_hbm, w_up), (w_down_hbm, w_down)))
    ]
    for load in loads:
        load.start()
    beside, across_way = cube.beside(1), cube.beside(2)
    cube.greet([cube.mirror(), beside, across_way] + [cube.along(bit) for bit in cube.bits])
    cube.met(3 + bits)
    order = (4, 3, 2, 1, 0)
    reduced = HeadSum(cube, copies, part_ref, sibling, kept, across_in, total, CHUNKS)
    for c in range(CHUNKS):
        reduced.halve(c)
    arriving = {c: copies.start(near_ref.at[c], far.at[c], cube.mirror()) for c in order[1:]}
    for c in range(CHUNKS):
        reduced.cross(c)
    arrivals = {
        ("sib", 0): copies.start(tok_own_ref, tok_sib_ref, beside),
        ("sib", 1): copies.start(grad_own_ref, grad_sib_ref, beside),
    }
    for side in (0, 1):
        arrivals["across", side] = copies.start(
            tok_own_ref.at[side], tok_across_ref.at[side], across_way
        )
    done = set()

    def ready(*names):
        for name in names:
            if name not in done:
                done.add(name)
                arrivals[name].wait_recv()

    def share_grads():
        for side, grads in ((0, grad_first_ref), (1, grad_second_ref)):
            arrivals["grads", side] = copies.start(grads, grad_both_ref.at[side], beside)

    def forward(side):
        ready(("across", side))
        arrivals["both", side] = copies.start(tok_across_ref.at[side], tok_both_ref.at[side], beside)

    sums = {}

    def partials(c):
        found = {}
        if c < parts:
            arriving[c].wait_recv()
        for m in cube.masks:
            within = cube.moved(m) % len(cube.masks)
            if c < parts:
                found[m] = mm(normed_half_ref[within], near_ref[c], 0, 0) + mm(
                    normed_far_ref[within], far[c], 0, 0
                )
            else:
                found[m] = mm(attn_half_ref[within], gated_ref[...], 0, 0) + mm(
                    attn_far_ref[within], gated_far_ref[...], 0, 0
                )
        sums[c] = Halving(cube, copies, outgoing.at[c], incoming.at[c])
        sums[c].begin(found)

    def store(c):
        for side, rows in enumerate(sums[c].result()):
            if c == parts:
                grad_wout_ref[side] = rows
                continue
            grad_proj_ref[pl.ds(side * rows.shape[0], rows.shape[0]), pl.ds(c * width, width)] = rows

    left = {c: bits for c in order}

    def advance(c):
        if left[c]:
            sums[c].advance()
            left[c] -= 1
            if not left[c]:
                store(c)

    span = grad_up_ref.shape[0]
    stretch = blocks.shape[2]
    owner_rows = pl.ds(
        pl.multiple_of(cube.place * (w_up.shape[0] // cube.count) // span * span, span), span
    )
    units = w_down.shape[0]
    pieces = []
    for first in range(0, cube.count, stretch):
        where = pl.ds(first, stretch)
        pieces.append(where)
    work = []
    for side in (0, 1):
        work += [(tok_own_ref.at[side, w], grad_own_ref.at[side, w], ()) for w in pieces]
    for side in (0, 1):
        work += [(tok_sib_ref.at[side, w], grad_sib_ref.at[side, w], (("sib", 0), ("sib", 1))) for w in pieces]
    for side in (0, 1):
        grads = (grad_first_ref, grad_second_ref)[side]
        work += [(tok_across_ref.at[side, w], grads.at[w], (("across", side),)) for w in pieces]
        work += [
            (tok_both_ref.at[side, w], grad_both_ref.at[side, w], (("both", side), ("grads", side)))
            for w in pieces
        ]
    fetched = {}

    def fetch(b):
        if b < len(work) and b not in fetched:
            fetched[b] = []
            for which in (0, 1):
                copy = pltpu.make_async_copy(
                    work[b][which], blocks.at[b % 2, which], block_sems.at[b % 2, which]
                )
                copy.start()
                fetched[b].append(copy)

    def weights(b):
        ready(*work[b][2])
        fetch(b)
        for copy in fetched[b]:
            copy.wait()
        if b + 1 < len(work) and all(name in done for name in work[b + 1][2]):
            fetch(b + 1)
        tokens = blocks[b % 2, 0].reshape(-1, w_up.shape[0])
        grads = blocks[b % 2, 1].reshape(-1, w_up.shape[0])
        own_tokens = blocks[b % 2, 0, :, :, owner_rows].reshape(-1, span)
        own_grads = blocks[b % 2, 1, :, :, owner_rows].reshape(-1, span)
        hidden, grad_gate, grad_up = ff_tile(
            tokens, grads, w_up[:, pl.ds(0, units)], w_up[:, pl.ds(units, units)], w_down[...]
        )
        found = (mm(own_tokens, grad_gate, 0, 0), mm(own_tokens, grad_up, 0, 0), mm(own_grads, hidden, 0, 0))
        targets = (
            (grad_up_ref, pl.ds(0, units)), (grad_up_ref, pl.ds(units, units)), (grad_down_ref, pl.ds(0, units))
        )
        for value, (target, cols) in zip(found, targets):
            if b == 0:
                target[:, cols] = value
            else:
                target[:, cols] += value

    ways = [cube.along(bit) for bit in cube.bits] + [cube.mirror()]
    flights = []

    def small_send():
        step = len(flights)
        small_out[step] = small_ref[...].astype(BF)
        flights.append(copies.start(small_out.at[step], small_in.at[step], ways[step]))

    taken = []

    def small_take():
        step = len(taken)
        if step == len(ways):
            return
        taken.append(step)
        flights[step].wait_recv()
        small_ref[...] = small_out[step].astype(F32) + small_in[step].astype(F32)
        if step + 1 < len(ways):
            small_send()

    def inputs_back():
        for c in range(CHUNKS):
            reduced.share(c)
        by_gates = mm(gates_ref[...], normed_ref[...])
        for c in range(CHUNKS):
            reduced.arrive(c)
        gain = gains_ref[0:1, :]
        gain_sum = norm_back(inputs_ref, total, gain, middle_ref, grad_inputs_ref, None)
        flat = [head_gain_ref[h : h + 1, :] for h in range(head_gain_ref.shape[0])]
        flat += [decay_ref[h : h + 1, :] for h in range(decay_ref.shape[0])]
        flat.append(jnp.zeros((1, gain.shape[1] - sum(f.shape[1] for f in flat)), F32))
        small_ref[...] = jnp.concatenate(
            [by_gates, conv_ref[...], gain_sum, mid_gain_ref[...], jnp.concatenate(flat, axis=1),
             jnp.zeros((2, gain.shape[1]), F32)], axis=0
        )
        small_send()

    fetch(0)
    partials(order[0])
    for load in loads:
        load.wait()
    steps = [
        lambda: None,
        lambda: (inputs_back(), share_grads()),
        lambda: (partials(3), advance(4), small_take()),
        lambda: (forward(0), advance(4), advance(3), small_take()),
        lambda: (partials(2), advance(3)),
        lambda: (partials(1), advance(2), small_take()),
        lambda: (forward(1), partials(0), advance(2), advance(1)),
        lambda: (advance(1), advance(0)),
    ]
    each = len(work) // len(steps)
    for k, step in enumerate(steps):
        for b in range(k * each, (k + 1) * each):
            weights(b)
        step()
    for step in range(len(ways)):
        small_take()
    for step in range(bits):
        for c in order:
            advance(c)
    copies.finish()


def tail(
    near, normed_half, normed_far, gated, gated_far, attn_half, attn_far, normed, gates, part, inputs, gains,
    middle, conv, mid_gain, decay, head_gain, tok_own, grad_own, grad_first, grad_second, w_up, w_down,
):
    parts, size, width = near.shape
    owners = lax.axis_size("seq")
    bits = owners.bit_length() - 2
    slots = owners // 2 - 1
    kept = normed_half.shape[2]
    span = max(kept, LANES)
    features = inputs.shape[1]
    stretch = 8
    shape = jax.ShapeDtypeStruct
    vm = pl.BlockSpec(memory_space=pltpu.VMEM)
    hbm = pl.BlockSpec(memory_space=pl.ANY)
    copies = parts + 3 * CHUNKS + bits + 1 + (parts + 1) * 2 * bits + 8
    flying = pltpu.VMEM((parts + 1, 2, slots, kept // 2, width), BF)
    held = shape(tok_own.shape, BF)
    found = pl.pallas_call(
        tail_kernel,
        out_shape=(
            shape((kept, parts * width), F32), shape((2, kept // 2, width), F32),
            shape((size, features), F32), shape((16, features), F32),
            shape((span, w_up.shape[1]), F32), shape((span, w_down.shape[0]), F32),
            held, held, held, held, held,
        ),
        in_specs=[vm] * 17 + [hbm] * 6,
        out_specs=(vm,) * 6 + (hbm,) * 5,
        scratch_shapes=[
            pltpu.VMEM((parts, size, width), BF), flying, flying, *HeadSum.scratch(size, features),
            pltpu.VMEM((bits + 1, 16, features), BF), pltpu.VMEM((bits + 1, 16, features), BF),
            pltpu.VMEM(w_up.shape, BF), pltpu.VMEM(w_down.shape, BF),
            pltpu.VMEM((2, 2, stretch) + tok_own.shape[2:], BF),
            pltpu.SemaphoreType.DMA((2,)), pltpu.SemaphoreType.DMA((2, 2)),
            pltpu.SemaphoreType.DMA((copies,)), pltpu.SemaphoreType.DMA((copies,)),
        ],
        compiler_params=pltpu.CompilerParams(
            vmem_limit_bytes=63 << 20, collective_id=3, has_side_effects=True
        ),
        name="tail",
    )(
        near, normed_half, normed_far, gated, gated_far, attn_half, attn_far, normed, gates, part, inputs, gains,
        middle, conv, mid_gain, decay, head_gain, tok_own, grad_own, grad_first, grad_second, w_up, w_down,
    )
    return found[:6]


def rms_scale(values, gain):
    return values * lax.rsqrt(jnp.mean(values * values, axis=-1, keepdims=True) + EPS) * gain


def across(array, axis, mask):
    return lax.ppermute(array, axis, [(i, i ^ mask) for i in range(lax.axis_size(axis))])


def mirrored(array):
    return across(array, "seq", lax.axis_size("seq") - 2)


def mirrored_shared(array):
    half = array.shape[0] // 2
    odd = lax.axis_index("head") % 2
    mine = mirrored(lax.dynamic_slice_in_dim(array, odd * half, half, 0))
    other = across(mine, "head", 1)
    first = jnp.where(odd == 0, mine, other)
    second = jnp.where(odd == 0, other, mine)
    return jnp.concatenate([first, second], axis=0)


def own_half_columns(array, of):
    width = array.shape[1] // 2
    return lax.dynamic_slice_in_dim(array, of * width, width, 1)


def shards(
    inputs,
    gains,
    w_proj,
    w_gates,
    decay,
    conv_w,
    head_gain,
    w_out,
    w_up,
    w_down,
    seq_first,
    cotangent,
):
    tokens = inputs.shape[0]
    heads_here = decay.shape[1]
    owners = lax.axis_size("seq")
    place = lax.axis_index("seq")
    half = place // (owners // 2)
    masks = range(owners // 2)
    kept = inputs.shape[1] // owners

    normed_low = rms_scale(inputs, gains[0]).astype(BF)
    grad_low = cotangent.astype(BF)
    share = tokens // lax.axis_size("head")
    grad_own = lax.dynamic_slice_in_dim(cotangent, lax.axis_index("head") * share, share, 0)
    grad_own = grad_own.astype(BF).reshape(2, share // 2, -1)
    w_up_flat = w_up.reshape(w_up.shape[0], -1)
    projected = jnp.einsum("td,dkc->ktc", normed_low, w_proj, preferred_element_type=F32)
    gate_in = jnp.einsum("td,idh->iht", normed_low, w_gates, preferred_element_type=F32)
    gate_in = gate_in.reshape(2 * heads_here, tokens)
    gated_low, recurrent, lift, inverse, solved, gram, score, state, pair, rim, grad_far = recurrent_forward(
        seq_first, decay, gate_in, projected, conv_w, head_gain, grad_own
    )
    middle, normed_mid_low, grad_held = middle_of(gated_low, w_out, inputs, gains, grad_own, grad_far)
    grad_mid_part, mlp_part, mid_part_held, grad_first = near_part(
        normed_mid_low, grad_low, w_up_flat, w_down, grad_held
    )
    output = middle + lax.psum(mlp_part, "head").astype(F32)
    grad_middle, grad_attn_low, grad_gated, grad_gain_mid, mid_held = middle_back(
        grad_mid_part, middle, cotangent, gains, w_out, mid_part_held
    )
    gated_far = mirrored(gated_low)
    grad_attn_far = mirrored_shared(own_half_columns(grad_attn_low, 1 - half))
    grad_projected, grad_conv, grad_gate_in, grad_decay, grad_head_gain, grad_second = recurrent_backward(
        seq_first, decay, gate_in, projected, rim, conv_w, head_gain, grad_gated,
        (recurrent, lift, inverse, solved, gram, score, state, pair), grad_held,
    )
    grad_gate_low = grad_gate_in.reshape(2, heads_here, tokens).astype(BF)
    normed_far = mirrored_shared(own_half_columns(normed_low, 1 - half))
    grad_normed_part = jnp.einsum(
        "ktc,dkc->td", grad_projected, w_proj, preferred_element_type=jnp.float32
    )
    grad_normed_part = grad_normed_part + jnp.einsum(
        "iht,idh->td", grad_gate_low, w_gates, preferred_element_type=jnp.float32
    )
    by_owner = lambda array: jnp.swapaxes(array.reshape(tokens, len(masks), kept), 0, 1)
    grad_proj_part, grad_wout_part, grad_inputs, small, grad_up_part, grad_down_part = tail(
        grad_projected, by_owner(own_half_columns(normed_low, half)), by_owner(normed_far),
        gated_low, gated_far, by_owner(own_half_columns(grad_attn_low, half)), by_owner(grad_attn_far), normed_low,
        grad_gate_in.astype(BF), grad_normed_part.astype(BF), inputs, gains, grad_middle,
        grad_conv.reshape(3, -1), grad_gain_mid, grad_decay, grad_head_gain,
        mid_held, grad_held, grad_first, grad_second, w_up_flat, w_down,
    )
    features = inputs.shape[1]
    grad_proj_part = grad_proj_part.reshape(kept, 4, -1)
    grad_wgates = jnp.swapaxes(small[0 : 2 * heads_here].reshape(2, heads_here, features), 1, 2)
    grad_conv = small[8:11].reshape(grad_conv.shape)
    hdim = head_gain.shape[1]
    grad_head_gain = small[13, : heads_here * hdim].reshape(heads_here, hdim)
    grad_decay = small[13, heads_here * hdim : heads_here * (hdim + 128)].reshape(heads_here, 128)
    grad_decay = grad_decay[:, :2].T
    grad_wout_part = grad_wout_part.reshape(kept, -1).T
    first = place * kept % grad_up_part.shape[0]
    grad_up_part = lax.dynamic_slice_in_dim(grad_up_part, first, kept, 0).reshape(kept, 2, -1)
    grad_down_part = lax.dynamic_slice_in_dim(grad_down_part, first, kept, 0).T
    return (
        output,
        grad_inputs,
        small[11:13],
        grad_proj_part,
        grad_wgates,
        grad_decay,
        grad_conv,
        grad_head_gain,
        grad_wout_part,
        grad_up_part,
        grad_down_part,
    )


def solution(mesh):
    placed = (
        P("seq", None),
        P(),
        P(None, None, "head"),
        P(None, None, "head"),
        P(None, "head"),
        P(None, None, "head"),
        P("head", None),
        P("head", None),
        P(None, None, "head"),
        P("head", None),
        P("seq"),
        P("seq", None),
    )
    return jax.shard_map(
        shards,
        mesh=mesh,
        in_specs=placed,
        out_specs=(
            P("seq", None),
            P("seq", None),
            P(),
            P("seq", None, "head"),
            P(None, None, "head"),
            P(None, "head"),
            P(None, None, "head"),
            P("head", None),
            P("head", "seq"),
            P("seq", None, "head"),
            P("head", "seq"),
        ),
        check_vma=False,
    )
```

```python
import functools

import jax
import jax.numpy as jnp
from jax import lax
from jax.experimental import pallas as pl
from jax.experimental.pallas import tpu as pltpu
from jax.sharding import PartitionSpec as P

EPS = 1e-06
GROUP = 64
BF = jnp.bfloat16
F32 = jnp.float32


def mm(a, b, ca=1, cb=0):
    return lax.dot_general(
        a.astype(BF), b.astype(BF), (((ca,), (cb,)), ((), ())), preferred_element_type=F32
    )


def split(a):
    high = a.astype(BF)
    return high, (a - high.astype(F32)).astype(BF)


def mm3(a, b, ca=1, cb=0):
    ah, al = split(a)
    bh, bl = split(b)
    return mm(ah, bh, ca, cb) + (mm(ah, bl, ca, cb) + mm(al, bh, ca, cb))


def mm_exact(a, b):
    return lax.dot_general(
        a, b, (((1,), (0,)), ((), ())), preferred_element_type=F32, precision=lax.Precision.HIGHEST
    )


def sigmoid(v):
    return 1.0 / (1.0 + jnp.exp(-v))


def softplus(v):
    return jnp.maximum(v, 0.0) + jnp.log1p(jnp.exp(-jnp.abs(v)))


def block_sums(first_ref, shape, axis):
    block = lax.broadcasted_iota(jnp.int32, shape, axis) // GROUP
    seen = jnp.zeros(shape, F32)
    starts = jnp.zeros(shape, F32)
    for b in range(first_ref.shape[0]):
        flag = first_ref[b].astype(F32)
        seen = seen + jnp.where(block >= b, flag, 0.0)
        starts = starts + jnp.where(block == b, flag, 0.0)
    return seen, starts


def gate_rows(gates_ref, decay_ref, heads):
    rows = []
    size = gates_ref.shape[1]
    for h in range(heads):
        rate = jnp.exp(jnp.full((1, size), decay_ref[0, h], F32))
        bias = decay_ref[1, h]
        rows.append(-rate * softplus(gates_ref[heads + h : heads + h + 1, :] + bias))
    return jnp.concatenate(rows, axis=0)


def tap_keeps(starts, taps):
    size = starts.shape[0]
    offset = lax.broadcasted_iota(jnp.int32, (size, 1), 0) % GROUP
    return [1.0 - jnp.where(offset < taps - 1 - j, starts, 0.0) for j in range(taps)]


def convolved(ext_ref, part, cols, convw_ref, keeps):
    size = ext_ref.shape[1] - 8
    taps = len(keeps)
    total = None
    for j in range(taps):
        shifted = ext_ref[part, pl.ds(8 - (taps - 1) + j, size), cols]
        if j < taps - 1:
            shifted = shifted * keeps[j]
        term = shifted * convw_ref[part, j : j + 1, cols]
        total = term if total is None else total + term
    return total


def fade_of(cum_col, cum_row, seen_col, seen_row):
    size = cum_col.shape[0]
    row = lax.broadcasted_iota(jnp.int32, (size, size), 0)
    col = lax.broadcasted_iota(jnp.int32, (size, size), 1)
    inside = (row > col) & (seen_col == seen_row)
    fade = jnp.where(inside, jnp.exp(jnp.minimum(cum_col - cum_row, 0.0)), 0.0)
    return jnp.where(row == col, 1.0, fade), inside


def fill_ext(ext, proj_ref, rim_ref):
    size = proj_ref.shape[1]
    for part in range(3):
        ext[part, pl.ds(0, 8), :] = rim_ref[part]
        ext[part, pl.ds(8, size), :] = proj_ref[part].astype(BF).astype(F32)


def tri(size, upper):
    row = lax.broadcasted_iota(jnp.int32, (size, size), 0)
    col = lax.broadcasted_iota(jnp.int32, (size, size), 1)
    return jnp.where((row <= col) if upper else (row >= col), 1.0, 0.0).astype(F32)


class Scan:
    def __init__(self, first_ref, decay_ref, gates_ref, heads):
        size = gates_ref.shape[1]
        self.log_rows = gate_rows(gates_ref, decay_ref, heads)
        self.seen_row, _ = block_sums(first_ref, (1, size), 1)
        self.seen_col, self.starts = block_sums(first_ref, (size, 1), 0)
        padded = jnp.concatenate([self.log_rows, jnp.zeros((8 - heads, size), F32)], axis=0)
        self.cum_rows = mm_exact(padded, tri(size, True))
        strength_rows = sigmoid(gates_ref[0:heads, :])
        both = jnp.concatenate([self.cum_rows[0:heads], strength_rows], axis=0)
        both = jnp.concatenate([both, jnp.zeros((128 - 2 * heads, size), F32)], axis=0)
        cols = both.T
        self.cum_cols = [cols[:, h : h + 1] for h in range(heads)]
        self.strength = [cols[:, heads + h : heads + h + 1] for h in range(heads)]

    def of(self, h):
        cum_col, cum_row = self.cum_cols[h], self.cum_rows[h : h + 1, :]
        size = cum_col.shape[0]
        last = cum_col[size - 1 : size, :]
        fade, inside = fade_of(cum_col, cum_row, self.seen_col, self.seen_row)
        growth = jnp.where(self.seen_col == 0.0, jnp.exp(cum_col), 0.0)
        last_seen = self.seen_col[size - 1 : size, :]
        to_end = jnp.where(self.seen_col == last_seen, jnp.exp(jnp.minimum(last - cum_col, 0.0)), 0.0)
        carry = jnp.where(last_seen == 0.0, jnp.exp(last), 0.0)
        return fade, inside, growth, to_end, carry


def unit(a, scale):
    inverse = lax.rsqrt(jnp.sum(a * a, axis=1, keepdims=True) + EPS)
    return a * (inverse * scale), inverse


MESH = pl.DeviceIdType.MESH


class Ring:
    def __init__(self):
        self.count = lax.axis_size("seq")
        self.place = lax.axis_index("seq")
        self.head = lax.axis_index("head")
        self.side = self.place % 2
        self.pair = self.place // 2
        self.pairs = self.count // 2
        self.partner = self.place + 1 - 2 * self.side
        self.cross = self.place + 2 * self.side - 1
        self.mirror = self.count - 2 - self.place + 2 * self.side
        self.sibling = self.head + 1 - 2 * (self.head % 2)

    def device(self, place):
        return (place, self.head)

    def across(self):
        return (self.place, (self.head + 2) % lax.axis_size("head"))

    def across_copy(self, source, target, sems, index):
        return pltpu.make_async_remote_copy(
            src_ref=source, dst_ref=target, send_sem=sems[0].at[index], recv_sem=sems[1].at[index],
            device_id=self.across(), device_id_type=MESH,
        )

    def greet(self, mirror=False, across=False, sibling=False):
        barrier = pltpu.get_barrier_semaphore()

        def tell(place):
            pl.semaphore_signal(barrier, inc=1, device_id=self.device(place), device_id_type=MESH)

        tell(self.partner)
        if mirror:
            tell(self.mirror)
        if across:
            pl.semaphore_signal(barrier, inc=1, device_id=self.across(), device_id_type=MESH)
        if sibling:
            pl.semaphore_signal(barrier, inc=1, device_id=(self.place, self.sibling), device_id_type=MESH)
        for place in (self.place - 2, self.place + 2, self.cross):
            pl.when((place >= 0) & (place < self.count))(functools.partial(tell, place))

    def met(self, mirror=False, across=False, sibling=False):
        inside = lambda place: jnp.where((place >= 0) & (place < self.count), 1, 0)
        known = inside(self.place - 2) + inside(self.place + 2) + inside(self.cross)
        always = 1 + int(mirror) + int(across) + int(sibling)
        pl.semaphore_wait(pltpu.get_barrier_semaphore(), known + always)

    def copy(self, source, target, sems, index, place):
        return pltpu.make_async_remote_copy(
            src_ref=source, dst_ref=target, send_sem=sems[0].at[index], recv_sem=sems[1].at[index],
            device_id=self.device(place), device_id_type=MESH,
        )


def forward_kernel(
    heads, first_ref, decay_ref, gates_ref, proj_ref, convw_ref, gain_ref, cotangent_ref,
    gated_ref, rec_ref, lift_ref, inv_ref, solved_ref, gram_ref, score_ref, state_ref, pair_ref, rim_ref, own_ref, far_ref,
    ext, base, maps, other, chain_in, chain_out, state_out, state_in, rim_out, rim_in, send_sems, recv_sems,
):
    ring = Ring()
    ring.greet(True)
    sems = (send_sems, recv_sems)
    size = proj_ref.shape[1]
    hdim = proj_ref.shape[2] // heads
    taps = convw_ref.shape[1]
    mine = heads // 2
    for part in range(3):
        rows = proj_ref[part].astype(BF).astype(F32)
        ext[part, pl.ds(8, size), :] = rows
        rim_out[part] = rows[size - 8 :, :]
    share = own_ref.shape[0] * own_ref.shape[1]
    share_rows = pl.ds(pl.multiple_of(ring.head * share, share), share)
    own_ref[...] = cotangent_ref[share_rows, :].astype(BF).reshape(own_ref.shape)
    scan = Scan(first_ref, decay_ref, gates_ref, heads)
    ring.met(True)
    has_before, has_after = ring.place > 0, ring.place < ring.count - 1
    rim_copy = ring.copy(rim_out, rim_in, sems, 0, ring.place + 1)
    pl.when(has_after)(rim_copy.start)
    far_copy = ring.copy(own_ref, far_ref, sems, 1 + 3 * mine, ring.mirror)
    far_copy.start()

    @pl.when(ring.place == 0)
    def _():
        rim_in[...] = jnp.zeros_like(rim_in)

    keeps = tap_keeps(scan.starts, taps)
    eye = lax.broadcasted_iota(jnp.int32, (size, size), 0) == lax.broadcasted_iota(
        jnp.int32, (size, size), 1
    )
    apart = lax.broadcasted_iota(jnp.int32, (size, size), 0) ^ lax.broadcasted_iota(
        jnp.int32, (size, size), 1
    )
    pl.when(has_before)(rim_copy.wait_recv)
    for part in range(3):
        ext[part, pl.ds(0, 8), :] = rim_in[part]
        rim_ref[part] = rim_in[part]
    held = []
    for h in range(heads):
        cols = pl.ds(h * hdim, hdim)
        acts = []
        for part in range(3):
            u = convolved(ext, part, cols, convw_ref, keeps)
            acts.append(u * sigmoid(u))
        q, _ = unit(acts[0], hdim ** -0.5)
        k, _ = unit(acts[1], 1.0)
        v = acts[2]
        fade, inside, growth, to_end, carry = scan.of(h)
        beta = scan.strength[h]
        gram = mm(k, k, 1, 1) * jnp.where(inside, fade, 0.0)
        score = mm(q, k, 1, 1) * fade
        gram_ref[h] = gram.astype(BF)
        score_ref[h] = score.astype(BF)
        system = beta * gram
        held.append((q, k, v, growth, to_end, carry, beta, system))
    inverses = [jnp.where(eye, 1.0, 0.0) - jnp.where(apart == 1, t[7], 0.0) for t in held]
    block = 2
    while block < size:
        level = (apart >= block) & (apart < 2 * block)
        inner = [mm(jnp.where(level, t[7], 0.0), inv) for t, inv in zip(held, inverses)]
        inverses = [inv - mm(inv, y) for inv, y in zip(inverses, inner)]
        block *= 2
    left = [jnp.where(eye, 1.0, 0.0) - inv - mm3(t[7], inv) for t, inv in zip(held, inverses)]
    inverses = [inv + mm(inv, r) for inv, r in zip(inverses, left)]
    for h in range(heads):
        q, k, v, growth, to_end, carry, beta, system = held[h]
        inv = inverses[h].astype(BF)
        inv_ref[h] = inv
        right = jnp.concatenate([beta * growth * k, beta * v], axis=1)
        solved = mm(inv, right).astype(BF)
        solved_ref[h] = solved
        ends = mm(k * to_end, solved, 0, 0)
        factor = jnp.where(eye[:hdim, :hdim], carry, 0.0) - ends[:, :hdim]
        maps[h] = jnp.concatenate([factor, ends[:, hdim:]], axis=1).astype(BF)
    map_copies = [
        ring.copy(maps.at[(1 - ring.side) * mine + i], other.at[i], sems, 1 + i, ring.partner)
        for i in range(mine)
    ]
    for copy in map_copies:
        copy.start()
    for h in range(heads):
        q, k, v, growth, to_end, carry, beta, system = held[h]
        mixed = mm(score_ref[h], solved_ref[h])
        lift_ref[h] = (q * growth - mixed[:, :hdim]).astype(BF)
        base[h] = mixed[:, hdim:]
    chain_copies = [
        ring.copy(chain_out.at[i], chain_in.at[i], sems, 1 + mine + i, ring.place + 2) for i in range(mine)
    ]
    state_copies = [
        ring.copy(state_out.at[i], state_in.at[i], sems, 1 + 2 * mine + i, ring.partner) for i in range(mine)
    ]
    from_before, to_after = ring.pair > 0, ring.pair < ring.pairs - 1

    @pl.when(jnp.logical_not(from_before))
    def _():
        chain_in[...] = jnp.zeros_like(chain_in)

    whole, before = [], []
    for i in range(mine):
        map_copies[i].wait_recv()
        own, far = maps[ring.side * mine + i], other[i]
        early = jnp.where(ring.side == 0, own, far)
        late = jnp.where(ring.side == 0, far, own)
        both = mm(late[:, :hdim], early)
        whole.append((both[:, :hdim].astype(BF), both[:, hdim:] + late[:, hdim:].astype(F32)))
        before.append(early)
        pair_ref[0, i] = early[:, :hdim]
        pair_ref[1, i] = late[:, :hdim]
        pair_ref[2, i] = whole[i][0]
    for i in range(mine):
        pl.when(from_before)(chain_copies[i].wait_recv)
        chain_out[i] = (mm(whole[i][0], chain_in[i]) + whole[i][1]).astype(BF)
        pl.when(to_after)(chain_copies[i].start)
    for i in range(mine):
        first = chain_in[i]
        second = (mm(before[i][:, :hdim], first) + before[i][:, hdim:].astype(F32)).astype(BF)
        state_out[i] = jnp.where(ring.side == 0, second, first)
        state_copies[i].start()
        state_ref[ring.side * mine + i] = jnp.where(ring.side == 0, first, second)
    for i in range(mine):
        state_copies[i].wait_recv()
        state_ref[(1 - ring.side) * mine + i] = state_in[i]
    for h in range(heads):
        cols = pl.ds(h * hdim, hdim)
        rec = mm(lift_ref[h], state_ref[h]) + base[h]
        rec_ref[h] = rec
        inverse = lax.rsqrt(jnp.mean(rec * rec, axis=1, keepdims=True) + EPS)
        gate = proj_ref[3, :, cols]
        gated_ref[:, cols] = (
            rec * inverse * gain_ref[h : h + 1, :] * (gate * sigmoid(gate))
        ).astype(BF)
    pl.when(has_after)(rim_copy.wait_send)
    for i in range(mine):
        map_copies[i].wait_send()
        pl.when(to_after)(chain_copies[i].wait_send)
        state_copies[i].wait_send()
    far_copy.wait()


def recurrent_forward(first, decay, gates, proj, convw, gain, cotangent):
    heads = decay.shape[1]
    parts, size, width = proj.shape
    hdim = width // heads
    mine = heads // 2
    shape = jax.ShapeDtypeStruct
    vm = pl.BlockSpec(memory_space=pltpu.VMEM)
    sm = pl.BlockSpec(memory_space=pltpu.SMEM)
    square = shape((heads, size, size), BF)
    share = shape((2, size // (2 * lax.axis_size("head")), cotangent.shape[1]), BF)
    count = 2 + 3 * mine
    states = lambda count: pltpu.VMEM((count, hdim, hdim), BF)
    return pl.pallas_call(
        functools.partial(forward_kernel, heads),
        out_shape=(
            shape((size, width), BF), shape((heads, size, hdim), F32), shape((heads, size, hdim), BF),
            square, shape((heads, size, 2 * hdim), BF), square, square,
            shape((heads, hdim, hdim), BF), shape((3, mine, hdim, hdim), BF), shape((3, 8, width), F32),
            share, share,
        ),
        in_specs=[sm, sm, vm, vm, vm, vm, vm],
        out_specs=(vm,) * 12,
        scratch_shapes=[
            pltpu.VMEM((3, size + 8, width), F32), pltpu.VMEM((heads, size, hdim), F32),
            pltpu.VMEM((heads, hdim, 2 * hdim), BF), pltpu.VMEM((mine, hdim, 2 * hdim), BF),
            states(mine), states(mine), states(mine), states(mine),
            pltpu.VMEM((3, 8, width), F32), pltpu.VMEM((3, 8, width), F32),
            pltpu.SemaphoreType.DMA((count,)), pltpu.SemaphoreType.DMA((count,)),
        ],
        compiler_params=pltpu.CompilerParams(
            vmem_limit_bytes=56 << 20, collective_id=1, has_side_effects=True
        ),
        name="recurrent_forward",
    )(first, decay, gates, proj, convw, gain, cotangent)


class Cube:
    def __init__(self):
        self.count = lax.axis_size("seq")
        self.place = lax.axis_index("seq")
        self.head = lax.axis_index("head")
        self.bits = []
        bit = 1
        while bit < self.count // 2:
            self.bits.append(bit)
            bit *= 2
        self.masks = range(self.count // 2)

    def moved(self, mask, of=None):
        place = self.place if of is None else of
        bit = 1
        while bit <= mask:
            if mask & bit:
                place = place + bit - 2 * bit * ((place // bit) % 2)
            bit *= 2
        return place

    def along(self, mask):
        return (self.moved(mask), self.head)

    def mirror(self):
        return self.along(self.count - 2)

    def beside(self, bit):
        return (self.place, self.moved(bit, self.head))

    def greet(self, devices):
        barrier = pltpu.get_barrier_semaphore()
        for device in devices:
            pl.semaphore_signal(barrier, inc=1, device_id=device, device_id_type=MESH)

    def met(self, count):
        pl.semaphore_wait(pltpu.get_barrier_semaphore(), count)


class Copies:
    def __init__(self, send_sems, recv_sems):
        self.sems = (send_sems, recv_sems)
        self.made = []

    def start(self, source, target, device):
        index = len(self.made)
        copy = pltpu.make_async_remote_copy(
            src_ref=source, dst_ref=target, send_sem=self.sems[0].at[index],
            recv_sem=self.sems[1].at[index], device_id=device, device_id_type=MESH,
        )
        copy.start()
        self.made.append(copy)
        return copy

    def finish(self):
        for copy in self.made:
            copy.wait_send()


LANES = 128


class Spread:
    def __init__(self, cube, copies, held):
        self.cube, self.copies, self.held = cube, copies, held
        self.ways = (
            [cube.mirror()] + [cube.along(bit) for bit in cube.bits],
            [cube.mirror()] + [cube.along(bit) for bit in cube.bits[::-1]],
        )
        self.flights = []

    def send(self, step):
        count = 1 << step
        self.flights = [
            self.copies.start(
                self.held.at[side, pl.ds(0, count)], self.held.at[side, pl.ds(count, count)],
                self.ways[side][step],
            )
            for side in (0, 1)
        ]

    def take(self):
        for copy in self.flights:
            copy.wait_recv()


class HeadSum:
    def __init__(self, cube, copies, part, sibling, kept, across_in, total, chunks):
        self.cube, self.copies, self.chunks = cube, copies, chunks
        self.part, self.sibling, self.kept, self.across_in, self.total = (
            part, sibling, kept, across_in, total,
        )
        size, width = part.shape
        self.span, self.width = size // 2, width // chunks
        low = cube.head % 2
        self.own = pl.ds(pl.multiple_of(low * self.span, self.span), self.span)
        self.other = pl.ds(pl.multiple_of((1 - low) * self.span, self.span), self.span)
        self.flights = {}

    def cols(self, c):
        return pl.ds(c * self.width, self.width)

    def halve(self, c):
        cols = self.cols(c)
        self.flights[c] = self.copies.start(
            self.part.at[self.other, cols], self.sibling.at[:, cols], self.cube.beside(1)
        )

    def cross(self, c):
        cols = self.cols(c)
        self.flights[c].wait_recv()
        self.kept[:, cols] = (
            self.part[self.own, cols].astype(F32) + self.sibling[:, cols].astype(F32)
        ).astype(BF)
        self.flights[c] = self.copies.start(
            self.kept.at[:, cols], self.across_in.at[:, cols], self.cube.beside(2)
        )

    def share(self, c):
        cols = self.cols(c)
        self.flights[c].wait_recv()
        self.total[self.own, cols] = (
            self.kept[:, cols].astype(F32) + self.across_in[:, cols].astype(F32)
        ).astype(BF)
        rows = self.total.at[self.own, cols]
        self.flights[c] = self.copies.start(rows, rows, self.cube.beside(1))

    def arrive(self, c):
        self.flights[c].wait_recv()

    @staticmethod
    def scratch(size, width):
        half = pltpu.VMEM((size // 2, width), BF)
        return [half, half, half, pltpu.VMEM((size, width), BF)]


CHUNKS = 4


def unit_back(a, inverse, scale, grad):
    along = jnp.sum(a * grad, axis=1, keepdims=True)
    return scale * (inverse * grad - a * (inverse * inverse * inverse * along))


def backward_kernel(
    heads, first_ref, decay_ref, gates_ref, proj_ref, rim_ref, convw_ref,
    gain_ref, grad_gated_ref, rec_ref, lift_ref, inv_ref, solved_ref, gram_ref, score_ref, state_ref, pair_ref, grad_held_ref, mid_held_ref, attn_ref, normed_ref, mlp_ref, middle_ref,
    grad_proj_ref, grad_convw_ref, grad_gates_ref, grad_decay_ref, grad_gain_ref, grad_second_ref, tok_first_ref, attn_far_ref, by_gates_ref, output_ref,
    ext, back, grad_rec, local, other, chain_in, chain_out, state_out, state_in, grad_end_all,
    edge_out, edge_in, last_rows, sibling, kept, across_in, total, head_send, head_recv, send_sems, recv_sems,
):
    ring = Ring()
    ring.greet(mirror=True, across=True, sibling=True)
    sems = (send_sems, recv_sems)
    mine = heads // 2
    size = proj_ref.shape[1]
    hdim = proj_ref.shape[2] // heads
    taps = convw_ref.shape[1]
    for h in range(heads):
        cols = pl.ds(h * hdim, hdim)
        rec = rec_ref[h]
        inverse = lax.rsqrt(jnp.mean(rec * rec, axis=1, keepdims=True) + EPS)
        gate = proj_ref[3, :, cols]
        sig = sigmoid(gate)
        gain = gain_ref[h : h + 1, :]
        normed = rec * inverse
        grad_gated = grad_gated_ref[:, cols]
        by_normed = grad_gated * normed
        grad_proj_ref[3, :, cols] = (
            by_normed * gain * (sig * (1.0 + gate * (1.0 - sig)))
        ).astype(BF)
        active = gate * sig
        grad_gain_ref[h : h + 1, :] = jnp.sum(by_normed * active, axis=0, keepdims=True)
        grad_normed = grad_gated * (active * gain)
        along = jnp.mean(rec * grad_normed, axis=1, keepdims=True)
        grad_rec[h] = inverse * grad_normed - rec * (inverse * inverse * inverse * along)
        local[h] = mm(lift_ref[h], grad_rec[h], 0, 0).astype(BF)
    ring.met(mirror=True, across=True, sibling=True)
    base = 1 + 3 * mine
    early = ring.count // 2
    second_side = ring.across_copy(
        grad_held_ref.at[1, pl.ds(early, ring.count - early)], grad_second_ref, sems, base
    )
    second_side.start()
    head_copies = Copies(head_send, head_recv)
    head_sum = HeadSum(Cube(), head_copies, mlp_ref, sibling, kept, across_in, total, CHUNKS)
    for c in range(CHUNKS):
        head_sum.halve(c)
    local_copies = [
        ring.copy(local.at[(1 - ring.side) * mine + i], other.at[i], sems, 1 + i, ring.partner)
        for i in range(mine)
    ]
    for copy in local_copies:
        copy.start()
    for c in range(CHUNKS):
        head_sum.cross(c)
    tok_first = ring.across_copy(mid_held_ref.at[0, pl.ds(0, early)], tok_first_ref, sems, base + 1)
    tok_first.start()
    fill_ext(ext, proj_ref, rim_ref)
    scan = Scan(first_ref, decay_ref, gates_ref, heads)
    keeps = tap_keeps(scan.starts, taps)
    chain_copies = [
        ring.copy(chain_out.at[i], chain_in.at[i], sems, 1 + mine + i, ring.place - 2) for i in range(mine)
    ]
    state_copies = [
        ring.copy(state_out.at[i], state_in.at[i], sems, 1 + 2 * mine + i, ring.partner) for i in range(mine)
    ]
    from_after, to_before = ring.pair < ring.pairs - 1, ring.pair > 0

    @pl.when(jnp.logical_not(from_after))
    def _():
        chain_in[...] = jnp.zeros_like(chain_in)

    lates, boths = [], []
    for i in range(mine):
        local_copies[i].wait_recv()
        own, far = local[ring.side * mine + i], other[i]
        early = jnp.where(ring.side == 0, own, far)
        late = jnp.where(ring.side == 0, far, own)
        lates.append(late.astype(F32))
        boths.append(early.astype(F32) + mm(pair_ref[0, i], late, 0, 0))
    for i in range(mine):
        pl.when(from_after)(chain_copies[i].wait_recv)
        chain_out[i] = (mm(pair_ref[2, i], chain_in[i], 0, 0) + boths[i]).astype(BF)
        pl.when(to_before)(chain_copies[i].start)
    for i in range(mine):
        last = chain_in[i]
        mid = (mm(pair_ref[1, i], last, 0, 0) + lates[i]).astype(BF)
        state_out[i] = jnp.where(ring.side == 0, last, mid)
        state_copies[i].start()
        grad_end_all[ring.side * mine + i] = jnp.where(ring.side == 0, mid, last)
    for i in range(mine):
        state_copies[i].wait_recv()
        grad_end_all[(1 - ring.side) * mine + i] = state_in[i]
    core = ring.head % 2
    span = attn_ref.shape[2]
    core_rows = attn_far_ref.at[:, :, pl.ds(pl.multiple_of(core * span, span), span)]
    attn_copy = ring.copy(attn_ref, core_rows, sems, base + 2, ring.mirror)
    share_copy = pltpu.make_async_remote_copy(
        src_ref=core_rows, dst_ref=core_rows, send_sem=sems[0].at[base + 3], recv_sem=sems[1].at[base + 3],
        device_id=(ring.place, ring.sibling), device_id_type=MESH,
    )
    grad_cums = []
    grad_strengths = []
    for h in range(heads):
        if h == 0:
            attn_copy.start()
        cols = pl.ds(h * hdim, hdim)
        fade, inside, growth, to_end, carry = scan.of(h)
        beta = scan.strength[h]
        sums, sigs, acts = [], [], []
        for part in range(3):
            u = convolved(ext, part, cols, convw_ref, keeps)
            s = sigmoid(u)
            sums.append(u)
            sigs.append(s)
            acts.append(u * s)
        q, q_inv = unit(acts[0], hdim ** -0.5)
        k, k_inv = unit(acts[1], 1.0)
        v = acts[2]
        state, grad_out, grad_end = state_ref[h], grad_rec[h], grad_end_all[h]
        solved = solved_ref[h]
        score = score_ref[h]
        weights, values = solved[:, :hdim], solved[:, hdim:]
        k_end = k * to_end
        fresh = values.astype(F32) - mm(weights, state)
        grad_fresh = mm(score, grad_out, 0, 0) + mm(k_end, grad_end)
        over_state = mm(jnp.concatenate([grad_out, grad_fresh], axis=0), state, 1, 1)
        grad_q_grow = over_state[:size]
        grad_weights = -over_state[size:]
        grad_k_end = mm(fresh, grad_end, 1, 1)
        grad_score = mm(grad_out, fresh, 1, 1)
        grad_carry = jnp.sum(
            jnp.sum(grad_end.astype(F32) * state.astype(F32), axis=1, keepdims=True), axis=0, keepdims=True
        )
        grad_right = mm(inv_ref[h], jnp.concatenate([grad_weights, grad_fresh], axis=1), 0, 0)
        grad_system = -mm(grad_right, solved, 1, 1)
        gram = gram_ref[h].astype(F32)
        by_gram = grad_system * gram
        grad_gram = jnp.where(inside, grad_system * (beta * fade), 0.0)
        grad_pair = jnp.where(fade > 0.0, grad_score * fade, 0.0)
        stacked = jnp.concatenate([grad_gram, grad_pair], axis=0)
        forward_terms = mm(stacked, k)
        back_terms = mm(stacked, jnp.concatenate([k, q], axis=0), 0, 0)
        grad_right_k, grad_right_v = grad_right[:, :hdim], grad_right[:, hdim:]
        beta_growth = beta * growth
        grad_q = forward_terms[size:] + growth * grad_q_grow
        grad_k = forward_terms[:size] + back_terms + beta_growth * grad_right_k + to_end * grad_k_end
        grad_v = beta * grad_right_v
        right_k = jnp.sum(grad_right_k * k, axis=1, keepdims=True) * growth
        right_v = jnp.sum(grad_right_v * v, axis=1, keepdims=True)
        by_rows = jnp.sum(by_gram, axis=1, keepdims=True)
        grad_strengths.append(by_rows + right_k + right_v)
        spread = beta * by_gram + jnp.where(inside, grad_score * score.astype(F32), 0.0)
        ends = jnp.sum(grad_k_end * k_end, axis=1, keepdims=True)
        grad_cum = (
            jnp.sum(spread, axis=1, keepdims=True)
            + beta * right_k
            + jnp.sum(grad_q_grow * q, axis=1, keepdims=True) * growth
            - ends
        )
        to_last = jnp.sum(ends, axis=0, keepdims=True) + grad_carry * carry
        is_last = lax.broadcasted_iota(jnp.int32, (size, 1), 0) == size - 1
        grad_cum = grad_cum + jnp.where(is_last, to_last, 0.0)
        grad_cums.append((grad_cum, jnp.sum(spread, axis=0, keepdims=True)))
        grads = (
            unit_back(acts[0], q_inv, hdim ** -0.5, grad_q),
            unit_back(acts[1], k_inv, 1.0, grad_k),
            grad_v,
        )
        for part in range(3):
            u, s = sums[part], sigs[part]
            grad_u = grads[part] * (s * (1.0 + u * (1.0 - s)))
            total = None
            taps_here = []
            for j in range(taps):
                kept = grad_u * keeps[j] if j < taps - 1 else grad_u
                shifted = ext[part, pl.ds(8 - (taps - 1) + j, size), cols]
                taps_here.append(jnp.sum(kept * shifted, axis=0, keepdims=True))
                back[j, pl.ds(0, 8), :] = jnp.zeros((8, hdim), F32)
                back[j, pl.ds(8, size), :] = kept * convw_ref[part, j : j + 1, cols]
                back[j, pl.ds(8 + size, 8), :] = jnp.zeros((8, hdim), F32)
            grad_convw_ref[part, :, cols] = jnp.concatenate(taps_here, axis=0)
            for j in range(taps):
                term = back[j, pl.ds(8 + (taps - 1) - j, size), :]
                total = term if total is None else total + term
            grad_proj_ref[part, :, cols] = total.astype(BF)
            last_rows[part, :, cols] = total[size - 16 :, :]
            edge = None
            for j in range(taps):
                term = back[j, pl.ds((taps - 1) - j, 8), :]
                edge = term if edge is None else edge + term
            edge_out[part, :, cols] = edge
    edge_copy = ring.copy(edge_out, edge_in, sems, 0, ring.place - 1)
    has_before, has_after = ring.place > 0, ring.place < ring.count - 1
    pl.when(has_before)(edge_copy.start)
    columns = jnp.concatenate(
        [g for g, _ in grad_cums] + grad_strengths + [jnp.zeros((size, 128 - 2 * heads), F32)], axis=1
    )
    rows = columns.T
    cum_rows = rows[0:heads] - jnp.concatenate([r for _, r in grad_cums], axis=0)
    padded = jnp.concatenate([cum_rows, jnp.zeros((8 - heads, size), F32)], axis=0)
    grad_logs = mm_exact(padded, tri(size, False))[0:heads]
    strength = sigmoid(gates_ref[0:heads, :])
    grad_gates_ref[0:heads, :] = rows[heads : 2 * heads] * strength * (1.0 - strength)
    by_rate = jnp.sum(grad_logs * scan.log_rows, axis=1, keepdims=True)
    slopes = []
    for h in range(heads):
        rate = jnp.exp(jnp.full((1, size), decay_ref[0, h], F32))
        slopes.append(-rate * sigmoid(gates_ref[heads + h : heads + h + 1, :] + decay_ref[1, h]))
    grad_bias = grad_logs * jnp.concatenate(slopes, axis=0)
    grad_gates_ref[heads : 2 * heads, :] = grad_bias
    by_bias = jnp.sum(grad_bias, axis=1, keepdims=True)
    grad_decay_ref[...] = jnp.concatenate(
        [by_rate, by_bias, jnp.zeros((heads, 126), F32)], axis=1
    )

    @pl.when(jnp.logical_not(has_after))
    def _():
        edge_in[...] = jnp.zeros_like(edge_in)

    pl.when(has_after)(edge_copy.wait_recv)
    for part in range(3):
        rows = jnp.concatenate(
            [last_rows[part, 0:8, :], last_rows[part, 8:16, :] + edge_in[part]], axis=0
        )
        grad_proj_ref[part, pl.ds(size - 16, 16), :] = rows.astype(BF)
    for c in range(CHUNKS):
        head_sum.share(c)
    for c in range(CHUNKS):
        head_sum.arrive(c)
    for r in range(0, size, 32):
        rows = pl.ds(r, 32)
        output_ref[rows, :] = middle_ref[rows, :] + head_sum.total[rows, :].astype(F32)
    by_gates_ref[...] = mm(grad_gates_ref[...], normed_ref[...])
    attn_copy.wait_recv()
    share_copy.start()
    for i in range(mine):
        local_copies[i].wait_send()
        pl.when(to_before)(chain_copies[i].wait_send)
        state_copies[i].wait_send()
    pl.when(has_before)(edge_copy.wait_send)
    attn_copy.wait_send()
    share_copy.wait()
    second_side.wait()
    tok_first.wait()
    head_copies.finish()


def recurrent_backward(first, decay, gates, proj, rim, convw, gain, grad_gated, saved, grad_held, mid_held, attn, normed, mlp, middle):
    heads = decay.shape[1]
    parts, size, width = proj.shape
    hdim = width // heads
    mine = heads // 2
    taps = convw.shape[1]
    shape = jax.ShapeDtypeStruct
    vm = pl.BlockSpec(memory_space=pltpu.VMEM)
    sm = pl.BlockSpec(memory_space=pltpu.SMEM)
    hbm = pl.BlockSpec(memory_space=pl.ANY)
    count = 5 + 3 * mine
    states = lambda count: pltpu.VMEM((count, hdim, hdim), BF)
    return pl.pallas_call(
        functools.partial(backward_kernel, heads),
        out_shape=(
            shape((4, size, width), BF), shape((3, taps, width), F32),
            shape((2 * heads, size), F32), shape((heads, 128), F32), shape((heads, hdim), F32),
            shape((grad_held.shape[1] // 2,) + grad_held.shape[2:], BF), shape((grad_held.shape[1] // 2,) + grad_held.shape[2:], BF),
            shape((attn.shape[0], attn.shape[1], size), BF), shape((2 * heads, normed.shape[1]), F32),
            shape(middle.shape, F32),
        ),
        in_specs=[sm, sm] + [vm] * 14 + [hbm, hbm, vm, vm, vm, vm],
        out_specs=(vm,) * 5 + (hbm, hbm, vm, vm, vm),
        scratch_shapes=[
            pltpu.VMEM((3, size + 8, width), F32), pltpu.VMEM((taps, size + 16, hdim), F32),
            pltpu.VMEM((heads, size, hdim), F32), states(heads), states(mine), states(mine), states(mine),
            states(mine), states(mine), states(heads),
            pltpu.VMEM((3, 8, width), F32), pltpu.VMEM((3, 8, width), F32), pltpu.VMEM((3, 16, width), F32),
            *HeadSum.scratch(*middle.shape),
            pltpu.SemaphoreType.DMA((3 * CHUNKS,)), pltpu.SemaphoreType.DMA((3 * CHUNKS,)),
            pltpu.SemaphoreType.DMA((count,)), pltpu.SemaphoreType.DMA((count,)),
        ],
        compiler_params=pltpu.CompilerParams(
            vmem_limit_bytes=34 << 20, collective_id=2, has_side_effects=True
        ),
        name="recurrent_backward",
    )(first, decay, gates, proj, rim, convw, gain, grad_gated, *saved, grad_held, mid_held, attn, normed, mlp, middle)


def middle_kernel(
    gated_ref, w_out_ref, inputs_ref, gains_ref, own_ref, far_ref, middle_ref, normed_ref, held_ref,
    part, sibling, kept, across_in, total, send_sems, recv_sems,
):
    cube = Cube()
    copies = Copies(send_sems, recv_sems)
    cube.greet([cube.beside(1), cube.beside(2)] + [cube.along(bit) for bit in cube.bits])
    for side in (0, 1):
        held_ref[side, 0] = own_ref[side]
        held_ref[side, 1] = far_ref[side]
    spread = Spread(cube, copies, held_ref)
    sums = HeadSum(cube, copies, part, sibling, kept, across_in, total, CHUNKS)
    for c in range(CHUNKS):
        part[:, sums.cols(c)] = mm(gated_ref[...], w_out_ref[:, sums.cols(c)]).astype(BF)
        if c == 0:
            cube.met(2 + len(cube.bits))
        sums.halve(c)
    spread.send(1)
    for c in range(CHUNKS):
        sums.cross(c)
    spread.take()
    spread.send(2)
    for c in range(CHUNKS):
        sums.share(c)
    for c in range(CHUNKS):
        sums.arrive(c)
    gain = gains_ref[1:2, :]
    for r in range(0, inputs_ref.shape[0], 32):
        rows = pl.ds(r, 32)
        middle = inputs_ref[rows, :] + total[rows, :].astype(F32)
        middle_ref[rows, :] = middle
        inverse = lax.rsqrt(jnp.mean(middle * middle, axis=1, keepdims=True) + EPS)
        normed_ref[rows, :] = (middle * inverse * gain).astype(BF)
    spread.take()
    for step in range(3, len(cube.bits) + 1):
        spread.send(step)
        spread.take()
    copies.finish()


def middle_of(gated, w_out, inputs, gains, own, far):
    size, features = inputs.shape
    owners = lax.axis_size("seq")
    count = 3 * CHUNKS + 2 * (owners.bit_length() - 2)
    shape = jax.ShapeDtypeStruct
    vm = pl.BlockSpec(memory_space=pltpu.VMEM)
    return pl.pallas_call(
        middle_kernel,
        out_shape=(
            shape((size, features), F32), shape((size, features), BF),
            shape((2, owners) + own.shape[1:], BF),
        ),
        in_specs=[vm] * 6,
        out_specs=(vm,) * 3,
        scratch_shapes=[pltpu.VMEM((size, features), BF)] + HeadSum.scratch(size, features) + [
            pltpu.SemaphoreType.DMA((count,)), pltpu.SemaphoreType.DMA((count,)),
        ],
        compiler_params=pltpu.CompilerParams(
            vmem_limit_bytes=40 << 20, collective_id=4, has_side_effects=True
        ),
        name="middle",
    )(gated, w_out, inputs, gains, own, far)


def by_half(cube, array, near, leaving):
    features = array.shape[1]
    kept = near.shape[1]
    half = cube.place // (cube.count // 2)
    span = leaving.shape[2]
    rows = pl.ds(pl.multiple_of(cube.head % 2 * span, span), span)
    width = features // 2
    mine = array[:, pl.ds(pl.multiple_of(half * width, width), width)]
    others = array[rows, pl.ds(pl.multiple_of((1 - half) * width, width), width)]
    for j in range(near.shape[0]):
        near[j] = mine[:, j * kept : (j + 1) * kept].T
        leaving[j] = others[:, j * kept : (j + 1) * kept].T


def middle_back_kernel(
    part_ref, middle_ref, cotangent_ref, gains_ref, w_out_ref, part_held_ref, normed_ref, grad_held_ref,
    grad_middle_ref, near_ref, leaving_ref, grad_gated_ref, grad_gain_ref, held_ref, normed_near_ref, normed_far_ref, grad_second_ref,
    grad_low, normed_leaving, sibling, kept, across_in, total, send_sems, recv_sems,
):
    cube = Cube()
    copies = Copies(send_sems, recv_sems)
    cube.greet([cube.mirror(), cube.beside(1), cube.beside(2)] + [cube.along(bit) for bit in cube.bits])
    held_ref[:, pl.ds(0, 4)] = part_held_ref[...]
    spread = Spread(cube, copies, held_ref)
    sums = HeadSum(cube, copies, part_ref, sibling, kept, across_in, total, CHUNKS)
    by_half(cube, normed_ref, normed_near_ref, normed_leaving)
    cube.met(3 + len(cube.bits))
    span = normed_leaving.shape[2]
    core_rows = normed_far_ref.at[:, :, pl.ds(pl.multiple_of(cube.head % 2 * span, span), span)]
    far_copy = copies.start(normed_leaving, core_rows, cube.mirror())
    spread.send(2)
    for c in range(CHUNKS):
        sums.halve(c)
    for c in range(CHUNKS):
        sums.cross(c)
    early = cube.count // 2
    side_copy = copies.start(grad_held_ref.at[1, pl.ds(0, early)], grad_second_ref, cube.beside(2))
    for c in range(CHUNKS):
        sums.share(c)
    for c in range(CHUNKS):
        sums.arrive(c)
    far_copy.wait_recv()
    share_copy = copies.start(core_rows, core_rows, cube.beside(1))
    grad_gain_ref[...] = norm_back(
        middle_ref, total, gains_ref[1:2, :], cotangent_ref, grad_middle_ref, grad_low
    )
    grad_gated_ref[...] = mm(grad_low[...], w_out_ref[...], 1, 1)
    by_half(cube, grad_low, near_ref, leaving_ref)
    spread.take()
    for step in range(3, len(cube.bits) + 1):
        spread.send(step)
        spread.take()
    share_copy.wait_recv()
    side_copy.wait_recv()
    copies.finish()


def norm_back(values_ref, grad_ref, gain, added_ref, out_ref, low_ref):
    gain_sum = None
    for r in range(0, values_ref.shape[0], 32):
        rows = pl.ds(r, 32)
        values = values_ref[rows, :]
        inverse = lax.rsqrt(jnp.mean(values * values, axis=1, keepdims=True) + EPS)
        grad = grad_ref[rows, :].astype(F32)
        scaled = grad * gain
        along = jnp.mean(values * scaled, axis=1, keepdims=True)
        out = added_ref[rows, :] + inverse * scaled - values * (inverse * inverse * inverse * along)
        out_ref[rows, :] = out
        if low_ref is not None:
            low_ref[rows, :] = out.astype(BF)
        here = jnp.sum(grad * (values * inverse), axis=0, keepdims=True)
        gain_sum = here if gain_sum is None else gain_sum + here
    return gain_sum


def middle_back(part, middle, cotangent, gains, w_out, held, normed, grad_held):
    size, features = middle.shape
    owners = lax.axis_size("seq")
    count = 3 + 3 * CHUNKS + 2 * (owners.bit_length() - 3)
    shape = jax.ShapeDtypeStruct
    hbm = pl.BlockSpec(memory_space=pl.ANY)
    by_owner = shape((owners // 2, features // owners, size), BF)
    vm = pl.BlockSpec(memory_space=pltpu.VMEM)
    return pl.pallas_call(
        middle_back_kernel,
        out_shape=(
            shape((size, features), F32), by_owner,
            shape((owners // 2, features // owners, size // 2), BF),
            shape((size, w_out.shape[0]), F32), shape((1, features), F32),
            shape((2, owners) + held.shape[2:], BF), by_owner, by_owner,
            shape((owners // 2,) + held.shape[2:], BF),
        ),
        in_specs=[vm] * 7 + [hbm],
        out_specs=(vm,) * 8 + (hbm,),
        scratch_shapes=[
            pltpu.VMEM((size, features), BF), pltpu.VMEM((owners // 2, features // owners, size // 2), BF),
        ] + HeadSum.scratch(size, features) + [
            pltpu.SemaphoreType.DMA((count,)), pltpu.SemaphoreType.DMA((count,)),
        ],
        compiler_params=pltpu.CompilerParams(
            vmem_limit_bytes=40 << 20, collective_id=5, has_side_effects=True
        ),
        name="middle_back",
    )(part, middle, cotangent, gains, w_out, held, normed, grad_held)


class Halving:
    def __init__(self, cube, copies, outgoing, incoming):
        self.cube, self.copies, self.outgoing, self.incoming = cube, copies, outgoing, incoming
        self.orders = (cube.bits, cube.bits[::-1])
        self.held = [None, None]
        self.step = [0, 0]
        self.slot = [0, 0]
        self.flying = [None, None]

    def begin(self, partials):
        for side in (0, 1):
            rows = partials[0].shape[0] // 2
            self.held[side] = {m: p[side * rows : (side + 1) * rows] for m, p in partials.items()}
            self.send(side)

    def send(self, side):
        bit = self.orders[side][self.step[side]]
        leaving = sorted(m for m in self.held[side] if m & bit)
        first = self.slot[side]
        for k, m in enumerate(leaving):
            self.outgoing[side, first + k] = self.held[side].pop(m).astype(BF)
        span = pl.ds(first, len(leaving))
        self.flying[side] = (
            self.copies.start(
                self.outgoing.at[side, span], self.incoming.at[side, span], self.cube.along(bit)
            ),
            first,
        )
        self.slot[side] += len(leaving)
        self.step[side] += 1

    def advance(self):
        for side in (0, 1):
            copy, first = self.flying[side]
            copy.wait_recv()
            for k, m in enumerate(sorted(self.held[side])):
                self.held[side][m] = self.held[side][m] + self.incoming[side, first + k].astype(F32)
            if self.step[side] < len(self.orders[side]):
                self.send(side)

    def result(self):
        return [self.held[side][0] for side in (0, 1)]


def ff_tile(tokens, grads, w_gate, w_up, w_down):
    gate = mm(tokens, w_gate)
    up = mm(tokens, w_up)
    grad = mm(grads, w_down, 1, 1)
    sig = sigmoid(gate)
    active = gate * sig
    hidden = (active * up).astype(BF)
    grad_gate = (grad * up * (sig * (1.0 + gate * (1.0 - sig)))).astype(BF)
    return hidden, grad_gate, (grad * active).astype(BF)


def near_kernel(
    tokens_ref, grads_ref, w_up_hbm, w_down_hbm, grad_held_ref, gated_ref,
    grad_ref, out_ref, held_ref, grad_first_ref, gated_far_ref, w_up_ref, w_down_ref, load_sems, send_sems, recv_sems,
):
    cube = Cube()
    units = w_down_ref.shape[0]
    loads = [
        pltpu.make_async_copy(source, target, load_sems.at[k])
        for k, (source, target) in enumerate(((w_up_hbm, w_up_ref), (w_down_hbm, w_down_ref)))
    ]
    for load in loads:
        load.start()
    copies = Copies(send_sems, recv_sems)
    cube.greet([cube.mirror(), cube.along(cube.bits[0]), cube.along(cube.bits[-1]), cube.beside(2)])
    rows = held_ref.shape[2]
    for side in (0, 1):
        first = pl.multiple_of((2 * cube.head + side) * rows, rows)
        held_ref[side, 0] = tokens_ref[pl.ds(first, rows), :]
    spread = Spread(cube, copies, held_ref)
    cube.met(4)
    spread.send(0)
    first_side = copies.start(grad_held_ref.at[0], grad_first_ref, cube.beside(2))
    gated_copy = copies.start(gated_ref, gated_far_ref, cube.mirror())
    for load in loads:
        load.wait()
    w_gate, w_up = w_up_ref[:, pl.ds(0, units)], w_up_ref[:, pl.ds(units, units)]
    hidden, grad_gate, grad_up = ff_tile(tokens_ref[...], grads_ref[...].astype(BF), w_gate, w_up, w_down_ref[...])
    spread.take()
    spread.send(1)
    grad_ref[...] = (mm(grad_gate, w_gate, 1, 1) + mm(grad_up, w_up, 1, 1)).astype(BF)
    out_ref[...] = mm(hidden, w_down_ref[...]).astype(BF)
    spread.take()
    gated_copy.wait_recv()
    first_side.wait_recv()
    copies.finish()


def near_part(tokens, grads, w_up, w_down, grad_held, gated):
    size, features = tokens.shape
    low = jax.ShapeDtypeStruct((size, features), BF)
    rows = size // (2 * lax.axis_size("head"))
    vm = pl.BlockSpec(memory_space=pltpu.VMEM)
    hbm = pl.BlockSpec(memory_space=pl.ANY)
    return pl.pallas_call(
        near_kernel,
        out_shape=(
            low, low, jax.ShapeDtypeStruct((2, 4, rows, features), BF),
            jax.ShapeDtypeStruct(grad_held.shape[1:], BF), jax.ShapeDtypeStruct(gated.shape, BF),
        ),
        in_specs=[vm, vm] + [hbm] * 4,
        out_specs=(vm,) * 3 + (hbm, hbm),
        scratch_shapes=[
            pltpu.VMEM(w_up.shape, BF), pltpu.VMEM(w_down.shape, BF), pltpu.SemaphoreType.DMA((2,)),
            pltpu.SemaphoreType.DMA((6,)), pltpu.SemaphoreType.DMA((6,)),
        ],
        compiler_params=pltpu.CompilerParams(
            vmem_limit_bytes=40 << 20, collective_id=6, has_side_effects=True
        ),
        name="feed_forward",
    )(tokens, grads, w_up, w_down, grad_held, gated)


def tail_kernel(
    near_ref, normed_half_ref, normed_far_ref, gated_ref, gated_far_ref, attn_half_ref, attn_far_ref,
    gates_ref, part_ref, inputs_hbm, gains_ref,
    middle_hbm, conv_ref, mid_gain_ref, decay_ref, head_gain_ref,
    tok_own_ref, grad_own_ref, tok_first_ref, grad_first_ref, grad_second_ref, grad_third_ref, w_up_hbm, w_down_hbm,
    grad_proj_ref, grad_wout_ref, grad_inputs_ref, grad_up_ref, grad_down_ref,
    by_gates_ref, by_conv_ref, by_gains_ref, by_head_ref, by_decay_ref,
    tok_sib_ref, grad_sib_ref, tok_across_ref, tok_both_ref, grad_both_ref,
    far, outgoing, incoming, sibling, kept, across_in, total, small_ref, small_out, small_in,
    w_up, w_down, blocks, spare, load_sems, block_sems, send_sems, recv_sems,
):
    cube = Cube()
    copies = Copies(send_sems, recv_sems)
    parts, size, width = near_ref.shape
    bits = len(cube.bits)
    loads = [
        pltpu.make_async_copy(source, target, load_sems.at[k])
        for k, (source, target) in enumerate(((w_up_hbm, w_up), (w_down_hbm, w_down)))
    ]
    middle_load = pltpu.make_async_copy(middle_hbm, grad_inputs_ref, load_sems.at[2])
    middle_load.start()
    inputs_ref = grad_proj_ref if grad_proj_ref.shape == inputs_hbm.shape else spare
    inputs_load = pltpu.make_async_copy(inputs_hbm, inputs_ref, load_sems.at[3])
    inputs_load.start()
    for load in loads:
        load.start()
    beside, across_way = cube.beside(1), cube.beside(2)
    cube.greet([cube.mirror(), beside, across_way] + [cube.along(bit) for bit in cube.bits])
    cube.met(3 + bits)
    order = (4, 3, 2, 1, 0)
    reduced = HeadSum(cube, copies, part_ref, sibling, kept, across_in, total, CHUNKS)
    for c in range(CHUNKS):
        reduced.halve(c)
    arriving = {c: copies.start(near_ref.at[c], far.at[c], cube.mirror()) for c in order[1:]}
    for c in range(CHUNKS):
        reduced.cross(c)
    arrivals = {
        ("sib", 0): copies.start(tok_own_ref, tok_sib_ref, beside),
        ("sib", 1): copies.start(grad_own_ref, grad_sib_ref, beside),
    }
    early = cube.count // 2
    sides = (pl.ds(early, cube.count - early), pl.ds(0, cube.count))
    for side, where in enumerate(sides):
        arrivals["across", side] = copies.start(
            tok_own_ref.at[side, where], tok_across_ref.at[side, where], across_way
        )
    done = set()

    def ready(*names):
        for name in names:
            if name not in done:
                done.add(name)
                arrivals[name].wait_recv()

    def share_grads():
        first, last = pl.ds(0, early), pl.ds(early, cube.count - early)
        arrivals["grads", 0] = copies.start(grad_first_ref, grad_both_ref.at[0], beside)
        arrivals["grads", 1] = copies.start(grad_second_ref, grad_both_ref.at[1, first], beside)
        arrivals["grads", 2] = copies.start(grad_third_ref, grad_both_ref.at[1, last], beside)
        arrivals["first", 0] = copies.start(tok_first_ref, tok_both_ref.at[0, first], beside)

    def forward(side):
        ready(("across", side))
        where = sides[side]
        arrivals["both", side] = copies.start(
            tok_across_ref.at[side, where], tok_both_ref.at[side, where], beside
        )

    sums = {}

    def partials(c):
        found = {}
        if c < parts:
            arriving[c].wait_recv()
        for m in cube.masks:
            within = cube.moved(m) % len(cube.masks)
            if c < parts:
                found[m] = mm(normed_half_ref[within], near_ref[c]) + mm(normed_far_ref[within], far[c])
            else:
                found[m] = mm(attn_half_ref[within], gated_ref[...]) + mm(attn_far_ref[within], gated_far_ref[...])
        sums[c] = Halving(cube, copies, outgoing.at[c], incoming.at[c])
        sums[c].begin(found)

    def store(c):
        for side, rows in enumerate(sums[c].result()):
            if c == parts:
                half = rows.shape[0]
                grad_wout_ref[:, side * half : (side + 1) * half] = rows.T
                continue
            grad_proj_ref[pl.ds(side * rows.shape[0], rows.shape[0]), pl.ds(c * width, width)] = rows

    left = {c: bits for c in order}

    def advance(c):
        if left[c]:
            sums[c].advance()
            left[c] -= 1
            if not left[c]:
                store(c)

    span = grad_up_ref.shape[0]
    stretch = blocks.shape[2]
    owner_rows = pl.ds(
        pl.multiple_of(cube.place * (w_up.shape[0] // cube.count) // span * span, span), span
    )
    units = w_down.shape[0]
    features = w_up.shape[0]
    pieces = cube.count // stretch

    def weights(tokens_of, grads_of, count):
        def fetch(k, slot):
            at = pl.ds(pl.multiple_of(k % pieces * stretch, stretch), stretch)
            return [
                pltpu.make_async_copy(
                    of(k // pieces).at[at], blocks.at[slot, which], block_sems.at[slot, which]
                )
                for which, of in enumerate((tokens_of, grads_of))
            ]

        for copy in fetch(0, 0):
            copy.start()

        def piece(k, carry):
            slot = k % 2
            for copy in fetch(k, slot):
                copy.wait()

            @pl.when(k + 1 < count * pieces)
            def _():
                for copy in fetch(k + 1, 1 - slot):
                    copy.start()

            accumulate(slot, False)
            return carry

        lax.fori_loop(0, count * pieces, piece, 0)

    def weights_across(tokens_of, grads_of):
        cuts = sorted({c for of in (tokens_of, grads_of) for _, _, first, rows in of for c in (first, first + rows)})
        if pieces == 1:
            made = []
            for which, of in enumerate((tokens_of, grads_of)):
                for k, (ref, start, first, rows) in enumerate(of):
                    copy = pltpu.make_async_copy(
                        ref.at[pl.ds(start, rows)], blocks.at[0, which, pl.ds(first, rows)],
                        block_sems.at[k, which],
                    )
                    copy.start()
                    made.append(copy)
            for copy in made:
                copy.wait()

            def once(k, carry):
                accumulate(0, False)
                return carry

            lax.fori_loop(0, 1, once, 0)
            return
        for low, high in zip(cuts[:-1], cuts[1:]):
            found = []
            for of in (tokens_of, grads_of):
                ref, start, first, _ = next(p for p in of if p[2] <= low < p[2] + p[3])
                found.append((ref, start + low - first))

            def piece(k, carry):
                made = [
                    pltpu.make_async_copy(
                        ref.at[pl.ds(pl.multiple_of(start + k * stretch, stretch), stretch)],
                        blocks.at[0, which], block_sems.at[0, which],
                    )
                    for which, (ref, start) in enumerate(found)
                ]
                for copy in made:
                    copy.start()
                for copy in made:
                    copy.wait()
                accumulate(0, False)
                return carry

            lax.fori_loop(0, (high - low) // stretch, piece, 0)

    def accumulate(slot, start):
        tokens = blocks[slot, 0].reshape(-1, features)
        grads = blocks[slot, 1].reshape(-1, features)
        own_tokens = blocks[slot, 0, :, :, owner_rows].reshape(-1, span)
        own_grads = blocks[slot, 1, :, :, owner_rows].reshape(-1, span)
        hidden, grad_gate, grad_up = ff_tile(
            tokens, grads, w_up[:, pl.ds(0, units)], w_up[:, pl.ds(units, units)], w_down[...]
        )
        found = (mm(own_tokens, grad_gate, 0, 0), mm(own_tokens, grad_up, 0, 0), mm(own_grads, hidden, 0, 0))
        targets = (
            (grad_up_ref, pl.ds(0, units)), (grad_up_ref, pl.ds(units, units)), (grad_down_ref, pl.ds(0, units))
        )
        for value, (target, cols) in zip(found, targets):
            if start:
                target[:, cols] = value
            else:
                target[:, cols] += value

    ways = [cube.along(bit) for bit in cube.bits] + [cube.mirror()]
    flights = []

    def small_send():
        step = len(flights)
        small_out[step] = small_ref[...].astype(BF)
        flights.append(copies.start(small_out.at[step], small_in.at[step], ways[step]))

    taken = []

    def small_take():
        step = len(taken)
        if step == len(ways):
            return
        taken.append(step)
        flights[step].wait_recv()
        small_ref[...] = small_out[step].astype(F32) + small_in[step].astype(F32)
        if step + 1 < len(ways):
            small_send()

    def share_sums():
        for c in range(CHUNKS):
            reduced.share(c)

    def inputs_back():
        for c in range(CHUNKS):
            reduced.arrive(c)
        gain = gains_ref[0:1, :]
        middle_load.wait()
        inputs_load.wait()
        gain_sum = norm_back(inputs_ref, total, gain, grad_inputs_ref, grad_inputs_ref, None)
        flat = [head_gain_ref[h : h + 1, :] for h in range(head_gain_ref.shape[0])]
        flat += [decay_ref[h : h + 1, :] for h in range(decay_ref.shape[0])]
        flat.append(jnp.zeros((1, gain.shape[1] - sum(f.shape[1] for f in flat)), F32))
        small_ref[...] = jnp.concatenate(
            [gates_ref[...], conv_ref[...], gain_sum, mid_gain_ref[...], jnp.concatenate(flat, axis=1),
             jnp.zeros((2, gain.shape[1]), F32)], axis=0
        )
        small_send()

    grad_up_ref[...] = jnp.zeros_like(grad_up_ref)
    grad_down_ref[...] = jnp.zeros_like(grad_down_ref)
    partials(order[0])
    for load in loads:
        load.wait()
    weights(lambda k: tok_own_ref.at[k], lambda k: grad_own_ref.at[k], 2)
    share_sums()
    partials(3)
    advance(4)
    ready(("sib", 0), ("sib", 1))
    weights(lambda k: tok_sib_ref.at[k], lambda k: grad_sib_ref.at[k], 2)
    inputs_back()
    share_grads()
    advance(4)
    advance(3)
    partials(2)
    forward(0)
    every = cube.count
    weights_across(
        [(tok_first_ref, 0, 0, early), (tok_across_ref.at[0], early, early, every - early)],
        [(grad_first_ref, 0, 0, every)],
    )
    small_take()
    advance(3)
    advance(2)
    partials(1)
    ready(("grads", 0), ("first", 0), ("both", 0))
    weights_across([(tok_both_ref.at[0], 0, 0, every)], [(grad_both_ref.at[0], 0, 0, every)])
    small_take()
    advance(2)
    advance(1)
    partials(0)
    forward(1)
    weights_across(
        [(tok_across_ref.at[1], 0, 0, every)],
        [(grad_second_ref, 0, 0, early), (grad_third_ref, 0, early, every - early)],
    )
    small_take()
    advance(1)
    advance(0)
    ready(("both", 1), ("grads", 1), ("grads", 2))
    weights_across([(tok_both_ref.at[1], 0, 0, every)], [(grad_both_ref.at[1], 0, 0, every)])
    for step in range(len(ways)):
        small_take()
    heads, hdim = by_head_ref.shape
    for i in (0, 1):
        by_gates_ref[i] = small_ref[i * heads : (i + 1) * heads, :]
    conv_taps = by_conv_ref.shape[1]
    for p in range(3):
        for t in range(conv_taps):
            by_conv_ref[p, t : t + 1, :] = small_ref[2 * heads + p : 2 * heads + p + 1, t * width : (t + 1) * width]
    by_gains_ref[...] = small_ref[2 * heads + 3 : 2 * heads + 5, :]
    last = small_ref[2 * heads + 5 : 2 * heads + 6, :]
    for h in range(heads):
        by_head_ref[h : h + 1, :] = last[:, h * hdim : (h + 1) * hdim]
        at = heads * hdim + h * LANES
        by_decay_ref[h : h + 1, :] = last[:, at : at + LANES]
    for step in range(bits):
        for c in order:
            advance(c)
    copies.finish()


def tail(
    near, normed_half, normed_far, gated, gated_far, attn_half, attn_far, gates, part, inputs, gains,
    middle, conv, mid_gain, decay, head_gain, tok_own, grad_own, tok_first, grad_first, grad_second, grad_third, w_up, w_down,
):
    parts, size, width = near.shape
    owners = lax.axis_size("seq")
    bits = owners.bit_length() - 2
    slots = owners // 2 - 1
    kept = normed_half.shape[1]
    span = max(kept, LANES)
    features = inputs.shape[1]
    stretch = 8
    heads = head_gain.shape[0]
    taps = conv.shape[1] // width
    shape = jax.ShapeDtypeStruct
    vm = pl.BlockSpec(memory_space=pltpu.VMEM)
    hbm = pl.BlockSpec(memory_space=pl.ANY)
    copies = parts + 3 * CHUNKS + bits + 1 + (parts + 1) * 2 * bits + 10
    flying = pltpu.VMEM((parts + 1, 2, slots, kept // 2, width), BF)
    held = shape(tok_own.shape, BF)
    spare = pltpu.VMEM((8, LANES) if (kept, parts * width) == inputs.shape else inputs.shape, F32)
    found = pl.pallas_call(
        tail_kernel,
        out_shape=(
            shape((kept, parts * width), F32), shape((width, kept), F32), shape((size, features), F32),
            shape((span, w_up.shape[1]), F32), shape((span, w_down.shape[0]), F32),
            shape((2, heads, features), F32), shape((3, taps, width), F32), shape((2, features), F32),
            shape(head_gain.shape, F32), shape(decay.shape, F32),
            held, held, held, held, held,
        ),
        in_specs=[vm] * 9 + [hbm, vm, hbm] + [vm] * 4 + [hbm] * 8,
        out_specs=(vm,) * 10 + (hbm,) * 5,
        scratch_shapes=[
            pltpu.VMEM((parts, size, width), BF), flying, flying, *HeadSum.scratch(size, features),
            pltpu.VMEM((16, features), F32),
            pltpu.VMEM((bits + 1, 16, features), BF), pltpu.VMEM((bits + 1, 16, features), BF),
            pltpu.VMEM(w_up.shape, BF), pltpu.VMEM(w_down.shape, BF),
            pltpu.VMEM((2, 2, stretch) + tok_own.shape[2:], BF),
            spare, pltpu.SemaphoreType.DMA((4,)), pltpu.SemaphoreType.DMA((2, 2)),
            pltpu.SemaphoreType.DMA((copies,)), pltpu.SemaphoreType.DMA((copies,)),
        ],
        compiler_params=pltpu.CompilerParams(
            vmem_limit_bytes=63 << 20, collective_id=3, has_side_effects=True
        ),
        name="tail",
    )(
        near, normed_half, normed_far, gated, gated_far, attn_half, attn_far, gates, part, inputs, gains,
        middle, conv, mid_gain, decay, head_gain, tok_own, grad_own, tok_first, grad_first, grad_second, grad_third, w_up, w_down,
    )
    return found[:10]


def rms_scale(values, gain):
    return values * lax.rsqrt(jnp.mean(values * values, axis=-1, keepdims=True) + EPS) * gain


def shards(
    inputs,
    gains,
    w_proj,
    w_gates,
    decay,
    conv_w,
    head_gain,
    w_out,
    w_up,
    w_down,
    seq_first,
    cotangent,
):
    tokens = inputs.shape[0]
    heads_here = decay.shape[1]
    owners = lax.axis_size("seq")
    place = lax.axis_index("seq")
    kept = inputs.shape[1] // owners

    normed_low = rms_scale(inputs, gains[0]).astype(BF)
    w_up_flat = w_up.reshape(w_up.shape[0], -1)
    projected = jnp.einsum("td,dkc->ktc", normed_low, w_proj, preferred_element_type=F32)
    gate_in = jnp.einsum("td,idh->iht", normed_low, w_gates, preferred_element_type=F32)
    gate_in = gate_in.reshape(2 * heads_here, tokens)
    (
        gated_low, recurrent, lift, inverse, solved, gram, score, state, pair, rim, grad_own, grad_far
    ) = recurrent_forward(seq_first, decay, gate_in, projected, conv_w, head_gain, cotangent)
    middle, normed_mid_low, grad_held = middle_of(gated_low, w_out, inputs, gains, grad_own, grad_far)
    grad_mid_part, mlp_part, mid_part_held, grad_first, gated_far = near_part(
        normed_mid_low, cotangent, w_up_flat, w_down, grad_held, gated_low
    )
    grad_middle, attn_near, attn_leaving, grad_gated, grad_gain_mid, mid_held, normed_near, normed_far, grad_second = middle_back(
        grad_mid_part, middle, cotangent, gains, w_out, mid_part_held, normed_low, grad_held
    )
    (
        grad_projected, grad_conv, grad_gate_in, grad_decay, grad_head_gain, grad_third, tok_first, attn_far, by_gates,
        output,
    ) = recurrent_backward(
        seq_first, decay, gate_in, projected, rim, conv_w, head_gain, grad_gated,
        (recurrent, lift, inverse, solved, gram, score, state, pair), grad_held, mid_held, attn_leaving, normed_low,
        mlp_part, middle,
    )
    grad_gate_low = grad_gate_in.astype(BF)
    grad_normed_part = jnp.einsum("ktc,dkc->td", grad_projected, w_proj, preferred_element_type=F32)
    grad_normed_part = grad_normed_part + jnp.einsum(
        "iht,idh->td", grad_gate_low.reshape(2, heads_here, tokens), w_gates, preferred_element_type=F32
    )
    (
        grad_proj_part, grad_wout_part, grad_inputs, grad_up_part, grad_down_part,
        grad_wgates, grad_conv, grad_gains, grad_head_gain, grad_decay,
    ) = tail(
        grad_projected, normed_near, normed_far, gated_low, gated_far, attn_near, attn_far, by_gates,
        grad_normed_part.astype(BF), inputs, gains, grad_middle,
        grad_conv.reshape(3, -1), grad_gain_mid, grad_decay, grad_head_gain,
        mid_held, grad_held, tok_first, grad_first, grad_second, grad_third, w_up_flat, w_down,
    )
    grad_proj_part = grad_proj_part.reshape(kept, 4, -1)
    grad_wgates = jnp.swapaxes(grad_wgates, 1, 2)
    grad_decay = grad_decay[:, :2].T
    first = place * kept % grad_up_part.shape[0]
    grad_up_part = lax.dynamic_slice_in_dim(grad_up_part, first, kept, 0).reshape(kept, 2, -1)
    grad_down_part = lax.dynamic_slice_in_dim(grad_down_part, first, kept, 0).T
    return (
        output,
        grad_inputs,
        grad_gains,
        grad_proj_part,
        grad_wgates,
        grad_decay,
        grad_conv,
        grad_head_gain,
        grad_wout_part,
        grad_up_part,
        grad_down_part,
    )


def solution(mesh):
    placed = (
        P("seq", None),
        P(),
        P(None, None, "head"),
        P(None, None, "head"),
        P(None, "head"),
        P(None, None, "head"),
        P("head", None),
        P("head", None),
        P(None, None, "head"),
        P("head", None),
        P("seq"),
        P("seq", None),
    )
    return jax.shard_map(
        shards,
        mesh=mesh,
        in_specs=placed,
        out_specs=(
            P("seq", None),
            P("seq", None),
            P(),
            P("seq", None, "head"),
            P(None, None, "head"),
            P(None, "head"),
            P(None, None, "head"),
            P("head", None),
            P("head", "seq"),
            P("seq", None, "head"),
            P("head", "seq"),
        ),
        check_vma=False,
    )
```

```python
import functools

import jax
import jax.numpy as jnp
from jax import lax
from jax.experimental import pallas as pl
from jax.experimental.pallas import tpu as pltpu
from jax.sharding import PartitionSpec as P

EPS = 1e-06
GROUP = 64
BF = jnp.bfloat16
F32 = jnp.float32


def mm(a, b, ca=1, cb=0):
    return lax.dot_general(
        a.astype(BF), b.astype(BF), (((ca,), (cb,)), ((), ())), preferred_element_type=F32
    )


def split(a):
    high = a.astype(BF)
    return high, (a - high.astype(F32)).astype(BF)


def mm3(a, b, ca=1, cb=0):
    ah, al = split(a)
    bh, bl = split(b)
    return mm(ah, bh, ca, cb) + (mm(ah, bl, ca, cb) + mm(al, bh, ca, cb))


def mm_exact(a, b):
    return lax.dot_general(
        a, b, (((1,), (0,)), ((), ())), preferred_element_type=F32, precision=lax.Precision.HIGHEST
    )


def sigmoid(v):
    return 1.0 / (1.0 + jnp.exp(-v))


def softplus(v):
    return jnp.maximum(v, 0.0) + jnp.log1p(jnp.exp(-jnp.abs(v)))


def block_sums(first_ref, shape, axis):
    block = lax.broadcasted_iota(jnp.int32, shape, axis) // GROUP
    seen = jnp.zeros(shape, F32)
    starts = jnp.zeros(shape, F32)
    for b in range(first_ref.shape[0]):
        flag = first_ref[b].astype(F32)
        seen = seen + jnp.where(block >= b, flag, 0.0)
        starts = starts + jnp.where(block == b, flag, 0.0)
    return seen, starts


def gate_rows(gates_ref, decay_ref, heads):
    rows = []
    size = gates_ref.shape[1]
    for h in range(heads):
        rate = jnp.exp(jnp.full((1, size), decay_ref[0, h], F32))
        bias = decay_ref[1, h]
        rows.append(-rate * softplus(gates_ref[heads + h : heads + h + 1, :] + bias))
    return jnp.concatenate(rows, axis=0)


def tap_keeps(starts, taps):
    size = starts.shape[0]
    offset = lax.broadcasted_iota(jnp.int32, (size, 1), 0) % GROUP
    return [1.0 - jnp.where(offset < taps - 1 - j, starts, 0.0) for j in range(taps)]


def convolved(ext_ref, part, cols, convw_ref, keeps):
    size = ext_ref.shape[1] - 8
    taps = len(keeps)
    total = None
    for j in range(taps):
        shifted = ext_ref[part, pl.ds(8 - (taps - 1) + j, size), cols]
        if j < taps - 1:
            shifted = shifted * keeps[j]
        term = shifted * convw_ref[part, j : j + 1, cols]
        total = term if total is None else total + term
    return total


def fade_of(cum_col, cum_row, seen_col, seen_row):
    size = cum_col.shape[0]
    row = lax.broadcasted_iota(jnp.int32, (size, size), 0)
    col = lax.broadcasted_iota(jnp.int32, (size, size), 1)
    inside = (row > col) & (seen_col == seen_row)
    fade = jnp.where(inside, jnp.exp(jnp.minimum(cum_col - cum_row, 0.0)), 0.0)
    return jnp.where(row == col, 1.0, fade), inside


def fill_ext(ext, proj_ref, rim_ref):
    size = proj_ref.shape[1]
    for part in range(3):
        ext[part, pl.ds(0, 8), :] = rim_ref[part]
        ext[part, pl.ds(8, size), :] = proj_ref[part].astype(BF).astype(F32)


def tri(size, upper):
    row = lax.broadcasted_iota(jnp.int32, (size, size), 0)
    col = lax.broadcasted_iota(jnp.int32, (size, size), 1)
    return jnp.where((row <= col) if upper else (row >= col), 1.0, 0.0).astype(F32)


class Scan:
    def __init__(self, first_ref, decay_ref, gates_ref, heads):
        size = gates_ref.shape[1]
        self.log_rows = gate_rows(gates_ref, decay_ref, heads)
        self.seen_row, _ = block_sums(first_ref, (1, size), 1)
        self.seen_col, self.starts = block_sums(first_ref, (size, 1), 0)
        padded = jnp.concatenate([self.log_rows, jnp.zeros((8 - heads, size), F32)], axis=0)
        self.cum_rows = mm_exact(padded, tri(size, True))
        strength_rows = sigmoid(gates_ref[0:heads, :])
        both = jnp.concatenate([self.cum_rows[0:heads], strength_rows], axis=0)
        both = jnp.concatenate([both, jnp.zeros((128 - 2 * heads, size), F32)], axis=0)
        cols = both.T
        self.cum_cols = [cols[:, h : h + 1] for h in range(heads)]
        self.strength = [cols[:, heads + h : heads + h + 1] for h in range(heads)]

    def of(self, h):
        cum_col, cum_row = self.cum_cols[h], self.cum_rows[h : h + 1, :]
        size = cum_col.shape[0]
        last = cum_col[size - 1 : size, :]
        fade, inside = fade_of(cum_col, cum_row, self.seen_col, self.seen_row)
        growth = jnp.where(self.seen_col == 0.0, jnp.exp(cum_col), 0.0)
        last_seen = self.seen_col[size - 1 : size, :]
        to_end = jnp.where(self.seen_col == last_seen, jnp.exp(jnp.minimum(last - cum_col, 0.0)), 0.0)
        carry = jnp.where(last_seen == 0.0, jnp.exp(last), 0.0)
        return fade, inside, growth, to_end, carry


def unit(a, scale):
    inverse = lax.rsqrt(jnp.sum(a * a, axis=1, keepdims=True) + EPS)
    return a * (inverse * scale), inverse


MESH = pl.DeviceIdType.MESH


class Ring:
    def __init__(self):
        self.count = lax.axis_size("seq")
        self.place = lax.axis_index("seq")
        self.head = lax.axis_index("head")
        self.side = self.place % 2
        self.pair = self.place // 2
        self.pairs = self.count // 2
        self.partner = self.place + 1 - 2 * self.side
        self.cross = self.place + 2 * self.side - 1
        self.mirror = self.count - 2 - self.place + 2 * self.side
        self.sibling = self.head + 1 - 2 * (self.head % 2)

    def device(self, place):
        return (place, self.head)

    def across(self):
        return (self.place, (self.head + 2) % lax.axis_size("head"))

    def across_copy(self, source, target, sems, index):
        return pltpu.make_async_remote_copy(
            src_ref=source, dst_ref=target, send_sem=sems[0].at[index], recv_sem=sems[1].at[index],
            device_id=self.across(), device_id_type=MESH,
        )

    def greet(self, mirror=False, across=False, sibling=False):
        barrier = pltpu.get_barrier_semaphore()

        def tell(place):
            pl.semaphore_signal(barrier, inc=1, device_id=self.device(place), device_id_type=MESH)

        tell(self.partner)
        if mirror:
            tell(self.mirror)
        if across:
            pl.semaphore_signal(barrier, inc=1, device_id=self.across(), device_id_type=MESH)
        if sibling:
            pl.semaphore_signal(barrier, inc=1, device_id=(self.place, self.sibling), device_id_type=MESH)
        for place in (self.place - 2, self.place + 2, self.cross):
            pl.when((place >= 0) & (place < self.count))(functools.partial(tell, place))

    def met(self, mirror=False, across=False, sibling=False):
        inside = lambda place: jnp.where((place >= 0) & (place < self.count), 1, 0)
        known = inside(self.place - 2) + inside(self.place + 2) + inside(self.cross)
        always = 1 + int(mirror) + int(across) + int(sibling)
        pl.semaphore_wait(pltpu.get_barrier_semaphore(), known + always)

    def copy(self, source, target, sems, index, place):
        return pltpu.make_async_remote_copy(
            src_ref=source, dst_ref=target, send_sem=sems[0].at[index], recv_sem=sems[1].at[index],
            device_id=self.device(place), device_id_type=MESH,
        )


def forward_kernel(
    heads, first_ref, decay_ref, gates_ref, proj_ref, convw_ref, gain_ref, cotangent_ref,
    gated_ref, rec_ref, lift_ref, inv_ref, solved_ref, gram_ref, score_ref, state_ref, pair_ref, rim_ref, own_ref, far_ref,
    ext, base, maps, other, chain_in, chain_out, state_out, state_in, rim_out, rim_in, send_sems, recv_sems,
):
    ring = Ring()
    ring.greet(True)
    sems = (send_sems, recv_sems)
    size = proj_ref.shape[1]
    hdim = proj_ref.shape[2] // heads
    taps = convw_ref.shape[1]
    mine = heads // 2
    for part in range(3):
        rows = proj_ref[part].astype(BF).astype(F32)
        ext[part, pl.ds(8, size), :] = rows
        rim_out[part] = rows[size - 8 :, :]
    share = own_ref.shape[0] * own_ref.shape[1]
    share_rows = pl.ds(pl.multiple_of(ring.head * share, share), share)
    own_ref[...] = cotangent_ref[share_rows, :].astype(BF).reshape(own_ref.shape)
    scan = Scan(first_ref, decay_ref, gates_ref, heads)
    ring.met(True)
    has_before, has_after = ring.place > 0, ring.place < ring.count - 1
    rim_copy = ring.copy(rim_out, rim_in, sems, 0, ring.place + 1)
    pl.when(has_after)(rim_copy.start)
    far_copy = ring.copy(own_ref, far_ref, sems, 1 + 3 * mine, ring.mirror)
    far_copy.start()

    @pl.when(ring.place == 0)
    def _():
        rim_in[...] = jnp.zeros_like(rim_in)

    keeps = tap_keeps(scan.starts, taps)
    eye = lax.broadcasted_iota(jnp.int32, (size, size), 0) == lax.broadcasted_iota(
        jnp.int32, (size, size), 1
    )
    apart = lax.broadcasted_iota(jnp.int32, (size, size), 0) ^ lax.broadcasted_iota(
        jnp.int32, (size, size), 1
    )
    pl.when(has_before)(rim_copy.wait_recv)
    for part in range(3):
        ext[part, pl.ds(0, 8), :] = rim_in[part]
        rim_ref[part] = rim_in[part]
    held = []
    for h in range(heads):
        cols = pl.ds(h * hdim, hdim)
        acts = []
        for part in range(3):
            u = convolved(ext, part, cols, convw_ref, keeps)
            acts.append(u * sigmoid(u))
        q, _ = unit(acts[0], hdim ** -0.5)
        k, _ = unit(acts[1], 1.0)
        v = acts[2]
        fade, inside, growth, to_end, carry = scan.of(h)
        beta = scan.strength[h]
        gram = mm(k, k, 1, 1) * jnp.where(inside, fade, 0.0)
        score = mm(q, k, 1, 1) * fade
        gram_ref[h] = gram.astype(BF)
        score_ref[h] = score.astype(BF)
        system = beta * gram
        held.append((q, k, v, growth, to_end, carry, beta, system))
    inverses = [jnp.where(eye, 1.0, 0.0) - jnp.where(apart == 1, t[7], 0.0) for t in held]
    block = 2
    while block < size:
        level = (apart >= block) & (apart < 2 * block)
        inner = [mm(jnp.where(level, t[7], 0.0), inv) for t, inv in zip(held, inverses)]
        inverses = [inv - mm(inv, y) for inv, y in zip(inverses, inner)]
        block *= 2
    left = [jnp.where(eye, 1.0, 0.0) - inv - mm3(t[7], inv) for t, inv in zip(held, inverses)]
    inverses = [inv + mm(inv, r) for inv, r in zip(inverses, left)]
    for h in range(heads):
        q, k, v, growth, to_end, carry, beta, system = held[h]
        inv = inverses[h].astype(BF)
        inv_ref[h] = inv
        right = jnp.concatenate([beta * growth * k, beta * v], axis=1)
        solved = mm(inv, right).astype(BF)
        solved_ref[h] = solved
        ends = mm(k * to_end, solved, 0, 0)
        factor = jnp.where(eye[:hdim, :hdim], carry, 0.0) - ends[:, :hdim]
        maps[h] = jnp.concatenate([factor, ends[:, hdim:]], axis=1).astype(BF)
    map_copies = [
        ring.copy(maps.at[(1 - ring.side) * mine + i], other.at[i], sems, 1 + i, ring.partner)
        for i in range(mine)
    ]
    for copy in map_copies:
        copy.start()
    for h in range(heads):
        q, k, v, growth, to_end, carry, beta, system = held[h]
        mixed = mm(score_ref[h], solved_ref[h])
        lift_ref[h] = (q * growth - mixed[:, :hdim]).astype(BF)
        base[h] = mixed[:, hdim:]
    chain_copies = [
        ring.copy(chain_out.at[i], chain_in.at[i], sems, 1 + mine + i, ring.place + 2) for i in range(mine)
    ]
    state_copies = [
        ring.copy(state_out.at[i], state_in.at[i], sems, 1 + 2 * mine + i, ring.partner) for i in range(mine)
    ]
    from_before, to_after = ring.pair > 0, ring.pair < ring.pairs - 1

    @pl.when(jnp.logical_not(from_before))
    def _():
        chain_in[...] = jnp.zeros_like(chain_in)

    whole, before = [], []
    for i in range(mine):
        map_copies[i].wait_recv()
        own, far = maps[ring.side * mine + i], other[i]
        early = jnp.where(ring.side == 0, own, far)
        late = jnp.where(ring.side == 0, far, own)
        both = mm(late[:, :hdim], early)
        whole.append((both[:, :hdim].astype(BF), both[:, hdim:] + late[:, hdim:].astype(F32)))
        before.append(early)
        pair_ref[0, i] = early[:, :hdim]
        pair_ref[1, i] = late[:, :hdim]
        pair_ref[2, i] = whole[i][0]
    for i in range(mine):
        pl.when(from_before)(chain_copies[i].wait_recv)
        chain_out[i] = (mm(whole[i][0], chain_in[i]) + whole[i][1]).astype(BF)
        pl.when(to_after)(chain_copies[i].start)
    for i in range(mine):
        first = chain_in[i]
        second = (mm(before[i][:, :hdim], first) + before[i][:, hdim:].astype(F32)).astype(BF)
        state_out[i] = jnp.where(ring.side == 0, second, first)
        state_copies[i].start()
        state_ref[ring.side * mine + i] = jnp.where(ring.side == 0, first, second)
    for i in range(mine):
        state_copies[i].wait_recv()
        state_ref[(1 - ring.side) * mine + i] = state_in[i]
    for h in range(heads):
        cols = pl.ds(h * hdim, hdim)
        rec = mm(lift_ref[h], state_ref[h]) + base[h]
        rec_ref[h] = rec
        inverse = lax.rsqrt(jnp.mean(rec * rec, axis=1, keepdims=True) + EPS)
        gate = proj_ref[3, :, cols]
        gated_ref[:, cols] = (
            rec * inverse * gain_ref[h : h + 1, :] * (gate * sigmoid(gate))
        ).astype(BF)
    pl.when(has_after)(rim_copy.wait_send)
    for i in range(mine):
        map_copies[i].wait_send()
        pl.when(to_after)(chain_copies[i].wait_send)
        state_copies[i].wait_send()
    far_copy.wait()


def recurrent_forward(first, decay, gates, proj, convw, gain, cotangent):
    heads = decay.shape[1]
    parts, size, width = proj.shape
    hdim = width // heads
    mine = heads // 2
    shape = jax.ShapeDtypeStruct
    vm = pl.BlockSpec(memory_space=pltpu.VMEM)
    sm = pl.BlockSpec(memory_space=pltpu.SMEM)
    square = shape((heads, size, size), BF)
    share = shape((2, size // (2 * lax.axis_size("head")), cotangent.shape[1]), BF)
    count = 2 + 3 * mine
    states = lambda count: pltpu.VMEM((count, hdim, hdim), BF)
    return pl.pallas_call(
        functools.partial(forward_kernel, heads),
        out_shape=(
            shape((size, width), BF), shape((heads, size, hdim), F32), shape((heads, size, hdim), BF),
            square, shape((heads, size, 2 * hdim), BF), square, square,
            shape((heads, hdim, hdim), BF), shape((3, mine, hdim, hdim), BF), shape((3, 8, width), F32),
            share, share,
        ),
        in_specs=[sm, sm, vm, vm, vm, vm, vm],
        out_specs=(vm,) * 12,
        scratch_shapes=[
            pltpu.VMEM((3, size + 8, width), F32), pltpu.VMEM((heads, size, hdim), F32),
            pltpu.VMEM((heads, hdim, 2 * hdim), BF), pltpu.VMEM((mine, hdim, 2 * hdim), BF),
            states(mine), states(mine), states(mine), states(mine),
            pltpu.VMEM((3, 8, width), F32), pltpu.VMEM((3, 8, width), F32),
            pltpu.SemaphoreType.DMA((count,)), pltpu.SemaphoreType.DMA((count,)),
        ],
        compiler_params=pltpu.CompilerParams(
            vmem_limit_bytes=56 << 20, collective_id=1, has_side_effects=True
        ),
        name="recurrent_forward",
    )(first, decay, gates, proj, convw, gain, cotangent)


class Cube:
    def __init__(self):
        self.count = lax.axis_size("seq")
        self.place = lax.axis_index("seq")
        self.head = lax.axis_index("head")
        self.bits = []
        bit = 1
        while bit < self.count // 2:
            self.bits.append(bit)
            bit *= 2
        self.masks = range(self.count // 2)

    def moved(self, mask, of=None):
        place = self.place if of is None else of
        bit = 1
        while bit <= mask:
            if mask & bit:
                place = place + bit - 2 * bit * ((place // bit) % 2)
            bit *= 2
        return place

    def along(self, mask):
        return (self.moved(mask), self.head)

    def mirror(self):
        return self.along(self.count - 2)

    def beside(self, bit):
        return (self.place, self.moved(bit, self.head))

    def greet(self, devices):
        barrier = pltpu.get_barrier_semaphore()
        for device in devices:
            pl.semaphore_signal(barrier, inc=1, device_id=device, device_id_type=MESH)

    def met(self, count):
        pl.semaphore_wait(pltpu.get_barrier_semaphore(), count)


class Copies:
    def __init__(self, send_sems, recv_sems):
        self.sems = (send_sems, recv_sems)
        self.made = []

    def start(self, source, target, device):
        index = len(self.made)
        copy = pltpu.make_async_remote_copy(
            src_ref=source, dst_ref=target, send_sem=self.sems[0].at[index],
            recv_sem=self.sems[1].at[index], device_id=device, device_id_type=MESH,
        )
        copy.start()
        self.made.append(copy)
        return copy

    def finish(self):
        for copy in self.made:
            copy.wait_send()


LANES = 128


class Spread:
    def __init__(self, cube, copies, held):
        self.cube, self.copies, self.held = cube, copies, held
        self.ways = (
            [cube.mirror()] + [cube.along(bit) for bit in cube.bits],
            [cube.mirror()] + [cube.along(bit) for bit in cube.bits[::-1]],
        )
        self.flights = []

    def send(self, step):
        count = 1 << step
        self.flights = [
            self.copies.start(
                self.held.at[side, pl.ds(0, count)], self.held.at[side, pl.ds(count, count)],
                self.ways[side][step],
            )
            for side in (0, 1)
        ]

    def take(self):
        for copy in self.flights:
            copy.wait_recv()


class HeadSum:
    def __init__(self, cube, copies, part, sibling, kept, across_in, total, chunks):
        self.cube, self.copies, self.chunks = cube, copies, chunks
        self.part, self.sibling, self.kept, self.across_in, self.total = (
            part, sibling, kept, across_in, total,
        )
        size, width = part.shape
        self.span, self.width = size // 2, width // chunks
        low = cube.head % 2
        self.own = pl.ds(pl.multiple_of(low * self.span, self.span), self.span)
        self.other = pl.ds(pl.multiple_of((1 - low) * self.span, self.span), self.span)
        self.flights = {}

    def cols(self, c):
        return pl.ds(c * self.width, self.width)

    def halve(self, c):
        cols = self.cols(c)
        self.flights[c] = self.copies.start(
            self.part.at[self.other, cols], self.sibling.at[:, cols], self.cube.beside(1)
        )

    def cross(self, c):
        cols = self.cols(c)
        self.flights[c].wait_recv()
        self.kept[:, cols] = (
            self.part[self.own, cols].astype(F32) + self.sibling[:, cols].astype(F32)
        ).astype(BF)
        self.flights[c] = self.copies.start(
            self.kept.at[:, cols], self.across_in.at[:, cols], self.cube.beside(2)
        )

    def share(self, c):
        cols = self.cols(c)
        self.flights[c].wait_recv()
        self.total[self.own, cols] = (
            self.kept[:, cols].astype(F32) + self.across_in[:, cols].astype(F32)
        ).astype(BF)
        rows = self.total.at[self.own, cols]
        self.flights[c] = self.copies.start(rows, rows, self.cube.beside(1))

    def arrive(self, c):
        self.flights[c].wait_recv()

    @staticmethod
    def scratch(size, width):
        half = pltpu.VMEM((size // 2, width), BF)
        return [half, half, half, pltpu.VMEM((size, width), BF)]


CHUNKS = 4


def unit_back(a, inverse, scale, grad):
    along = jnp.sum(a * grad, axis=1, keepdims=True)
    return scale * (inverse * grad - a * (inverse * inverse * inverse * along))


def backward_kernel(
    heads, first_ref, decay_ref, gates_ref, proj_ref, rim_ref, convw_ref,
    gain_ref, grad_gated_ref, rec_ref, lift_ref, inv_ref, solved_ref, gram_ref, score_ref, state_ref, pair_ref, grad_held_ref, attn_ref, normed_ref, mlp_ref, middle_ref,
    grad_proj_ref, grad_convw_ref, grad_gates_ref, grad_decay_ref, grad_gain_ref, grad_second_ref, attn_far_ref, by_gates_ref, output_ref,
    ext, back, grad_rec, local, other, chain_in, chain_out, state_out, state_in, grad_end_all,
    edge_out, edge_in, last_rows, sibling, kept, across_in, total, head_send, head_recv, send_sems, recv_sems,
):
    ring = Ring()
    ring.greet(mirror=True, across=True, sibling=True)
    sems = (send_sems, recv_sems)
    mine = heads // 2
    size = proj_ref.shape[1]
    hdim = proj_ref.shape[2] // heads
    taps = convw_ref.shape[1]
    for h in range(heads):
        cols = pl.ds(h * hdim, hdim)
        rec = rec_ref[h]
        inverse = lax.rsqrt(jnp.mean(rec * rec, axis=1, keepdims=True) + EPS)
        gate = proj_ref[3, :, cols]
        sig = sigmoid(gate)
        gain = gain_ref[h : h + 1, :]
        normed = rec * inverse
        grad_gated = grad_gated_ref[:, cols]
        by_normed = grad_gated * normed
        grad_proj_ref[3, :, cols] = (
            by_normed * gain * (sig * (1.0 + gate * (1.0 - sig)))
        ).astype(BF)
        active = gate * sig
        grad_gain_ref[h : h + 1, :] = jnp.sum(by_normed * active, axis=0, keepdims=True)
        grad_normed = grad_gated * (active * gain)
        along = jnp.mean(rec * grad_normed, axis=1, keepdims=True)
        grad_rec[h] = inverse * grad_normed - rec * (inverse * inverse * inverse * along)
        local[h] = mm(lift_ref[h], grad_rec[h], 0, 0).astype(BF)
    ring.met(mirror=True, across=True, sibling=True)
    base = 1 + 3 * mine
    second_side = ring.across_copy(
        grad_held_ref.at[1], grad_second_ref, sems, base
    )
    second_side.start()
    head_copies = Copies(head_send, head_recv)
    head_sum = HeadSum(Cube(), head_copies, mlp_ref, sibling, kept, across_in, total, CHUNKS)
    for c in range(CHUNKS):
        head_sum.halve(c)
    local_copies = [
        ring.copy(local.at[(1 - ring.side) * mine + i], other.at[i], sems, 1 + i, ring.partner)
        for i in range(mine)
    ]
    for copy in local_copies:
        copy.start()
    for c in range(CHUNKS):
        head_sum.cross(c)
    fill_ext(ext, proj_ref, rim_ref)
    scan = Scan(first_ref, decay_ref, gates_ref, heads)
    keeps = tap_keeps(scan.starts, taps)
    chain_copies = [
        ring.copy(chain_out.at[i], chain_in.at[i], sems, 1 + mine + i, ring.place - 2) for i in range(mine)
    ]
    state_copies = [
        ring.copy(state_out.at[i], state_in.at[i], sems, 1 + 2 * mine + i, ring.partner) for i in range(mine)
    ]
    from_after, to_before = ring.pair < ring.pairs - 1, ring.pair > 0

    @pl.when(jnp.logical_not(from_after))
    def _():
        chain_in[...] = jnp.zeros_like(chain_in)

    lates, boths = [], []
    for i in range(mine):
        local_copies[i].wait_recv()
        own, far = local[ring.side * mine + i], other[i]
        early = jnp.where(ring.side == 0, own, far)
        late = jnp.where(ring.side == 0, far, own)
        lates.append(late.astype(F32))
        boths.append(early.astype(F32) + mm(pair_ref[0, i], late, 0, 0))
    for i in range(mine):
        pl.when(from_after)(chain_copies[i].wait_recv)
        chain_out[i] = (mm(pair_ref[2, i], chain_in[i], 0, 0) + boths[i]).astype(BF)
        pl.when(to_before)(chain_copies[i].start)
    for i in range(mine):
        last = chain_in[i]
        mid = (mm(pair_ref[1, i], last, 0, 0) + lates[i]).astype(BF)
        state_out[i] = jnp.where(ring.side == 0, last, mid)
        state_copies[i].start()
        grad_end_all[ring.side * mine + i] = jnp.where(ring.side == 0, mid, last)
    for i in range(mine):
        state_copies[i].wait_recv()
        grad_end_all[(1 - ring.side) * mine + i] = state_in[i]
    core = ring.head % 2
    span = attn_ref.shape[2]
    core_rows = attn_far_ref.at[:, :, pl.ds(pl.multiple_of(core * span, span), span)]
    attn_copy = ring.copy(attn_ref, core_rows, sems, base + 1, ring.mirror)
    share_copy = pltpu.make_async_remote_copy(
        src_ref=core_rows, dst_ref=core_rows, send_sem=sems[0].at[base + 2], recv_sem=sems[1].at[base + 2],
        device_id=(ring.place, ring.sibling), device_id_type=MESH,
    )
    grad_cums = []
    grad_strengths = []
    for h in range(heads):
        if h == 0:
            attn_copy.start()
        cols = pl.ds(h * hdim, hdim)
        fade, inside, growth, to_end, carry = scan.of(h)
        beta = scan.strength[h]
        sums, sigs, acts = [], [], []
        for part in range(3):
            u = convolved(ext, part, cols, convw_ref, keeps)
            s = sigmoid(u)
            sums.append(u)
            sigs.append(s)
            acts.append(u * s)
        q, q_inv = unit(acts[0], hdim ** -0.5)
        k, k_inv = unit(acts[1], 1.0)
        v = acts[2]
        state, grad_out, grad_end = state_ref[h], grad_rec[h], grad_end_all[h]
        solved = solved_ref[h]
        score = score_ref[h]
        weights, values = solved[:, :hdim], solved[:, hdim:]
        k_end = k * to_end
        fresh = values.astype(F32) - mm(weights, state)
        grad_fresh = mm(score, grad_out, 0, 0) + mm(k_end, grad_end)
        over_state = mm(jnp.concatenate([grad_out, grad_fresh], axis=0), state, 1, 1)
        grad_q_grow = over_state[:size]
        grad_weights = -over_state[size:]
        grad_k_end = mm(fresh, grad_end, 1, 1)
        grad_score = mm(grad_out, fresh, 1, 1)
        grad_carry = jnp.sum(
            jnp.sum(grad_end.astype(F32) * state.astype(F32), axis=1, keepdims=True), axis=0, keepdims=True
        )
        grad_right = mm(inv_ref[h], jnp.concatenate([grad_weights, grad_fresh], axis=1), 0, 0)
        grad_system = -mm(grad_right, solved, 1, 1)
        gram = gram_ref[h].astype(F32)
        by_gram = grad_system * gram
        grad_gram = jnp.where(inside, grad_system * (beta * fade), 0.0)
        grad_pair = jnp.where(fade > 0.0, grad_score * fade, 0.0)
        stacked = jnp.concatenate([grad_gram, grad_pair], axis=0)
        forward_terms = mm(stacked, k)
        back_terms = mm(stacked, jnp.concatenate([k, q], axis=0), 0, 0)
        grad_right_k, grad_right_v = grad_right[:, :hdim], grad_right[:, hdim:]
        beta_growth = beta * growth
        grad_q = forward_terms[size:] + growth * grad_q_grow
        grad_k = forward_terms[:size] + back_terms + beta_growth * grad_right_k + to_end * grad_k_end
        grad_v = beta * grad_right_v
        right_k = jnp.sum(grad_right_k * k, axis=1, keepdims=True) * growth
        right_v = jnp.sum(grad_right_v * v, axis=1, keepdims=True)
        by_rows = jnp.sum(by_gram, axis=1, keepdims=True)
        grad_strengths.append(by_rows + right_k + right_v)
        spread = beta * by_gram + jnp.where(inside, grad_score * score.astype(F32), 0.0)
        ends = jnp.sum(grad_k_end * k_end, axis=1, keepdims=True)
        grad_cum = (
            jnp.sum(spread, axis=1, keepdims=True)
            + beta * right_k
            + jnp.sum(grad_q_grow * q, axis=1, keepdims=True) * growth
            - ends
        )
        to_last = jnp.sum(ends, axis=0, keepdims=True) + grad_carry * carry
        is_last = lax.broadcasted_iota(jnp.int32, (size, 1), 0) == size - 1
        grad_cum = grad_cum + jnp.where(is_last, to_last, 0.0)
        grad_cums.append((grad_cum, jnp.sum(spread, axis=0, keepdims=True)))
        grads = (
            unit_back(acts[0], q_inv, hdim ** -0.5, grad_q),
            unit_back(acts[1], k_inv, 1.0, grad_k),
            grad_v,
        )
        for part in range(3):
            u, s = sums[part], sigs[part]
            grad_u = grads[part] * (s * (1.0 + u * (1.0 - s)))
            total = None
            taps_here = []
            for j in range(taps):
                kept = grad_u * keeps[j] if j < taps - 1 else grad_u
                shifted = ext[part, pl.ds(8 - (taps - 1) + j, size), cols]
                taps_here.append(jnp.sum(kept * shifted, axis=0, keepdims=True))
                back[j, pl.ds(0, 8), :] = jnp.zeros((8, hdim), F32)
                back[j, pl.ds(8, size), :] = kept * convw_ref[part, j : j + 1, cols]
                back[j, pl.ds(8 + size, 8), :] = jnp.zeros((8, hdim), F32)
            grad_convw_ref[part, :, cols] = jnp.concatenate(taps_here, axis=0)
            for j in range(taps):
                term = back[j, pl.ds(8 + (taps - 1) - j, size), :]
                total = term if total is None else total + term
            grad_proj_ref[part, :, cols] = total.astype(BF)
            last_rows[part, :, cols] = total[size - 16 :, :]
            edge = None
            for j in range(taps):
                term = back[j, pl.ds((taps - 1) - j, 8), :]
                edge = term if edge is None else edge + term
            edge_out[part, :, cols] = edge
    edge_copy = ring.copy(edge_out, edge_in, sems, 0, ring.place - 1)
    has_before, has_after = ring.place > 0, ring.place < ring.count - 1
    pl.when(has_before)(edge_copy.start)
    columns = jnp.concatenate(
        [g for g, _ in grad_cums] + grad_strengths + [jnp.zeros((size, 128 - 2 * heads), F32)], axis=1
    )
    rows = columns.T
    cum_rows = rows[0:heads] - jnp.concatenate([r for _, r in grad_cums], axis=0)
    padded = jnp.concatenate([cum_rows, jnp.zeros((8 - heads, size), F32)], axis=0)
    grad_logs = mm_exact(padded, tri(size, False))[0:heads]
    strength = sigmoid(gates_ref[0:heads, :])
    grad_gates_ref[0:heads, :] = rows[heads : 2 * heads] * strength * (1.0 - strength)
    by_rate = jnp.sum(grad_logs * scan.log_rows, axis=1, keepdims=True)
    slopes = []
    for h in range(heads):
        rate = jnp.exp(jnp.full((1, size), decay_ref[0, h], F32))
        slopes.append(-rate * sigmoid(gates_ref[heads + h : heads + h + 1, :] + decay_ref[1, h]))
    grad_bias = grad_logs * jnp.concatenate(slopes, axis=0)
    grad_gates_ref[heads : 2 * heads, :] = grad_bias
    by_bias = jnp.sum(grad_bias, axis=1, keepdims=True)
    grad_decay_ref[...] = jnp.concatenate(
        [by_rate, by_bias, jnp.zeros((heads, 126), F32)], axis=1
    )

    @pl.when(jnp.logical_not(has_after))
    def _():
        edge_in[...] = jnp.zeros_like(edge_in)

    pl.when(has_after)(edge_copy.wait_recv)
    for part in range(3):
        rows = jnp.concatenate(
            [last_rows[part, 0:8, :], last_rows[part, 8:16, :] + edge_in[part]], axis=0
        )
        grad_proj_ref[part, pl.ds(size - 16, 16), :] = rows.astype(BF)
    for c in range(CHUNKS):
        head_sum.share(c)
    for c in range(CHUNKS):
        head_sum.arrive(c)
    for r in range(0, size, 32):
        rows = pl.ds(r, 32)
        output_ref[rows, :] = middle_ref[rows, :] + head_sum.total[rows, :].astype(F32)
    by_gates_ref[...] = mm(grad_gates_ref[...], normed_ref[...])
    attn_copy.wait_recv()
    share_copy.start()
    for i in range(mine):
        local_copies[i].wait_send()
        pl.when(to_before)(chain_copies[i].wait_send)
        state_copies[i].wait_send()
    pl.when(has_before)(edge_copy.wait_send)
    attn_copy.wait_send()
    share_copy.wait()
    second_side.wait()
    head_copies.finish()


def recurrent_backward(first, decay, gates, proj, rim, convw, gain, grad_gated, saved, grad_held, attn, normed, mlp, middle):
    heads = decay.shape[1]
    parts, size, width = proj.shape
    hdim = width // heads
    mine = heads // 2
    taps = convw.shape[1]
    shape = jax.ShapeDtypeStruct
    vm = pl.BlockSpec(memory_space=pltpu.VMEM)
    sm = pl.BlockSpec(memory_space=pltpu.SMEM)
    hbm = pl.BlockSpec(memory_space=pl.ANY)
    count = 4 + 3 * mine
    states = lambda count: pltpu.VMEM((count, hdim, hdim), BF)
    return pl.pallas_call(
        functools.partial(backward_kernel, heads),
        out_shape=(
            shape((4, size, width), BF), shape((3, taps, width), F32),
            shape((2 * heads, size), F32), shape((heads, 128), F32), shape((heads, hdim), F32),
            shape(grad_held.shape[1:], BF),
            shape((attn.shape[0], attn.shape[1], size), BF), shape((2 * heads, normed.shape[1]), F32),
            shape(middle.shape, F32),
        ),
        in_specs=[sm, sm] + [vm] * 14 + [hbm, vm, vm, vm, vm],
        out_specs=(vm,) * 5 + (hbm, vm, vm, vm),
        scratch_shapes=[
            pltpu.VMEM((3, size + 8, width), F32), pltpu.VMEM((taps, size + 16, hdim), F32),
            pltpu.VMEM((heads, size, hdim), F32), states(heads), states(mine), states(mine), states(mine),
            states(mine), states(mine), states(heads),
            pltpu.VMEM((3, 8, width), F32), pltpu.VMEM((3, 8, width), F32), pltpu.VMEM((3, 16, width), F32),
            *HeadSum.scratch(*middle.shape),
            pltpu.SemaphoreType.DMA((3 * CHUNKS,)), pltpu.SemaphoreType.DMA((3 * CHUNKS,)),
            pltpu.SemaphoreType.DMA((count,)), pltpu.SemaphoreType.DMA((count,)),
        ],
        compiler_params=pltpu.CompilerParams(
            vmem_limit_bytes=34 << 20, collective_id=2, has_side_effects=True
        ),
        name="recurrent_backward",
    )(first, decay, gates, proj, rim, convw, gain, grad_gated, *saved, grad_held, attn, normed, mlp, middle)


def middle_kernel(
    gated_ref, w_out_ref, inputs_ref, gains_ref, own_ref, far_ref, middle_ref, normed_ref, held_ref,
    part, sibling, kept, across_in, total, send_sems, recv_sems,
):
    cube = Cube()
    copies = Copies(send_sems, recv_sems)
    cube.greet([cube.beside(1), cube.beside(2)] + [cube.along(bit) for bit in cube.bits])
    for side in (0, 1):
        held_ref[side, 0] = own_ref[side]
        held_ref[side, 1] = far_ref[side]
    spread = Spread(cube, copies, held_ref)
    sums = HeadSum(cube, copies, part, sibling, kept, across_in, total, CHUNKS)
    for c in range(CHUNKS):
        part[:, sums.cols(c)] = mm(gated_ref[...], w_out_ref[:, sums.cols(c)]).astype(BF)
        if c == 0:
            cube.met(2 + len(cube.bits))
        sums.halve(c)
    spread.send(1)
    for c in range(CHUNKS):
        sums.cross(c)
    spread.take()
    spread.send(2)
    for c in range(CHUNKS):
        sums.share(c)
    for c in range(CHUNKS):
        sums.arrive(c)
    gain = gains_ref[1:2, :]
    for r in range(0, inputs_ref.shape[0], 32):
        rows = pl.ds(r, 32)
        middle = inputs_ref[rows, :] + total[rows, :].astype(F32)
        middle_ref[rows, :] = middle
        inverse = lax.rsqrt(jnp.mean(middle * middle, axis=1, keepdims=True) + EPS)
        normed_ref[rows, :] = (middle * inverse * gain).astype(BF)
    spread.take()
    for step in range(3, len(cube.bits) + 1):
        spread.send(step)
        spread.take()
    copies.finish()


def middle_of(gated, w_out, inputs, gains, own, far):
    size, features = inputs.shape
    owners = lax.axis_size("seq")
    count = 3 * CHUNKS + 2 * (owners.bit_length() - 2)
    shape = jax.ShapeDtypeStruct
    vm = pl.BlockSpec(memory_space=pltpu.VMEM)
    return pl.pallas_call(
        middle_kernel,
        out_shape=(
            shape((size, features), F32), shape((size, features), BF),
            shape((2, owners) + own.shape[1:], BF),
        ),
        in_specs=[vm] * 6,
        out_specs=(vm,) * 3,
        scratch_shapes=[pltpu.VMEM((size, features), BF)] + HeadSum.scratch(size, features) + [
            pltpu.SemaphoreType.DMA((count,)), pltpu.SemaphoreType.DMA((count,)),
        ],
        compiler_params=pltpu.CompilerParams(
            vmem_limit_bytes=40 << 20, collective_id=4, has_side_effects=True
        ),
        name="middle",
    )(gated, w_out, inputs, gains, own, far)


def by_half(cube, array, near, leaving):
    features = array.shape[1]
    kept = near.shape[1]
    half = cube.place // (cube.count // 2)
    span = leaving.shape[2]
    rows = pl.ds(pl.multiple_of(cube.head % 2 * span, span), span)
    width = features // 2
    mine = array[:, pl.ds(pl.multiple_of(half * width, width), width)]
    others = array[rows, pl.ds(pl.multiple_of((1 - half) * width, width), width)]
    for j in range(near.shape[0]):
        near[j] = mine[:, j * kept : (j + 1) * kept].T
        leaving[j] = others[:, j * kept : (j + 1) * kept].T


def middle_back_kernel(
    part_ref, middle_ref, cotangent_ref, gains_ref, w_out_ref, part_held_ref, normed_ref,
    grad_middle_ref, near_ref, leaving_ref, grad_gated_ref, grad_gain_ref, held_ref, normed_near_ref, normed_far_ref,
    grad_low, normed_leaving, sibling, kept, across_in, total, send_sems, recv_sems,
):
    cube = Cube()
    copies = Copies(send_sems, recv_sems)
    cube.greet([cube.mirror(), cube.beside(1), cube.beside(2)] + [cube.along(bit) for bit in cube.bits])
    held_ref[:, pl.ds(0, 4)] = part_held_ref[...]
    spread = Spread(cube, copies, held_ref)
    sums = HeadSum(cube, copies, part_ref, sibling, kept, across_in, total, CHUNKS)
    by_half(cube, normed_ref, normed_near_ref, normed_leaving)
    cube.met(3 + len(cube.bits))
    span = normed_leaving.shape[2]
    core_rows = normed_far_ref.at[:, :, pl.ds(pl.multiple_of(cube.head % 2 * span, span), span)]
    far_copy = copies.start(normed_leaving, core_rows, cube.mirror())
    spread.send(2)
    for c in range(CHUNKS):
        sums.halve(c)
    for c in range(CHUNKS):
        sums.cross(c)
    for c in range(CHUNKS):
        sums.share(c)
    for c in range(CHUNKS):
        sums.arrive(c)
    far_copy.wait_recv()
    share_copy = copies.start(core_rows, core_rows, cube.beside(1))
    grad_gain_ref[...] = norm_back(
        middle_ref, total, gains_ref[1:2, :], cotangent_ref, grad_middle_ref, grad_low
    )
    grad_gated_ref[...] = mm(grad_low[...], w_out_ref[...], 1, 1)
    by_half(cube, grad_low, near_ref, leaving_ref)
    spread.take()
    for step in range(3, len(cube.bits) + 1):
        spread.send(step)
        spread.take()
    share_copy.wait_recv()
    copies.finish()


def norm_back(values_ref, grad_ref, gain, added_ref, out_ref, low_ref):
    gain_sum = None
    for r in range(0, values_ref.shape[0], 32):
        rows = pl.ds(r, 32)
        values = values_ref[rows, :]
        inverse = lax.rsqrt(jnp.mean(values * values, axis=1, keepdims=True) + EPS)
        grad = grad_ref[rows, :].astype(F32)
        scaled = grad * gain
        along = jnp.mean(values * scaled, axis=1, keepdims=True)
        out = added_ref[rows, :] + inverse * scaled - values * (inverse * inverse * inverse * along)
        out_ref[rows, :] = out
        if low_ref is not None:
            low_ref[rows, :] = out.astype(BF)
        here = jnp.sum(grad * (values * inverse), axis=0, keepdims=True)
        gain_sum = here if gain_sum is None else gain_sum + here
    return gain_sum


def middle_back(part, middle, cotangent, gains, w_out, held, normed):
    size, features = middle.shape
    owners = lax.axis_size("seq")
    count = 2 + 3 * CHUNKS + 2 * (owners.bit_length() - 3)
    shape = jax.ShapeDtypeStruct
    by_owner = shape((owners // 2, features // owners, size), BF)
    vm = pl.BlockSpec(memory_space=pltpu.VMEM)
    return pl.pallas_call(
        middle_back_kernel,
        out_shape=(
            shape((size, features), F32), by_owner,
            shape((owners // 2, features // owners, size // 2), BF),
            shape((size, w_out.shape[0]), F32), shape((1, features), F32),
            shape((2, owners) + held.shape[2:], BF), by_owner, by_owner,
        ),
        in_specs=[vm] * 7,
        out_specs=(vm,) * 8,
        scratch_shapes=[
            pltpu.VMEM((size, features), BF), pltpu.VMEM((owners // 2, features // owners, size // 2), BF),
        ] + HeadSum.scratch(size, features) + [
            pltpu.SemaphoreType.DMA((count,)), pltpu.SemaphoreType.DMA((count,)),
        ],
        compiler_params=pltpu.CompilerParams(
            vmem_limit_bytes=40 << 20, collective_id=5, has_side_effects=True
        ),
        name="middle_back",
    )(part, middle, cotangent, gains, w_out, held, normed)


class Halving:
    def __init__(self, cube, copies, outgoing, incoming):
        self.cube, self.copies, self.outgoing, self.incoming = cube, copies, outgoing, incoming
        self.orders = (cube.bits, cube.bits[::-1])
        self.held = [None, None]
        self.step = [0, 0]
        self.slot = [0, 0]
        self.flying = [None, None]

    def begin(self, partials):
        for side in (0, 1):
            rows = partials[0].shape[0] // 2
            self.held[side] = {m: p[side * rows : (side + 1) * rows] for m, p in partials.items()}
            self.send(side)

    def send(self, side):
        bit = self.orders[side][self.step[side]]
        leaving = sorted(m for m in self.held[side] if m & bit)
        first = self.slot[side]
        for k, m in enumerate(leaving):
            self.outgoing[side, first + k] = self.held[side].pop(m).astype(BF)
        span = pl.ds(first, len(leaving))
        self.flying[side] = (
            self.copies.start(
                self.outgoing.at[side, span], self.incoming.at[side, span], self.cube.along(bit)
            ),
            first,
        )
        self.slot[side] += len(leaving)
        self.step[side] += 1

    def advance(self):
        for side in (0, 1):
            copy, first = self.flying[side]
            copy.wait_recv()
            for k, m in enumerate(sorted(self.held[side])):
                self.held[side][m] = self.held[side][m] + self.incoming[side, first + k].astype(F32)
            if self.step[side] < len(self.orders[side]):
                self.send(side)

    def result(self):
        return [self.held[side][0] for side in (0, 1)]


def ff_tile(tokens, grads, w_gate, w_up, w_down):
    gate = mm(tokens, w_gate)
    up = mm(tokens, w_up)
    grad = mm(grads, w_down, 1, 1)
    sig = sigmoid(gate)
    active = gate * sig
    hidden = (active * up).astype(BF)
    grad_gate = (grad * up * (sig * (1.0 + gate * (1.0 - sig)))).astype(BF)
    return hidden, grad_gate, (grad * active).astype(BF)


def near_kernel(
    tokens_ref, grads_ref, w_up_hbm, w_down_hbm, grad_held_ref, gated_ref,
    grad_ref, out_ref, held_ref, grad_first_ref, gated_far_ref, w_up_ref, w_down_ref, load_sems, send_sems, recv_sems,
):
    cube = Cube()
    units = w_down_ref.shape[0]
    loads = [
        pltpu.make_async_copy(source, target, load_sems.at[k])
        for k, (source, target) in enumerate(((w_up_hbm, w_up_ref), (w_down_hbm, w_down_ref)))
    ]
    for load in loads:
        load.start()
    copies = Copies(send_sems, recv_sems)
    cube.greet([cube.mirror(), cube.along(cube.bits[0]), cube.along(cube.bits[-1]), cube.beside(2)])
    rows = held_ref.shape[2]
    for side in (0, 1):
        first = pl.multiple_of((2 * cube.head + side) * rows, rows)
        held_ref[side, 0] = tokens_ref[pl.ds(first, rows), :]
    spread = Spread(cube, copies, held_ref)
    cube.met(4)
    spread.send(0)
    first_side = copies.start(grad_held_ref.at[0], grad_first_ref, cube.beside(2))
    gated_copy = copies.start(gated_ref, gated_far_ref, cube.mirror())
    for load in loads:
        load.wait()
    w_gate, w_up = w_up_ref[:, pl.ds(0, units)], w_up_ref[:, pl.ds(units, units)]
    hidden, grad_gate, grad_up = ff_tile(tokens_ref[...], grads_ref[...].astype(BF), w_gate, w_up, w_down_ref[...])
    spread.take()
    spread.send(1)
    grad_ref[...] = (mm(grad_gate, w_gate, 1, 1) + mm(grad_up, w_up, 1, 1)).astype(BF)
    out_ref[...] = mm(hidden, w_down_ref[...]).astype(BF)
    spread.take()
    gated_copy.wait_recv()
    first_side.wait_recv()
    copies.finish()


def near_part(tokens, grads, w_up, w_down, grad_held, gated):
    size, features = tokens.shape
    low = jax.ShapeDtypeStruct((size, features), BF)
    rows = size // (2 * lax.axis_size("head"))
    vm = pl.BlockSpec(memory_space=pltpu.VMEM)
    hbm = pl.BlockSpec(memory_space=pl.ANY)
    return pl.pallas_call(
        near_kernel,
        out_shape=(
            low, low, jax.ShapeDtypeStruct((2, 4, rows, features), BF),
            jax.ShapeDtypeStruct(grad_held.shape[1:], BF), jax.ShapeDtypeStruct(gated.shape, BF),
        ),
        in_specs=[vm, vm] + [hbm] * 4,
        out_specs=(vm,) * 3 + (hbm, hbm),
        scratch_shapes=[
            pltpu.VMEM(w_up.shape, BF), pltpu.VMEM(w_down.shape, BF), pltpu.SemaphoreType.DMA((2,)),
            pltpu.SemaphoreType.DMA((6,)), pltpu.SemaphoreType.DMA((6,)),
        ],
        compiler_params=pltpu.CompilerParams(
            vmem_limit_bytes=40 << 20, collective_id=6, has_side_effects=True
        ),
        name="feed_forward",
    )(tokens, grads, w_up, w_down, grad_held, gated)


def tail_kernel(
    near_ref, normed_half_ref, normed_far_ref, gated_ref, gated_far_ref, attn_half_ref, attn_far_ref,
    gates_ref, part_ref, inputs_hbm, gains_ref,
    middle_hbm, conv_ref, mid_gain_ref, decay_ref, head_gain_ref,
    tok_own_ref, grad_own_ref, grad_first_ref, grad_second_ref, w_up_hbm, w_down_hbm,
    grad_proj_ref, grad_wout_ref, grad_inputs_ref, grad_up_ref, grad_down_ref,
    by_gates_ref, by_conv_ref, by_gains_ref, by_head_ref, by_decay_ref,
    tok_sib_ref, grad_sib_ref, tok_across_ref, tok_both_ref, grad_both_ref,
    far, outgoing, incoming, sibling, kept, across_in, total, small_ref, small_out, small_in,
    w_up, w_down, blocks, spare, load_sems, block_sems, send_sems, recv_sems,
):
    cube = Cube()
    copies = Copies(send_sems, recv_sems)
    parts, size, width = near_ref.shape
    bits = len(cube.bits)
    loads = [
        pltpu.make_async_copy(source, target, load_sems.at[k])
        for k, (source, target) in enumerate(((w_up_hbm, w_up), (w_down_hbm, w_down)))
    ]
    middle_load = pltpu.make_async_copy(middle_hbm, grad_inputs_ref, load_sems.at[2])
    middle_load.start()
    inputs_ref = grad_proj_ref if grad_proj_ref.shape == inputs_hbm.shape else spare
    inputs_load = pltpu.make_async_copy(inputs_hbm, inputs_ref, load_sems.at[3])
    inputs_load.start()
    for load in loads:
        load.start()
    beside, across_way = cube.beside(1), cube.beside(2)
    cube.greet([cube.mirror(), beside, across_way] + [cube.along(bit) for bit in cube.bits])
    cube.met(3 + bits)
    order = (4, 3, 2, 1, 0)
    reduced = HeadSum(cube, copies, part_ref, sibling, kept, across_in, total, CHUNKS)
    for c in range(CHUNKS):
        reduced.halve(c)
    arriving = {c: copies.start(near_ref.at[c], far.at[c], cube.mirror()) for c in order[1:]}
    for c in range(CHUNKS):
        reduced.cross(c)
    arrivals = {
        ("sib", 0): copies.start(tok_own_ref, tok_sib_ref, beside),
        ("sib", 1): copies.start(grad_own_ref, grad_sib_ref, beside),
    }
    for side in (0, 1):
        arrivals["across", side] = copies.start(
            tok_own_ref.at[side], tok_across_ref.at[side], across_way
        )
    done = set()

    def ready(*names):
        for name in names:
            if name not in done:
                done.add(name)
                arrivals[name].wait_recv()

    def share_grads():
        for side, grads in enumerate((grad_first_ref, grad_second_ref)):
            arrivals["grads", side] = copies.start(grads, grad_both_ref.at[side], beside)

    def forward(side):
        ready(("across", side))
        arrivals["both", side] = copies.start(tok_across_ref.at[side], tok_both_ref.at[side], beside)

    sums = {}

    def partials(c):
        found = {}
        if c < parts:
            arriving[c].wait_recv()
        for m in cube.masks:
            within = cube.moved(m) % len(cube.masks)
            if c < parts:
                found[m] = mm(normed_half_ref[within], near_ref[c]) + mm(normed_far_ref[within], far[c])
            else:
                found[m] = mm(attn_half_ref[within], gated_ref[...]) + mm(attn_far_ref[within], gated_far_ref[...])
        sums[c] = Halving(cube, copies, outgoing.at[c], incoming.at[c])
        sums[c].begin(found)

    def store(c):
        for side, rows in enumerate(sums[c].result()):
            if c == parts:
                half = rows.shape[0]
                grad_wout_ref[:, side * half : (side + 1) * half] = rows.T
                continue
            grad_proj_ref[pl.ds(side * rows.shape[0], rows.shape[0]), pl.ds(c * width, width)] = rows

    left = {c: bits for c in order}

    def advance(c):
        if left[c]:
            sums[c].advance()
            left[c] -= 1
            if not left[c]:
                store(c)

    span = grad_up_ref.shape[0]
    stretch = blocks.shape[2]
    owner_rows = pl.ds(
        pl.multiple_of(cube.place * (w_up.shape[0] // cube.count) // span * span, span), span
    )
    units = w_down.shape[0]
    features = w_up.shape[0]
    pieces = cube.count // stretch

    def weights(tokens_of, grads_of, count):
        def fetch(k, slot):
            at = pl.ds(pl.multiple_of(k % pieces * stretch, stretch), stretch)
            return [
                pltpu.make_async_copy(
                    of(k // pieces).at[at], blocks.at[slot, which], block_sems.at[slot, which]
                )
                for which, of in enumerate((tokens_of, grads_of))
            ]

        for copy in fetch(0, 0):
            copy.start()

        def piece(k, carry):
            slot = k % 2
            for copy in fetch(k, slot):
                copy.wait()

            @pl.when(k + 1 < count * pieces)
            def _():
                for copy in fetch(k + 1, 1 - slot):
                    copy.start()

            accumulate(slot, False)
            return carry

        lax.fori_loop(0, count * pieces, piece, 0)

    def weights_across(tokens_of, grads_of):
        cuts = sorted({c for of in (tokens_of, grads_of) for _, _, first, rows in of for c in (first, first + rows)})
        if pieces == 1:
            made = []
            for which, of in enumerate((tokens_of, grads_of)):
                for k, (ref, start, first, rows) in enumerate(of):
                    copy = pltpu.make_async_copy(
                        ref.at[pl.ds(start, rows)], blocks.at[0, which, pl.ds(first, rows)],
                        block_sems.at[k, which],
                    )
                    copy.start()
                    made.append(copy)
            for copy in made:
                copy.wait()

            def once(k, carry):
                accumulate(0, False)
                return carry

            lax.fori_loop(0, 1, once, 0)
            return
        for low, high in zip(cuts[:-1], cuts[1:]):
            found = []
            for of in (tokens_of, grads_of):
                ref, start, first, _ = next(p for p in of if p[2] <= low < p[2] + p[3])
                found.append((ref, start + low - first))

            def piece(k, carry):
                made = [
                    pltpu.make_async_copy(
                        ref.at[pl.ds(pl.multiple_of(start + k * stretch, stretch), stretch)],
                        blocks.at[0, which], block_sems.at[0, which],
                    )
                    for which, (ref, start) in enumerate(found)
                ]
                for copy in made:
                    copy.start()
                for copy in made:
                    copy.wait()
                accumulate(0, False)
                return carry

            lax.fori_loop(0, (high - low) // stretch, piece, 0)

    def accumulate(slot, start):
        tokens = blocks[slot, 0].reshape(-1, features)
        grads = blocks[slot, 1].reshape(-1, features)
        own_tokens = blocks[slot, 0, :, :, owner_rows].reshape(-1, span)
        own_grads = blocks[slot, 1, :, :, owner_rows].reshape(-1, span)
        hidden, grad_gate, grad_up = ff_tile(
            tokens, grads, w_up[:, pl.ds(0, units)], w_up[:, pl.ds(units, units)], w_down[...]
        )
        found = (mm(own_tokens, grad_gate, 0, 0), mm(own_tokens, grad_up, 0, 0), mm(own_grads, hidden, 0, 0))
        targets = (
            (grad_up_ref, pl.ds(0, units)), (grad_up_ref, pl.ds(units, units)), (grad_down_ref, pl.ds(0, units))
        )
        for value, (target, cols) in zip(found, targets):
            if start:
                target[:, cols] = value
            else:
                target[:, cols] += value

    ways = [cube.along(bit) for bit in cube.bits] + [cube.mirror()]
    flights = []

    def small_send():
        step = len(flights)
        small_out[step] = small_ref[...].astype(BF)
        flights.append(copies.start(small_out.at[step], small_in.at[step], ways[step]))

    taken = []

    def small_take():
        step = len(taken)
        if step == len(ways):
            return
        taken.append(step)
        flights[step].wait_recv()
        small_ref[...] = small_out[step].astype(F32) + small_in[step].astype(F32)
        if step + 1 < len(ways):
            small_send()

    def share_sums():
        for c in range(CHUNKS):
            reduced.share(c)

    def inputs_back():
        for c in range(CHUNKS):
            reduced.arrive(c)
        gain = gains_ref[0:1, :]
        middle_load.wait()
        inputs_load.wait()
        gain_sum = norm_back(inputs_ref, total, gain, grad_inputs_ref, grad_inputs_ref, None)
        flat = [head_gain_ref[h : h + 1, :] for h in range(head_gain_ref.shape[0])]
        flat += [decay_ref[h : h + 1, :] for h in range(decay_ref.shape[0])]
        flat.append(jnp.zeros((1, gain.shape[1] - sum(f.shape[1] for f in flat)), F32))
        small_ref[...] = jnp.concatenate(
            [gates_ref[...], conv_ref[...], gain_sum, mid_gain_ref[...], jnp.concatenate(flat, axis=1),
             jnp.zeros((2, gain.shape[1]), F32)], axis=0
        )
        small_send()

    grad_up_ref[...] = jnp.zeros_like(grad_up_ref)
    grad_down_ref[...] = jnp.zeros_like(grad_down_ref)
    partials(order[0])
    for load in loads:
        load.wait()
    weights(lambda k: tok_own_ref.at[k], lambda k: grad_own_ref.at[k], 2)
    share_sums()
    partials(3)
    advance(4)
    ready(("sib", 0), ("sib", 1))
    weights(lambda k: tok_sib_ref.at[k], lambda k: grad_sib_ref.at[k], 2)
    inputs_back()
    share_grads()
    advance(4)
    advance(3)
    partials(2)
    forward(0)
    every = cube.count
    weights_across([(tok_across_ref.at[0], 0, 0, every)], [(grad_first_ref, 0, 0, every)])
    small_take()
    advance(3)
    advance(2)
    partials(1)
    ready(("grads", 0), ("both", 0))
    weights_across([(tok_both_ref.at[0], 0, 0, every)], [(grad_both_ref.at[0], 0, 0, every)])
    small_take()
    advance(2)
    advance(1)
    partials(0)
    forward(1)
    weights_across([(tok_across_ref.at[1], 0, 0, every)], [(grad_second_ref, 0, 0, every)])
    small_take()
    advance(1)
    advance(0)
    ready(("both", 1), ("grads", 1))
    weights_across([(tok_both_ref.at[1], 0, 0, every)], [(grad_both_ref.at[1], 0, 0, every)])
    for step in range(len(ways)):
        small_take()
    heads, hdim = by_head_ref.shape
    for i in (0, 1):
        by_gates_ref[i] = small_ref[i * heads : (i + 1) * heads, :]
    conv_taps = by_conv_ref.shape[1]
    for p in range(3):
        for t in range(conv_taps):
            by_conv_ref[p, t : t + 1, :] = small_ref[2 * heads + p : 2 * heads + p + 1, t * width : (t + 1) * width]
    by_gains_ref[...] = small_ref[2 * heads + 3 : 2 * heads + 5, :]
    last = small_ref[2 * heads + 5 : 2 * heads + 6, :]
    for h in range(heads):
        by_head_ref[h : h + 1, :] = last[:, h * hdim : (h + 1) * hdim]
        at = heads * hdim + h * LANES
        by_decay_ref[h : h + 1, :] = last[:, at : at + LANES]
    for step in range(bits):
        for c in order:
            advance(c)
    copies.finish()


def tail(
    near, normed_half, normed_far, gated, gated_far, attn_half, attn_far, gates, part, inputs, gains,
    middle, conv, mid_gain, decay, head_gain, tok_own, grad_own, grad_first, grad_second, w_up, w_down,
):
    parts, size, width = near.shape
    owners = lax.axis_size("seq")
    bits = owners.bit_length() - 2
    slots = owners // 2 - 1
    kept = normed_half.shape[1]
    span = max(kept, LANES)
    features = inputs.shape[1]
    stretch = 8
    heads = head_gain.shape[0]
    taps = conv.shape[1] // width
    shape = jax.ShapeDtypeStruct
    vm = pl.BlockSpec(memory_space=pltpu.VMEM)
    hbm = pl.BlockSpec(memory_space=pl.ANY)
    copies = parts + 3 * CHUNKS + bits + 1 + (parts + 1) * 2 * bits + 8
    flying = pltpu.VMEM((parts + 1, 2, slots, kept // 2, width), BF)
    held = shape(tok_own.shape, BF)
    spare = pltpu.VMEM((8, LANES) if (kept, parts * width) == inputs.shape else inputs.shape, F32)
    found = pl.pallas_call(
        tail_kernel,
        out_shape=(
            shape((kept, parts * width), F32), shape((width, kept), F32), shape((size, features), F32),
            shape((span, w_up.shape[1]), F32), shape((span, w_down.shape[0]), F32),
            shape((2, heads, features), F32), shape((3, taps, width), F32), shape((2, features), F32),
            shape(head_gain.shape, F32), shape(decay.shape, F32),
            held, held, held, held, held,
        ),
        in_specs=[vm] * 9 + [hbm, vm, hbm] + [vm] * 4 + [hbm] * 6,
        out_specs=(vm,) * 10 + (hbm,) * 5,
        scratch_shapes=[
            pltpu.VMEM((parts, size, width), BF), flying, flying, *HeadSum.scratch(size, features),
            pltpu.VMEM((16, features), F32),
            pltpu.VMEM((bits + 1, 16, features), BF), pltpu.VMEM((bits + 1, 16, features), BF),
            pltpu.VMEM(w_up.shape, BF), pltpu.VMEM(w_down.shape, BF),
            pltpu.VMEM((2, 2, stretch) + tok_own.shape[2:], BF),
            spare, pltpu.SemaphoreType.DMA((4,)), pltpu.SemaphoreType.DMA((2, 2)),
            pltpu.SemaphoreType.DMA((copies,)), pltpu.SemaphoreType.DMA((copies,)),
        ],
        compiler_params=pltpu.CompilerParams(
            vmem_limit_bytes=63 << 20, collective_id=3, has_side_effects=True
        ),
        name="tail",
    )(
        near, normed_half, normed_far, gated, gated_far, attn_half, attn_far, gates, part, inputs, gains,
        middle, conv, mid_gain, decay, head_gain, tok_own, grad_own, grad_first, grad_second, w_up, w_down,
    )
    return found[:10]


def rms_scale(values, gain):
    return values * lax.rsqrt(jnp.mean(values * values, axis=-1, keepdims=True) + EPS) * gain


def shards(
    inputs,
    gains,
    w_proj,
    w_gates,
    decay,
    conv_w,
    head_gain,
    w_out,
    w_up,
    w_down,
    seq_first,
    cotangent,
):
    tokens = inputs.shape[0]
    heads_here = decay.shape[1]
    owners = lax.axis_size("seq")
    place = lax.axis_index("seq")
    kept = inputs.shape[1] // owners

    normed_low = rms_scale(inputs, gains[0]).astype(BF)
    w_up_flat = w_up.reshape(w_up.shape[0], -1)
    projected = jnp.einsum("td,dkc->ktc", normed_low, w_proj, preferred_element_type=F32)
    gate_in = jnp.einsum("td,idh->iht", normed_low, w_gates, preferred_element_type=F32)
    gate_in = gate_in.reshape(2 * heads_here, tokens)
    (
        gated_low, recurrent, lift, inverse, solved, gram, score, state, pair, rim, grad_own, grad_far
    ) = recurrent_forward(seq_first, decay, gate_in, projected, conv_w, head_gain, cotangent)
    middle, normed_mid_low, grad_held = middle_of(gated_low, w_out, inputs, gains, grad_own, grad_far)
    grad_mid_part, mlp_part, mid_part_held, grad_first, gated_far = near_part(
        normed_mid_low, cotangent, w_up_flat, w_down, grad_held, gated_low
    )
    grad_middle, attn_near, attn_leaving, grad_gated, grad_gain_mid, mid_held, normed_near, normed_far = middle_back(
        grad_mid_part, middle, cotangent, gains, w_out, mid_part_held, normed_low
    )
    (
        grad_projected, grad_conv, grad_gate_in, grad_decay, grad_head_gain, grad_second, attn_far, by_gates,
        output,
    ) = recurrent_backward(
        seq_first, decay, gate_in, projected, rim, conv_w, head_gain, grad_gated,
        (recurrent, lift, inverse, solved, gram, score, state, pair), grad_held, attn_leaving, normed_low,
        mlp_part, middle,
    )
    grad_gate_low = grad_gate_in.astype(BF)
    grad_normed_part = jnp.einsum("ktc,dkc->td", grad_projected, w_proj, preferred_element_type=F32)
    grad_normed_part = grad_normed_part + jnp.einsum(
        "iht,idh->td", grad_gate_low.reshape(2, heads_here, tokens), w_gates, preferred_element_type=F32
    )
    (
        grad_proj_part, grad_wout_part, grad_inputs, grad_up_part, grad_down_part,
        grad_wgates, grad_conv, grad_gains, grad_head_gain, grad_decay,
    ) = tail(
        grad_projected, normed_near, normed_far, gated_low, gated_far, attn_near, attn_far, by_gates,
        grad_normed_part.astype(BF), inputs, gains, grad_middle,
        grad_conv.reshape(3, -1), grad_gain_mid, grad_decay, grad_head_gain,
        mid_held, grad_held, grad_first, grad_second, w_up_flat, w_down,
    )
    grad_proj_part = grad_proj_part.reshape(kept, 4, -1)
    grad_wgates = jnp.swapaxes(grad_wgates, 1, 2)
    grad_decay = grad_decay[:, :2].T
    first = place * kept % grad_up_part.shape[0]
    grad_up_part = lax.dynamic_slice_in_dim(grad_up_part, first, kept, 0).reshape(kept, 2, -1)
    grad_down_part = lax.dynamic_slice_in_dim(grad_down_part, first, kept, 0).T
    return (
        output,
        grad_inputs,
        grad_gains,
        grad_proj_part,
        grad_wgates,
        grad_decay,
        grad_conv,
        grad_head_gain,
        grad_wout_part,
        grad_up_part,
        grad_down_part,
    )


def solution(mesh):
    placed = (
        P("seq", None),
        P(),
        P(None, None, "head"),
        P(None, None, "head"),
        P(None, "head"),
        P(None, None, "head"),
        P("head", None),
        P("head", None),
        P(None, None, "head"),
        P("head", None),
        P("seq"),
        P("seq", None),
    )
    return jax.shard_map(
        shards,
        mesh=mesh,
        in_specs=placed,
        out_specs=(
            P("seq", None),
            P("seq", None),
            P(),
            P("seq", None, "head"),
            P(None, None, "head"),
            P(None, "head"),
            P(None, None, "head"),
            P("head", None),
            P("head", "seq"),
            P("seq", None, "head"),
            P("head", "seq"),
        ),
        check_vma=False,
    )
```
